32 devices in a mesh: dp: 8 (over z, x), mp: 4 (over y, core).
Axes of the slice: x: 2, y: 2, z: 4, core: 2. Of those that a mesh axis runs over, the one named last changes fastest.
Arguments:
- frames: bfloat16 [16384, 1024], P(('dp', 'mp')), may hold values from -12 to 12
- out_cotangent: bfloat16 [16384, 1024], P(('dp', 'mp')), may hold values from -6 to 6
- lengths: int32 [16], P('dp'), may hold values from 512 to 1024, as said below
- masked_rows: int32 [8192], P(('dp', 'mp')), may hold values from 0 to 511, as said below
- targets: int32 [8192], P(('dp', 'mp')), may hold values from 0 to 8191
- head_device: int32 [8192, 1], P(('dp', 'mp')), may hold values from 0 to 7; in each aligned block of 256 rows (0 to 255, 256 to 511, ...) at most 64 rows name the same one
- first_gain: float32 [1024], replicated, may hold values from 0.1 to 1.9
- first_in: bfloat16 [1024, 4096], P(None, 'mp'), may hold values from -0.1875 to 0.1875
- first_out: bfloat16 [4096, 1024], P('mp'), may hold values from -0.1875 to 0.1875
- attend_gain: float32 [1024], replicated, may hold values from 0.1 to 1.9
- query_weight: bfloat16 [1024, 1024], P(None, 'mp'), may hold values from -0.375 to 0.375
- key_weight: bfloat16 [1024, 1024], P(None, 'mp'), may hold values from -0.1875 to 0.1875
- value_weight: bfloat16 [1024, 1024], P(None, 'mp'), may hold values from -0.1875 to 0.1875
- attend_out: bfloat16 [1024, 1024], P('mp'), may hold values from -0.75 to 0.75
- mixer_gain: float32 [1024], replicated, may hold values from 0.1 to 1.9
- mixer_value: bfloat16 [1024, 1024], P(None, 'mp'), may hold values from -0.1875 to 0.1875
- mixer_gate: bfloat16 [1024, 1024], P(None, 'mp'), may hold values from -0.1875 to 0.1875
- mixer_depth: float32 [5, 1024], P(None, 'mp'), may hold values from -2.5 to 2.5
- batch_scale: float32 [1024], P('mp'), may hold values from 0.1 to 1.9
- batch_shift: float32 [1024], P('mp'), may hold values from -3 to 3
- mixer_out: bfloat16 [1024, 1024], P('mp'), may hold values from -0.1875 to 0.1875
- second_gain: float32 [1024], replicated, may hold values from 0.1 to 1.9
- second_in: bfloat16 [1024, 4096], P(None, 'mp'), may hold values from -0.1875 to 0.1875
- second_out: bfloat16 [4096, 1024], P('mp'), may hold values from -0.1875 to 0.1875
- final_gain: float32 [1024], replicated, may hold values from 0.1 to 1.9
- head_weight: bfloat16 [1024, 8192], P(None, 'mp'), may hold values from -2 to 2
Outputs:
- output: float32 [16384, 1024], P(('dp', 'mp'))
- loss: float32 [], replicated
- input_grad: float32 [16384, 1024], P(('dp', 'mp'))
- first_gain_grad: float32 [1024], replicated
- first_in_grad: float32 [1024, 4096], P('dp', 'mp')
- first_out_grad: float32 [4096, 1024], P('mp', 'dp')
- attend_gain_grad: float32 [1024], replicated
- query_weight_grad: float32 [1024, 1024], P('dp', 'mp')
- key_weight_grad: float32 [1024, 1024], P('dp', 'mp')
- value_weight_grad: float32 [1024, 1024], P('dp', 'mp')
- attend_out_grad: float32 [1024, 1024], P('mp', 'dp')
- mixer_gain_grad: float32 [1024], replicated
- mixer_value_grad: float32 [1024, 1024], P('dp', 'mp')
- mixer_gate_grad: float32 [1024, 1024], P('dp', 'mp')
- mixer_depth_grad: float32 [5, 1024], P(None, 'mp')
- batch_scale_grad: float32 [1024], P('mp')
- batch_shift_grad: float32 [1024], P('mp')
- mixer_out_grad: float32 [1024, 1024], P('mp', 'dp')
- second_gain_grad: float32 [1024], replicated
- second_in_grad: float32 [1024, 4096], P('dp', 'mp')
- second_out_grad: float32 [4096, 1024], P('mp', 'dp')
- final_gain_grad: float32 [1024], replicated
- head_weight_grad: float32 [1024, 8192], P('dp', 'mp')
The draws below stay inside these ranges and needn't reach their ends.
Inputs may be any that keep to these rules, and one draw needn't show every extreme that they name: `lengths`: one utterance of every draw has exactly 1024 live frames. `masked_rows`: A row among the device's own 512 frames; where the device holds live frames, the row is one of them. `head_device`: among the 256 slots of one device, at most 64 name the same data index.
All inputs are finite; a program needn't handle non-finite values.
Results may differ from the reference program's by a relative error of at most 0.025.
Values may be sent and summed in bfloat16 or wider, within the bound.
No kernel may reach another device: no remote copies, remote signals or barrier semaphores. Data moves between devices by JAX's collectives and lax.ppermute only.
A program may use at most 256 MiB of HBM per device.

```python
import math
import jax
import jax.numpy as jnp
import numpy as np
from jax import lax

D = 1024
FF = 4096
HEADS = 8
HEAD_DIM = 128
VOCAB = 8192
KERNEL = 5
LEN = 1024
SEQ_DEV = 2
TOK_DEV = 2048
ROWS = 512
MASK_DEV = 256
CAP = 64
TOKENS = 16384
MASKED = 8192
N_DP = 8


def utterance_lengths(key):
    number = TOKENS // LEN
    drawn = jax.random.randint(jax.random.fold_in(key, 101), (number,), LEN // 2, LEN + 1)
    longest = jax.random.randint(jax.random.fold_in(key, 102), (), 0, number)
    return jnp.where(jnp.arange(number) == longest, LEN, drawn).astype(jnp.int32)


def draw_lengths(key, part):
    shared = utterance_lengths(key)
    return shared


def first_reaching(running, wanted):
    return jnp.searchsorted(running, wanted, side='left')


def draw_masked_rows(key, part):
    lengths = utterance_lengths(key)
    key = jax.random.fold_in(key, 5)
    devices = TOKENS // ROWS
    frame = jnp.arange(TOKENS).reshape(devices, ROWS)
    inside = (frame % LEN < lengths[frame // LEN]).astype(jnp.int32)
    running = jnp.cumsum(inside, axis=1)
    total = jnp.maximum(running[:, -1], 1)
    wanted = jax.random.randint(key, (devices, MASK_DEV), 0, 1 << 20) % total[:, None] + 1
    picked = jax.vmap(first_reaching)(running, wanted)
    return jnp.minimum(picked, ROWS - 1).reshape(MASKED).astype(jnp.int32)


def draw_frames(key, part):
    key = jax.random.fold_in(key, 7)
    groups = TOKENS // TOK_DEV
    place = (jnp.arange(TOKENS) // TOK_DEV).astype(jnp.float32)
    rise = place / max(groups - 1, 1)
    common = jnp.clip(jax.random.normal(jax.random.fold_in(key, 1), (D,), jnp.float32), -3.0, 3.0)
    noise = jnp.clip(jax.random.normal(jax.random.fold_in(key, 2), (TOKENS, D), jnp.float32), -4.0, 4.0)
    level = 0.5 + 2.0 * rise
    return (noise + level[:, None] * common[None, :]).astype(jnp.bfloat16)


def draw_head_weight(key, part):
    key = jax.random.fold_in(key, 9)
    column = jnp.arange(VOCAB).astype(jnp.float32) / VOCAB
    scale = 1.5 * jnp.exp2(column) * D ** (-0.5)
    base = jnp.clip(jax.random.normal(key, (D, VOCAB), jnp.float32), -4.0, 4.0)
    return (base * scale[None, :]).astype(jnp.bfloat16)


def place_ends(array, key, smallest, high):
    shape = array.shape
    index_at = [jax.random.randint(jax.random.fold_in(key, axis), (), 0, shape[axis]) for axis in range(len(shape))]
    array = array.at[tuple(index_at)].set(smallest)
    longest = shape.index(max(shape))
    index_at[longest] = (index_at[longest] + 1) % shape[longest]
    return array.at[tuple(index_at)].set(high)


def level_of(stream_key, shape, split, least, high):
    level, own = 1.0, jax.random.fold_in(stream_key, 6)
    for axis_at, blocks in split:
        draws = jnp.exp(jax.random.uniform(jax.random.fold_in(own, axis_at), (blocks,), jnp.float32, least / len(split), high / len(split)))
        level = level * jnp.repeat(draws, shape[axis_at] // blocks).reshape([-1 if axis == axis_at else 1 for axis in range(len(shape))])
    return level


def routed_block(own_key, own, number, rows, number_of, top, most, lean):
    order = jax.random.permutation(own_key, number_of)
    packed, usual = portions_of(number_of, rows * top, most, lean, True), portions_of(number_of, rows * top, most, lean, False)
    places = jnp.arange(number_of)

    def named(sizes, offset_by):
        used = int((sizes > 0).sum())
        fixed = max(1, used // 4)
        moved = fixed + (places - fixed + offset_by * (used - fixed)) % max(1, number_of - fixed)
        return jnp.zeros((number_of,), jnp.int32).at[order[jnp.where(places < fixed, places, moved)]].set(jnp.asarray(sizes, jnp.int32))

    sizes = jnp.where(number % 4 == 0, named(packed, number // 4), named(usual, number - number // 4 - 1))
    mixed = jax.random.permutation(jax.random.fold_in(own, 3), number_of)
    giver, receiver = mixed[0:number_of // 2 * 2:2], mixed[1:number_of // 2 * 2:2]
    margin = jnp.minimum(sizes[giver] - 1, most - sizes[receiver]) // 2
    margin = jnp.where((giver == order[0]) | (receiver == order[0]) | (sizes[receiver] == 0), 0, jnp.maximum(margin, 0))
    moved = jax.random.randint(jax.random.fold_in(own, 4), (number_of // 2,), 0, 1 << 20) % (margin + 1)
    sizes = sizes.at[giver].add(-moved).at[receiver].add(moved)
    labels = jnp.searchsorted(jnp.cumsum(sizes), jnp.arange(rows * top), side="right").astype(jnp.int32)
    table = labels.reshape(top, rows).T
    table = table[jax.random.permutation(jax.random.fold_in(own, 1), rows)]
    offset_by = jax.random.randint(jax.random.fold_in(own, 2), (rows, 1), 0, top)
    return jnp.take_along_axis(table, (jnp.arange(top)[None, :] + offset_by) % top, axis=1)


def portions_of(number_of, total, most, slope, full):
    portions = [(1 << 20) // math.isqrt(standing ** slope) + 1 for standing in range(1, number_of + 1)]
    largest = most if full else min(most, max(-(-total // number_of), total * portions[0] // sum(portions)))
    least = 1 if total - largest >= number_of - 1 else 0
    counts, spare = [largest] + [least] * (number_of - 1), total - largest - least * (number_of - 1)
    while spare > 0:
        movable = [i for i in range(1, number_of) if counts[i] < largest] or [i for i in range(1, number_of) if counts[i] < most]
        pool, budget = sum([portions[i] for i in movable]), spare
        for i in movable:
            extra = min(most - counts[i], max(1, budget * portions[i] // pool), spare)
            counts[i] = counts[i] + extra
            spare = spare - extra
    return np.array(counts)


def bell_draw(rng, extent, deviation, most, split=(), kind=jnp.bfloat16):
    result = deviation * jax.random.normal(rng, extent, jnp.float32)
    if split:
        result = result * level_of(rng, extent, split, -0.22, 0.18)
    return jnp.clip(result, -most, most).astype(kind)


def setup_inputs(seed: int = 0) -> dict:
    key_of = jax.random.split(jax.random.key(seed), 27)
    frames = draw_frames(jax.random.fold_in(key_of[26], 71), 0)
    out_cotangent = bell_draw(key_of[1], (TOKENS, D), 1.0, 6.0, ((0, 32),))
    lengths = draw_lengths(jax.random.fold_in(key_of[26], 71), 0)
    masked_rows = draw_masked_rows(jax.random.fold_in(key_of[26], 71), 0)
    targets = place_ends(jax.random.randint(key_of[4], (MASKED,), 0, VOCAB), jax.random.fold_in(key_of[4], 1), 0, VOCAB - 1).astype(jnp.int32)
    head_device_keys = jax.random.split(jax.random.fold_in(key_of[5], 1), MASKED // MASK_DEV)
    head_device_turns = jax.random.permutation(jax.random.fold_in(key_of[5], 3), MASKED // MASK_DEV)
    head_device = jax.vmap(lambda own, number: routed_block(jax.random.fold_in(key_of[5], 2), own, number, MASK_DEV, N_DP, 1, CAP, 2))(head_device_keys, head_device_turns).reshape((MASKED, 1))
    first_gain = jnp.clip(1.0 + 0.18 * jax.random.normal(key_of[6], (D,), jnp.float32), 0.1, 1.9)
    first_in = bell_draw(key_of[7], (D, FF), D ** -0.5, 0.1875, ((1, 4),))
    first_out = bell_draw(key_of[8], (FF, D), (FF // 4) ** -0.5, 0.1875, ((0, 4),))
    attend_gain = jnp.clip(1.0 + 0.18 * jax.random.normal(key_of[9], (D,), jnp.float32), 0.1, 1.9)
    query_weight = bell_draw(key_of[10], (D, D), (D // 4) ** -0.5, 0.375, ((1, 4),))
    key_weight = bell_draw(key_of[11], (D, D), D ** -0.5, 0.1875, ((1, 4),))
    value_weight = bell_draw(key_of[12], (D, D), D ** -0.5, 0.1875, ((1, 4),))
    attend_out = bell_draw(key_of[13], (D, D), (D // 16) ** -0.5, 0.75, ((0, 4),))
    mixer_gain = jnp.clip(1.0 + 0.18 * jax.random.normal(key_of[14], (D,), jnp.float32), 0.1, 1.9)
    mixer_value = bell_draw(key_of[15], (D, D), D ** -0.5, 0.1875, ((1, 4),))
    mixer_gate = bell_draw(key_of[16], (D, D), D ** -0.5, 0.1875, ((1, 4),))
    mixer_depth = bell_draw(key_of[17], (KERNEL, D), KERNEL ** -0.5, 2.5, ((1, 4),), jnp.float32)
    batch_scale = jnp.clip(1.0 + 0.18 * jax.random.normal(key_of[18], (D,), jnp.float32), 0.1, 1.9)
    batch_shift = bell_draw(key_of[19], (D,), 0.5, 3.0, ((0, 4),), jnp.float32)
    mixer_out = bell_draw(key_of[20], (D, D), D ** -0.5, 0.1875, ((0, 4),))
    second_gain = jnp.clip(1.0 + 0.18 * jax.random.normal(key_of[21], (D,), jnp.float32), 0.1, 1.9)
    second_in = bell_draw(key_of[22], (D, FF), D ** -0.5, 0.1875, ((1, 4),))
    second_out = bell_draw(key_of[23], (FF, D), (FF // 4) ** -0.5, 0.1875, ((0, 4),))
    final_gain = jnp.clip(1.0 + 0.18 * jax.random.normal(key_of[24], (D,), jnp.float32), 0.1, 1.9)
    head_weight = draw_head_weight(jax.random.fold_in(key_of[26], 71), 0)
    return {"frames": frames, "out_cotangent": out_cotangent, "lengths": lengths, "masked_rows": masked_rows, "targets": targets, "head_device": head_device, "first_gain": first_gain, "first_in": first_in, "first_out": first_out, "attend_gain": attend_gain, "query_weight": query_weight, "key_weight": key_weight, "value_weight": value_weight, "attend_out": attend_out, "mixer_gain": mixer_gain, "mixer_value": mixer_value, "mixer_gate": mixer_gate, "mixer_depth": mixer_depth, "batch_scale": batch_scale, "batch_shift": batch_shift, "mixer_out": mixer_out, "second_gain": second_gain, "second_in": second_in, "second_out": second_out, "final_gain": final_gain, "head_weight": head_weight}


@jax.custom_vjp
def low(v):
    return lax.optimization_barrier(v.astype(jnp.bfloat16)).astype(jnp.float32)

@jax.custom_vjp
def low_back(v):
    return v

def low_keep(v):
    return (low(v), None)

def low_pass(kept, grad):
    return (grad,)

def back_keep(v):
    return (v, None)

def back_low(kept, grad):
    return (low(grad),)
low.defvjp(low_keep, low_pass)
low_back.defvjp(back_keep, back_low)
NORM_EPSILON = 1e-05
MASKED_SCORE = -1000000000.0
HIGHEST_PRECISION = lax.Precision.HIGHEST

def matmul(left, right):
    return jnp.dot(left, right, precision=HIGHEST_PRECISION)

def layer_norm(values, gain):
    center = values - lax.optimization_barrier(jnp.mean(values, axis=-1, keepdims=True))
    spread = lax.optimization_barrier(jnp.mean(center * center, axis=-1, keepdims=True))
    return center * lax.rsqrt(spread + NORM_EPSILON) * gain

def swish(values):
    return values * jax.nn.sigmoid(values)

def rounded(values):
    return low(low_back(values))

def block_sum(left, right):
    return low_back(matmul(left, right))

def depth_conv(glu, depth):
    length = glu.shape[1]
    half = KERNEL // 2
    padded = jnp.pad(glu, ((0, 0), (half, half), (0, 0)))
    total = padded[:, 0:length] * depth[0]
    for offset in range(1, KERNEL):
        total = total + padded[:, offset:offset + length] * depth[offset]
    return total

def feed_forward(resid, gain, expand, project):
    normed = low(layer_norm(resid, gain))
    inner = low_back(matmul(normed, expand))
    return block_sum(low(swish(inner)), project)

def attend(resid, gain, query_weight, key_weight, value_weight, attend_out, live):
    normed = low(layer_norm(resid, gain))
    shape = (SEQ_DEV, LEN, HEADS, HEAD_DIM)
    query = rounded(matmul(normed, query_weight)).reshape(shape)
    keys = rounded(matmul(normed, key_weight)).reshape(shape)
    values = rounded(matmul(normed, value_weight)).reshape(shape)
    scores = jnp.einsum('sqhe,skhe->shqk', query, keys, precision=HIGHEST_PRECISION) * HEAD_DIM ** (-0.5)
    scores = jnp.where(live[:, None, None, :] > 0, low_back(scores), MASKED_SCORE)
    top = lax.optimization_barrier(jnp.max(scores, axis=-1, keepdims=True))
    lifted = jnp.exp(scores - top)
    shares = low(lifted / lax.optimization_barrier(jnp.sum(lifted, axis=-1, keepdims=True)))
    mixed = rounded(jnp.einsum('shqk,skhe->sqhe', shares, values, precision=HIGHEST_PRECISION))
    return block_sum(mixed.reshape(TOK_DEV, D), attend_out)

def mixer_front(resid, gain, mixer_value, mixer_gate, mixer_depth, live):
    normed = low(layer_norm(resid, gain))
    value_in = low_back(matmul(normed, mixer_value))
    gate_in = low_back(matmul(normed, mixer_gate))
    glu = (value_in * jax.nn.sigmoid(gate_in)).reshape(SEQ_DEV, LEN, D) * live[:, :, None]
    return depth_conv(glu, mixer_depth).reshape(TOK_DEV, D)

def reference(frames, out_cotangent, lengths, masked_rows, targets, head_device, first_gain, first_in, first_out, attend_gain, query_weight, key_weight, value_weight, attend_out, mixer_gain, mixer_value, mixer_gate, mixer_depth, batch_scale, batch_shift, mixer_out, second_gain, second_in, second_out, final_gain, head_weight):
    groups = TOKENS // TOK_DEV
    live = (jnp.arange(LEN)[None, :] < lengths[:, None]).astype(jnp.float32)
    live_groups = live.reshape(groups, SEQ_DEV, LEN)
    live_flat = live.reshape(TOKENS)
    places = (jnp.arange(MASKED) // MASK_DEV * ROWS + masked_rows).astype(jnp.int32)
    keep = live_flat[places]
    blocks = MASKED // MASK_DEV
    weights = (first_gain, first_in, first_out, attend_gain, query_weight, key_weight, value_weight, attend_out, mixer_gain, mixer_value, mixer_gate, mixer_depth, batch_scale, batch_shift, mixer_out, second_gain, second_in, second_out, final_gain, head_weight)
    weights = tuple((item.astype(jnp.float32) for item in weights))

    def forward(inputs, first_gain, first_in, first_out, attend_gain, query_weight, key_weight, value_weight, attend_out, mixer_gain, mixer_value, mixer_gate, mixer_depth, batch_scale, batch_shift, mixer_out, second_gain, second_in, second_out, final_gain, head_weight):

        def front(pair):
            block, alive = pair
            after_first = block + 0.5 * feed_forward(block, first_gain, first_in, first_out)
            after_attend = after_first + attend(after_first, attend_gain, query_weight, key_weight, value_weight, attend_out, alive)
            return (after_attend, mixer_front(after_attend, mixer_gain, mixer_value, mixer_gate, mixer_depth, alive))
        after_attend, convolved = lax.map(jax.checkpoint(front), (inputs.reshape(groups, TOK_DEV, D), live_groups))
        convolved = convolved.reshape(TOKENS, D)
        count = jnp.sum(live_flat)
        bn_mean = lax.optimization_barrier(jnp.sum(convolved * live_flat[:, None], axis=0)) / count
        bn_var = lax.optimization_barrier(jnp.sum(convolved * convolved * live_flat[:, None], axis=0)) / count - bn_mean * bn_mean
        shaped = (convolved - bn_mean) * lax.rsqrt(bn_var + NORM_EPSILON) * batch_scale + batch_shift

        def back_half(pair):
            resid, block = pair
            after_mixer = resid + block_sum(low(swish(block)), mixer_out)
            after_second = after_mixer + 0.5 * feed_forward(after_mixer, second_gain, second_in, second_out)
            return layer_norm(after_second, final_gain)
        output = lax.map(jax.checkpoint(back_half), (after_attend, shaped.reshape(groups, TOK_DEV, D))).reshape(TOKENS, D)
        chosen = rounded(output[places])

        def head_block(pair):
            rows_block, target_block, keep_block = pair
            logits = low_back(matmul(rows_block, head_weight))
            top = lax.optimization_barrier(jnp.max(logits, axis=-1, keepdims=True))
            log_total = top[:, 0] + jnp.log(lax.optimization_barrier(jnp.sum(jnp.exp(logits - top), axis=-1)))
            picked = jnp.take_along_axis(logits, target_block[:, None], axis=-1)[:, 0]
            return jnp.sum(keep_block * (log_total - picked))
        losses = lax.map(jax.checkpoint(head_block), (chosen.reshape(blocks, MASK_DEV, D), targets.reshape(blocks, MASK_DEV), keep.reshape(blocks, MASK_DEV)))
        return (output, jnp.sum(losses))
    results, pullback = jax.vjp(forward, frames.astype(jnp.float32), *weights)
    output, ce_sum = results
    grads = pullback((out_cotangent.astype(jnp.float32), jnp.ones((), jnp.float32)))
    input_grad, first_gain_grad, first_in_grad, first_out_grad, attend_gain_grad, query_weight_grad, key_weight_grad, value_weight_grad, attend_out_grad, mixer_gain_grad, mixer_value_grad, mixer_gate_grad, mixer_depth_grad, batch_scale_grad, batch_shift_grad, mixer_out_grad, second_gain_grad, second_in_grad, second_out_grad, final_gain_grad, head_weight_grad = grads
    loss = ce_sum / jnp.sum(keep)
    return (output, loss, input_grad, first_gain_grad, first_in_grad, first_out_grad, attend_gain_grad, query_weight_grad, key_weight_grad, value_weight_grad, attend_out_grad, mixer_gain_grad, mixer_value_grad, mixer_gate_grad, mixer_depth_grad, batch_scale_grad, batch_shift_grad, mixer_out_grad, second_gain_grad, second_in_grad, second_out_grad, final_gain_grad, head_weight_grad)
```

```python
import jax
import jax.numpy as jnp
from jax import lax
from jax.experimental import pallas as pl
from jax.experimental.pallas import tpu as pltpu
from jax.sharding import PartitionSpec as P

D = 1024
HEAD_DIM = 128
KERNEL = 5
LEN = 1024
SEQ_DEV = 2
TOK_DEV = 2048


NORM_EPSILON = 1e-05
MASKED_SCORE = -1000000000.0


def joined(shard, axis, combine):
    everything = jax.tree.map(lambda part: lax.all_gather(part, axis), shard)
    leading = jax.tree.map(lambda part: part[0], everything)

    def hop(k, so_far):
        return combine(so_far, jax.tree.map(lambda part: part[k], everything))

    return lax.fori_loop(1, lax.axis_size(axis), hop, leading)


def layer_norm(values, gain):
    center = values - jnp.mean(values, axis=-1, keepdims=True)
    spread = jnp.mean(center * center, axis=-1, keepdims=True)
    return center * lax.rsqrt(spread + NORM_EPSILON) * gain


def swish(values):
    return values * jax.nn.sigmoid(values)


def swish_slope(values):
    sigma = jax.nn.sigmoid(values)
    return sigma * (1.0 + values * (1.0 - sigma))


def depth_conv(glu, depth):
    length = glu.shape[1]
    half = KERNEL // 2
    padded = jnp.pad(glu, ((0, 0), (half, half), (0, 0)))
    total = padded[:, 0:length] * depth[0]
    for offset in range(1, KERNEL):
        total = total + padded[:, offset : offset + length] * depth[offset]
    return total


def matmul(left, right):
    return jnp.dot(left, right, preferred_element_type=jnp.float32)


def matmul_t(left, right):
    return lax.dot_general(
        left, right, (((1,), (1,)), ((), ())), preferred_element_type=jnp.float32
    )


def weight_term(left, right):
    return lax.dot_general(
        left, right, (((0,), (0,)), ((), ())), preferred_element_type=jnp.float32
    )


def spread_rows(values):
    return lax.all_gather(values, "mp", axis=0, tiled=True)


def collect_rows(values):
    return lax.psum_scatter(values, "mp", scatter_dimension=0, tiled=True)


def spread_grads(values):
    return lax.all_gather(values, "mp", axis=0, tiled=True)


def collect_grads(values):
    return lax.psum_scatter(values, "mp", scatter_dimension=0, tiled=True)


def weight_grad(left, right):
    return weight_term(left, right)


def combine_parts(first, second):
    top = jnp.maximum(first[0], second[0])
    total = first[1] * jnp.exp(first[0] - top) + second[1] * jnp.exp(second[0] - top)
    return (top, total)


def feed_forward(resid, gain, expand, project):
    normed, norm_pullback = jax.vjp(layer_norm, resid, gain)
    gathered = spread_rows(normed.astype(jnp.bfloat16))
    inner = matmul(gathered, expand)
    active = swish(inner).astype(jnp.bfloat16)
    return (collect_rows(matmul(active, project)), (norm_pullback, gathered, inner, active))


def feed_backward(expand, project, kept, grad_branch):
    norm_pullback, gathered, inner, active = kept
    grad_full = spread_grads(grad_branch.astype(jnp.bfloat16))
    grad_inner = (matmul_t(grad_full, project) * swish_slope(inner)).astype(jnp.bfloat16)
    grad_project = weight_grad(grad_full, active)
    grad_expand = weight_grad(gathered, grad_inner)
    grad_resid, grad_gain = norm_pullback(collect_grads(matmul_t(grad_inner, expand)))
    return (grad_resid, grad_gain, grad_expand, grad_project)


def attend_forward(resid, gain, query_weight, key_weight, value_weight, attend_out, live):
    normed, norm_pullback = jax.vjp(layer_norm, resid, gain)
    gathered = spread_rows(normed.astype(jnp.bfloat16))
    width = query_weight.shape[1]
    shape = (SEQ_DEV, LEN, width // HEAD_DIM, HEAD_DIM)
    query = matmul(gathered, query_weight).astype(jnp.bfloat16).reshape(shape)
    keys = matmul(gathered, key_weight).astype(jnp.bfloat16).reshape(shape)
    values = matmul(gathered, value_weight).astype(jnp.bfloat16).reshape(shape)
    scale = HEAD_DIM ** (-0.5)

    def one_utterance(pack):
        query_part, keys_part, values_part, alive = pack
        scores = (
            jnp.einsum("qhe,khe->hqk", query_part, keys_part, preferred_element_type=jnp.float32)
            * scale
        )
        scores = jnp.where(alive[None, None, :] > 0, scores, MASKED_SCORE)
        top = jnp.max(scores, axis=-1, keepdims=True)
        lifted = jnp.exp(scores - top)
        total = jnp.sum(lifted, axis=-1, keepdims=True)
        shares = (lifted / total).astype(jnp.bfloat16)
        mixed_part = jnp.einsum(
            "hqk,khe->qhe", shares, values_part, preferred_element_type=jnp.float32
        )
        return (mixed_part.astype(jnp.bfloat16), (top + jnp.log(total))[:, :, 0])

    mixed, log_total = lax.map(one_utterance, (query, keys, values, live))
    mixed = mixed.reshape(TOK_DEV, width)
    branch = collect_rows(matmul(mixed, attend_out))
    return (branch, (norm_pullback, gathered, query, keys, values, mixed, log_total))


def attend_backward(query_weight, key_weight, value_weight, attend_out, live, kept, grad_branch):
    norm_pullback, gathered, query, keys, values, mixed, log_total = kept
    width = query_weight.shape[1]
    grad_full = spread_grads(grad_branch.astype(jnp.bfloat16))
    grad_mixed = matmul_t(grad_full, attend_out).astype(jnp.bfloat16).reshape(query.shape)
    grad_attend_out = weight_grad(grad_full, mixed)
    scale = HEAD_DIM ** (-0.5)

    def one_utterance(pack):
        query_part, keys_part, values_part, alive, log_part, grad_part = pack
        scores = (
            jnp.einsum("qhe,khe->hqk", query_part, keys_part, preferred_element_type=jnp.float32)
            * scale
        )
        scores = jnp.where(alive[None, None, :] > 0, scores, MASKED_SCORE)
        shares = jnp.exp(scores - log_part[:, :, None])
        grad_values = jnp.einsum(
            "hqk,qhe->khe",
            shares.astype(jnp.bfloat16),
            grad_part,
            preferred_element_type=jnp.float32,
        )
        grad_shares = jnp.einsum(
            "qhe,khe->hqk", grad_part, values_part, preferred_element_type=jnp.float32
        )
        inner = jnp.sum(shares * grad_shares, axis=-1, keepdims=True)
        grad_scores = (shares * (grad_shares - inner)).astype(jnp.bfloat16)
        grad_query = (
            jnp.einsum("hqk,khe->qhe", grad_scores, keys_part, preferred_element_type=jnp.float32)
            * scale
        )
        grad_keys = (
            jnp.einsum("hqk,qhe->khe", grad_scores, query_part, preferred_element_type=jnp.float32)
            * scale
        )
        return (
            grad_query.astype(jnp.bfloat16),
            grad_keys.astype(jnp.bfloat16),
            grad_values.astype(jnp.bfloat16),
        )

    grad_query, grad_keys, grad_values = lax.map(
        one_utterance, (query, keys, values, live, log_total, grad_mixed)
    )
    grad_query = grad_query.reshape(TOK_DEV, width)
    grad_keys = grad_keys.reshape(TOK_DEV, width)
    grad_values = grad_values.reshape(TOK_DEV, width)
    grad_query_weight = weight_grad(gathered, grad_query)
    grad_key_weight = weight_grad(gathered, grad_keys)
    grad_value_weight = weight_grad(gathered, grad_values)
    summed = (
        matmul_t(grad_query, query_weight)
        + matmul_t(grad_keys, key_weight)
        + matmul_t(grad_values, value_weight)
    )
    grad_resid, grad_gain = norm_pullback(collect_grads(summed))
    return (
        grad_resid,
        grad_gain,
        grad_query_weight,
        grad_key_weight,
        grad_value_weight,
        grad_attend_out,
    )


def mixer_forward(
    resid,
    gain,
    mixer_value,
    mixer_gate,
    mixer_depth,
    batch_scale,
    batch_shift,
    mixer_out,
    live_flat,
):
    normed, norm_pullback = jax.vjp(layer_norm, resid, gain)
    gathered = spread_rows(normed.astype(jnp.bfloat16))
    value_in = matmul(gathered, mixer_value)
    gate_in = matmul(gathered, mixer_gate)
    channels = value_in.shape[1]

    def front(value_part, gate_part, depth):
        glu = value_part * jax.nn.sigmoid(gate_part) * live_flat[:, None]
        return depth_conv(glu.reshape(SEQ_DEV, LEN, channels), depth).reshape(TOK_DEV, channels)

    convolved, front_pullback = jax.vjp(front, value_in, gate_in, mixer_depth)
    weighted = convolved * live_flat[:, None]
    count, first_sum, second_sum = lax.psum(
        (jnp.sum(live_flat), jnp.sum(weighted, axis=0), jnp.sum(weighted * convolved, axis=0)), "dp"
    )
    bn_mean = first_sum / count
    inverse = lax.rsqrt(second_sum / count - bn_mean * bn_mean + NORM_EPSILON)
    normal = (convolved - bn_mean) * inverse
    shaped = normal * batch_scale + batch_shift
    active = swish(shaped).astype(jnp.bfloat16)
    branch = collect_rows(matmul(active, mixer_out))
    return (
        branch,
        (norm_pullback, gathered, front_pullback, normal, inverse, count, shaped, active),
    )


def mixer_backward(mixer_value, mixer_gate, batch_scale, mixer_out, live_flat, kept, grad_branch):
    norm_pullback, gathered, front_pullback, normal, inverse, count, shaped, active = kept
    grad_full = spread_grads(grad_branch.astype(jnp.bfloat16))
    grad_mixer_out = weight_grad(grad_full, active)
    grad_shaped = matmul_t(grad_full, mixer_out) * swish_slope(shaped)
    shift_grad, scale_grad = lax.psum(
        (jnp.sum(grad_shaped, axis=0), jnp.sum(grad_shaped * normal, axis=0)), "dp"
    )
    grad_conv = (
        batch_scale
        * inverse
        * (grad_shaped - live_flat[:, None] / count * (shift_grad + normal * scale_grad))
    )
    grad_value, grad_gate, depth_grad = front_pullback(grad_conv)
    grad_value = grad_value.astype(jnp.bfloat16)
    grad_gate = grad_gate.astype(jnp.bfloat16)
    grad_mixer_value = weight_grad(gathered, grad_value)
    grad_mixer_gate = weight_grad(gathered, grad_gate)
    summed = matmul_t(grad_value, mixer_value) + matmul_t(grad_gate, mixer_gate)
    grad_resid, grad_gain = norm_pullback(collect_grads(summed))
    return (
        grad_resid,
        grad_gain,
        grad_mixer_value,
        grad_mixer_gate,
        depth_grad,
        scale_grad,
        shift_grad,
        grad_mixer_out,
    )


def masked_head(output, own_live, masked_rows, targets, head_device, head_weight):
    rows = output.shape[0]
    sources = lax.axis_size("dp")
    capacity = rows // sources
    keep = own_live[masked_rows]
    chosen = output[masked_rows].astype(jnp.bfloat16)
    destination = head_device[:, 0]
    marks = (destination[:, None] == jnp.arange(sources)[None, :]).astype(jnp.int32)
    order = jnp.sum((jnp.cumsum(marks, axis=0) - marks) * marks, axis=1)
    placer = (destination * capacity + order)[:, None] == jnp.arange(rows)[None, :]
    packed = weight_term(placer.astype(jnp.bfloat16), chosen).astype(jnp.bfloat16)
    labels = (targets + 1) * (keep > 0).astype(jnp.int32)
    codes = jnp.sum(jnp.where(placer, labels[:, None], 0), axis=0)
    arrived, arrived_codes = (
        lax.all_to_all(packed, "dp", split_axis=0, concat_axis=0, tiled=True),
        lax.all_to_all(codes, "dp", split_axis=0, concat_axis=0, tiled=True),
    )
    shared, shared_codes = (
        lax.all_gather(arrived, "mp", axis=0, tiled=True),
        lax.all_gather(arrived_codes, "mp", axis=0, tiled=True),
    )
    logits = matmul(shared, head_weight)
    vocab = head_weight.shape[1]
    hits = (shared_codes - 1 - lax.axis_index("mp") * vocab)[:, None] == jnp.arange(vocab)[None, :]
    top = jnp.max(logits, axis=1)
    total = jnp.sum(jnp.exp(logits - top[:, None]), axis=1)
    picked = jnp.sum(jnp.where(hits, logits, 0.0), axis=1)
    top_all, total_all = joined((top, total), "mp", combine_parts)
    log_total = top_all + jnp.log(total_all)
    counted = (shared_codes > 0).astype(jnp.float32)
    own_total = jnp.sum(
        lax.dynamic_slice_in_dim(counted * log_total, lax.axis_index("mp") * rows, rows)
    )
    own_loss = own_total - jnp.sum(counted * picked)
    grad_logits = (
        counted[:, None] * (jnp.exp(logits - log_total[:, None]) - hits.astype(jnp.float32))
    ).astype(jnp.bfloat16)
    grad_head = weight_grad(shared, grad_logits)
    grad_shared = lax.psum_scatter(
        matmul_t(grad_logits, head_weight), "mp", scatter_dimension=0, tiled=True
    )
    returned = lax.all_to_all(
        grad_shared.astype(jnp.bfloat16), "dp", split_axis=0, concat_axis=0, tiled=True
    )
    grad_chosen = matmul(placer.astype(jnp.bfloat16), returned).astype(jnp.bfloat16)
    picker = (masked_rows[:, None] == jnp.arange(rows)[None, :]).astype(jnp.bfloat16)
    grad_rows = weight_term(picker, grad_chosen)
    return (grad_rows, grad_head, own_loss, jnp.sum(keep))


def on_device_any(
    frames,
    out_cotangent,
    lengths,
    masked_rows,
    targets,
    head_device,
    first_gain,
    first_in,
    first_out,
    attend_gain,
    query_weight,
    key_weight,
    value_weight,
    attend_out,
    mixer_gain,
    mixer_value,
    mixer_gate,
    mixer_depth,
    batch_scale,
    batch_shift,
    mixer_out,
    second_gain,
    second_in,
    second_out,
    final_gain,
    head_weight,
):
    rows = frames.shape[0]
    live = (jnp.arange(LEN)[None, :] < lengths[:, None]).astype(jnp.float32)
    live_flat = live.reshape(TOK_DEV)
    own_live = lax.dynamic_slice_in_dim(live_flat, lax.axis_index("mp") * rows, rows)
    start = frames.astype(jnp.float32)
    branch, first_kept = feed_forward(start, first_gain, first_in, first_out)
    after_first = start + 0.5 * branch
    branch, attend_kept = attend_forward(
        after_first, attend_gain, query_weight, key_weight, value_weight, attend_out, live
    )
    after_attend = after_first + branch
    branch, mixer_kept = mixer_forward(
        after_attend,
        mixer_gain,
        mixer_value,
        mixer_gate,
        mixer_depth,
        batch_scale,
        batch_shift,
        mixer_out,
        live_flat,
    )
    after_mixer = after_attend + branch
    branch, second_kept = feed_forward(after_mixer, second_gain, second_in, second_out)
    after_second = after_mixer + 0.5 * branch
    output, final_pullback = jax.vjp(layer_norm, after_second, final_gain)
    grad_rows, grad_head, own_loss, own_count = masked_head(
        output, own_live, masked_rows, targets, head_device, head_weight
    )
    grad_second, final_gain_grad = final_pullback(out_cotangent.astype(jnp.float32) + grad_rows)
    back_resid, second_gain_grad, grad_second_in, grad_second_out = feed_backward(
        second_in, second_out, second_kept, 0.5 * grad_second
    )
    grad_mixer = grad_second + back_resid
    (
        back_resid,
        mixer_gain_grad,
        grad_mixer_value,
        grad_mixer_gate,
        depth_grad,
        batch_scale_grad,
        batch_shift_grad,
        grad_mixer_out,
    ) = mixer_backward(
        mixer_value, mixer_gate, batch_scale, mixer_out, live_flat, mixer_kept, grad_mixer
    )
    grad_attend = grad_mixer + back_resid
    back_resid, attend_gain_grad, grad_query, grad_key, grad_value, grad_attend_out = (
        attend_backward(
            query_weight, key_weight, value_weight, attend_out, live, attend_kept, grad_attend
        )
    )
    grad_first = grad_attend + back_resid
    back_resid, first_gain_grad, grad_first_in, grad_first_out = feed_backward(
        first_in, first_out, first_kept, 0.5 * grad_first
    )
    input_grad = grad_first + back_resid
    channels = mixer_value.shape[1]
    offset = lax.axis_index("mp") * channels
    depth_full = lax.dynamic_update_slice_in_dim(
        jnp.zeros((KERNEL, D), jnp.float32), depth_grad, offset, 1
    )
    (
        first_gain_grad,
        attend_gain_grad,
        mixer_gain_grad,
        second_gain_grad,
        final_gain_grad,
        depth_full,
        loss_sum,
        loss_count,
    ) = lax.psum(
        (
            first_gain_grad,
            attend_gain_grad,
            mixer_gain_grad,
            second_gain_grad,
            final_gain_grad,
            depth_full,
            own_loss,
            own_count,
        ),
        ("dp", "mp"),
    )
    mixer_depth_grad = lax.dynamic_slice_in_dim(depth_full, offset, channels, 1)
    loss = loss_sum / loss_count
    (
        grad_first_in,
        grad_first_out,
        grad_query,
        grad_key,
        grad_value,
        grad_attend_out,
        grad_mixer_value,
        grad_mixer_gate,
        grad_mixer_out,
        grad_second_in,
        grad_second_out,
        grad_head,
    ) = (
        lax.psum_scatter(grad_first_in, "dp", scatter_dimension=0, tiled=True),
        lax.psum_scatter(grad_first_out, "dp", scatter_dimension=0, tiled=True),
        lax.psum_scatter(grad_query, "dp", scatter_dimension=0, tiled=True),
        lax.psum_scatter(grad_key, "dp", scatter_dimension=0, tiled=True),
        lax.psum_scatter(grad_value, "dp", scatter_dimension=0, tiled=True),
        lax.psum_scatter(grad_attend_out, "dp", scatter_dimension=0, tiled=True),
        lax.psum_scatter(grad_mixer_value, "dp", scatter_dimension=0, tiled=True),
        lax.psum_scatter(grad_mixer_gate, "dp", scatter_dimension=0, tiled=True),
        lax.psum_scatter(grad_mixer_out, "dp", scatter_dimension=0, tiled=True),
        lax.psum_scatter(grad_second_in, "dp", scatter_dimension=0, tiled=True),
        lax.psum_scatter(grad_second_out, "dp", scatter_dimension=0, tiled=True),
        lax.psum_scatter(grad_head, "dp", scatter_dimension=0, tiled=True),
    )
    return (
        output,
        loss,
        input_grad,
        first_gain_grad,
        grad_first_in,
        grad_first_out.T,
        attend_gain_grad,
        grad_query,
        grad_key,
        grad_value,
        grad_attend_out.T,
        mixer_gain_grad,
        grad_mixer_value,
        grad_mixer_gate,
        mixer_depth_grad,
        batch_scale_grad,
        batch_shift_grad,
        grad_mixer_out.T,
        second_gain_grad,
        grad_second_in,
        grad_second_out.T,
        final_gain_grad,
        grad_head,
    )


BF16 = jnp.bfloat16
F32 = jnp.float32
SCALE = HEAD_DIM ** (-0.5)
CORE_PAIRS = [(0, 1), (1, 0), (2, 3), (3, 2)]
CHIP_PAIRS = [(0, 2), (2, 0), (1, 3), (3, 1)]
X_PAIRS = [(0, 1), (1, 0), (2, 3), (3, 2), (4, 5), (5, 4), (6, 7), (7, 6)]
Z_NEAR_PAIRS = [(0, 2), (2, 0), (1, 3), (3, 1), (4, 6), (6, 4), (5, 7), (7, 5)]
Z_FAR_PAIRS = [(0, 4), (4, 0), (1, 5), (5, 1), (2, 6), (6, 2), (3, 7), (7, 3)]


def swap(values):
    return lax.ppermute(values, "mp", CORE_PAIRS)


def cross(values):
    return lax.ppermute(values, "mp", CHIP_PAIRS)


def sum_over_dp(values):
    for pairs in (X_PAIRS, Z_NEAR_PAIRS, Z_FAR_PAIRS):
        values = values + lax.ppermute(values, "dp", pairs)
    return values


def sum_over_all(values):
    values = values + swap(values)
    values = values + cross(values)
    return sum_over_dp(values)


def sum_channels(values):
    other = cross(values)
    half = values.shape[-1] // 2
    turned = jnp.concatenate([other[..., half:], other[..., :half]], axis=-1)
    return sum_over_dp(values + turned)


def norm_forward(values, gain):
    center = values - jnp.mean(values, axis=-1, keepdims=True)
    spread = jnp.mean(center * center, axis=-1, keepdims=True)
    inverse = lax.rsqrt(spread + NORM_EPSILON)
    unit = center * inverse
    return (unit * gain, (unit, inverse))


def norm_backward(kept, gain, grad):
    unit, inverse = kept
    grad_gain = jnp.sum(grad * unit, axis=0, keepdims=True)
    scaled = grad * gain
    inner = jnp.mean(scaled * unit, axis=-1, keepdims=True)
    return (inverse * (scaled - jnp.mean(scaled, axis=-1, keepdims=True) - unit * inner), grad_gain)


def on_chip(values):
    return jnp.concatenate([values, swap(values)], axis=0)


def on_chip_sum(values):
    half = values.shape[0] // 2
    return values[:half].astype(F32) + swap(values[half:]).astype(F32)


def gather_parts(values, number):
    step = values.shape[0] // number
    far = [cross(values[k * step : (k + 1) * step]) for k in range(number)]
    near = on_chip(values)
    return [on_chip(part) for part in far] + [near]


def scatter_parts(parts):
    far = [cross(on_chip_sum(part).astype(BF16)) for part in parts[:-1]]
    far = far[0] if len(far) == 1 else jnp.concatenate(far, axis=0)
    return on_chip_sum(parts[-1]) + far.astype(F32)


def dot(left, right, kind=F32):
    return jnp.dot(left, right, preferred_element_type=F32).astype(kind)


def dot_t(left, right, kind=F32):
    return matmul_t(left, right).astype(kind)


def dot_rows(lefts, rights):
    total = weight_term(lefts, rights)
    return total.astype(BF16)


def branch_forward(resid, gain, expand, project, number):
    normed, norm_kept = norm_forward(resid, gain)
    parts = gather_parts(normed.astype(BF16), number)
    inners, actives, results = [], [], []
    for part in parts:
        inner = dot(part, expand)
        inners.append(inner.astype(BF16))
        active = swish(inner).astype(BF16)
        actives.append(active)
        results.append(dot(active, project, BF16))
    return (scatter_parts(results), (norm_kept, parts, inners, actives))


def branch_backward(gain, expand, project, kept, grad_branch, number):
    norm_kept, parts, inners, actives = kept
    grads = gather_parts(grad_branch.astype(BF16), number)
    grad_inners, results = [], []
    for grad, inner in zip(grads, inners):
        grad_inner = (matmul_t(grad, project) * swish_slope(inner.astype(F32))).astype(BF16)
        grad_inners.append(grad_inner)
        results.append(dot_t(grad_inner, expand, BF16))
    grad_resid, grad_gain = norm_backward(norm_kept, gain, scatter_parts(results))
    whole = lambda pieces: jnp.concatenate(pieces, axis=0)
    grad_project = dot_rows(whole(grads), whole(actives))
    grad_expand = dot_rows(whole(parts), whole(grad_inners))
    return (grad_resid, grad_gain, grad_expand, grad_project)


def attend_kernel(live_ref, query_ref, keys_ref, values_ref, mixed_ref, total_ref):
    scores = matmul_t(keys_ref[...], query_ref[...]) * SCALE
    scores = jnp.where(live_ref[...] > 0, scores, MASKED_SCORE)
    top = jnp.max(scores, axis=0, keepdims=True)
    lifted = jnp.exp(scores - top)
    total = jnp.sum(lifted, axis=0, keepdims=True)
    mixed = weight_term(values_ref[...], lifted.astype(BF16)) * (1.0 / total)
    mixed_ref[...] = mixed.T.astype(BF16)
    total_ref[0] = top + jnp.log(total)


def head_column(head, kind):
    return (head // 2) * 6 + kind * 2 + head % 2


def attend_forward_call(qkv, live_column):
    length = qkv.shape[0]
    heads = qkv.shape[1] // (3 * HEAD_DIM)
    block = length // 2

    def whole(kind):
        return pl.BlockSpec((length, HEAD_DIM), lambda h, b: (0, head_column(h, kind)))

    return pl.pallas_call(
        attend_kernel,
        grid=(heads, length // block),
        in_specs=[
            pl.BlockSpec((length, 1), lambda h, b: (0, 0)),
            pl.BlockSpec((block, HEAD_DIM), lambda h, b: (b, head_column(h, 0))),
            whole(1),
            whole(2),
        ],
        out_specs=[
            pl.BlockSpec((block, HEAD_DIM), lambda h, b: (b, h)),
            pl.BlockSpec((1, 1, block), lambda h, b: (h, 0, b)),
        ],
        out_shape=[
            jax.ShapeDtypeStruct((length, heads * HEAD_DIM), BF16),
            jax.ShapeDtypeStruct((heads, 1, length), F32),
        ],
        compiler_params=pltpu.CompilerParams(vmem_limit_bytes=32 << 20),
        cost_estimate=pl.CostEstimate(
            flops=4 * heads * length * length * HEAD_DIM,
            bytes_accessed=8 * length * heads * HEAD_DIM,
            transcendentals=heads * length * length,
        ),
        name="attend_forward",
    )(live_column, qkv, qkv, qkv)


def attend_back_kernel(
    live_ref, query_ref, keys_ref, values_ref, grad_ref, total_ref, out_ref, keys_sum, values_sum
):
    head, block = pl.program_id(0), pl.program_id(1)
    rows = query_ref.shape[0]
    query, keys, grad = query_ref[...], keys_ref[...], grad_ref[...]
    scores = matmul_t(keys, query) * SCALE
    scores = jnp.where(live_ref[...] > 0, scores, MASKED_SCORE)
    shares = jnp.exp(scores - total_ref[0])
    grad_shares = matmul_t(values_ref[...], grad)
    inner = jnp.sum(shares * grad_shares, axis=0, keepdims=True)
    grad_scores = (shares * (grad_shares - inner)).astype(BF16)
    grad_values = dot(shares.astype(BF16), grad)
    grad_keys = dot(grad_scores, query) * SCALE
    grad_query = (weight_term(keys, grad_scores) * SCALE).T.astype(BF16)

    def columns(kind):
        start = head_column(head, kind) * HEAD_DIM
        return pl.ds(pl.multiple_of(start, HEAD_DIM), HEAD_DIM)

    out_ref[pl.ds(pl.multiple_of(block * rows, rows), rows), columns(0)] = grad_query

    @pl.when(block == 0)
    def _():
        keys_sum[...] = grad_keys
        values_sum[...] = grad_values

    @pl.when(block > 0)
    def _():
        keys_sum[...] += grad_keys
        values_sum[...] += grad_values

    @pl.when(block == pl.num_programs(1) - 1)
    def _():
        out_ref[:, columns(1)] = keys_sum[...].astype(BF16)
        out_ref[:, columns(2)] = values_sum[...].astype(BF16)


def attend_backward_call(qkv, live_column, grad_mixed, log_total):
    length = qkv.shape[0]
    heads = qkv.shape[1] // (3 * HEAD_DIM)
    block = length // 2

    def whole(kind):
        return pl.BlockSpec((length, HEAD_DIM), lambda h, b: (0, head_column(h, kind)))

    return pl.pallas_call(
        attend_back_kernel,
        grid=(heads, length // block),
        in_specs=[
            pl.BlockSpec((length, 1), lambda h, b: (0, 0)),
            pl.BlockSpec((block, HEAD_DIM), lambda h, b: (b, head_column(h, 0))),
            whole(1),
            whole(2),
            pl.BlockSpec((block, HEAD_DIM), lambda h, b: (b, h)),
            pl.BlockSpec((1, 1, block), lambda h, b: (h, 0, b)),
        ],
        out_specs=pl.BlockSpec(qkv.shape, lambda h, b: (0, 0)),
        out_shape=jax.ShapeDtypeStruct(qkv.shape, BF16),
        scratch_shapes=[pltpu.VMEM((length, HEAD_DIM), F32), pltpu.VMEM((length, HEAD_DIM), F32)],
        compiler_params=pltpu.CompilerParams(vmem_limit_bytes=40 << 20),
        cost_estimate=pl.CostEstimate(
            flops=10 * heads * length * length * HEAD_DIM,
            bytes_accessed=16 * length * heads * HEAD_DIM,
            transcendentals=heads * length * length,
        ),
        name="attend_backward",
    )(live_column, qkv, qkv, qkv, grad_mixed, log_total)


def shifted(values, offset, position):
    if offset == 0:
        return values
    moved = jnp.roll(values, -offset, axis=0)
    place = position + offset
    return jnp.where((place >= 0) & (place < LEN), moved, 0.0)


def fetch_other(packed):
    number = lax.axis_size("dp")
    rows = packed.shape[0] // number
    piece = lax.dynamic_slice_in_dim(packed, lax.axis_index("dp") * rows, rows)
    return lax.all_gather(cross(piece), "dp", axis=0, tiled=True)


def reduce_weights(grads):
    sizes = [grad.shape[1] for grad in grads]
    packed = grads[0] if len(grads) == 1 else jnp.concatenate(grads, axis=1)
    reduced = lax.psum_scatter(packed, "dp", scatter_dimension=0, tiled=True).astype(F32)
    results, start = [], 0
    for size in sizes:
        results.append(reduced[:, start : start + size])
        start += size
    return results


def on_device_block(
    frames,
    out_cotangent,
    lengths,
    masked_rows,
    targets,
    head_device,
    first_gain,
    first_in,
    first_out,
    attend_gain,
    query_weight,
    key_weight,
    value_weight,
    attend_out,
    mixer_gain,
    mixer_value,
    mixer_gate,
    mixer_depth,
    batch_scale,
    batch_shift,
    mixer_out,
    second_gain,
    second_in,
    second_out,
    final_gain,
    head_weight,
):
    rows = frames.shape[0]
    own = lax.axis_index("mp")
    core, chip = own % 2, own // 2
    length = lax.dynamic_index_in_dim(lengths, chip, 0, keepdims=False)
    position = (jnp.arange(LEN) + core * rows) % LEN
    live = (position < length).astype(F32)
    live_column = live[:, None]
    place = position[:, None]

    attend_pack = jnp.concatenate(
        [query_weight, key_weight, value_weight, attend_out.reshape(D, -1)], axis=1
    )
    mixer_pack = jnp.concatenate([mixer_value, mixer_gate, mixer_out.reshape(D, -1)], axis=1)
    width = query_weight.shape[1]
    attend_other = fetch_other(attend_pack)
    mixer_other = fetch_other(mixer_pack)

    start = frames.astype(F32)
    branch, first_kept = branch_forward(start, first_gain, first_in, first_out, 2)
    after_first = start + 0.5 * branch

    qkv_weight = jnp.concatenate([attend_pack[:, : 3 * width], attend_other[:, : 3 * width]], axis=1)
    attend_out_both = jnp.concatenate(
        [attend_out, attend_other[:, 3 * width :].reshape(width, D)], axis=0
    )
    normed, attend_norm = norm_forward(after_first, attend_gain)
    attend_in = on_chip(normed.astype(BF16))
    qkv = dot(attend_in, qkv_weight, BF16)
    mixed, log_total = attend_forward_call(qkv, live_column)
    after_attend = after_first + on_chip_sum(dot(mixed, attend_out_both, BF16))

    value_both = jnp.concatenate([mixer_value, mixer_other[:, :width]], axis=1)
    gate_both = jnp.concatenate([mixer_gate, mixer_other[:, width : 2 * width]], axis=1)
    mixer_out_both = jnp.concatenate(
        [mixer_out, mixer_other[:, 2 * width :].reshape(width, D)], axis=0
    )
    channels = jnp.concatenate([mixer_depth, batch_scale[None], batch_shift[None]], axis=0)
    channels = jnp.concatenate([channels, cross(channels)], axis=1)
    depth, scale_both, shift_both = channels[:KERNEL], channels[KERNEL], channels[KERNEL + 1]
    normed, mixer_norm = norm_forward(after_attend, mixer_gain)
    mixer_in = on_chip(normed.astype(BF16))
    value_in = dot(mixer_in, value_both)
    gate_in = dot(mixer_in, gate_both)
    gate = jax.nn.sigmoid(gate_in)
    glu = value_in * gate * live_column
    half = KERNEL // 2
    convolved = sum(shifted(glu, j - half, place) * depth[j] for j in range(KERNEL))
    weighted = convolved * live_column
    sums = jnp.stack(
        [
            jnp.sum(weighted, axis=0),
            jnp.sum(weighted * convolved, axis=0),
            jnp.broadcast_to(jnp.sum(live), (2 * width,)),
        ]
    )
    sums = sum_channels(sums)
    count = sums[2]
    bn_mean = sums[0] / count
    inverse = lax.rsqrt(sums[1] / count - bn_mean * bn_mean + NORM_EPSILON)
    normal = (convolved - bn_mean) * inverse
    shaped = normal * scale_both + shift_both
    mixer_active = swish(shaped).astype(BF16)
    after_mixer = after_attend + on_chip_sum(dot(mixer_active, mixer_out_both, BF16))

    branch, second_kept = branch_forward(after_mixer, second_gain, second_in, second_out, 2)
    after_second = after_mixer + 0.5 * branch
    output, final_norm = norm_forward(after_second, final_gain)

    own_live = live[:rows]
    picker = (masked_rows[:, None] == jnp.arange(rows)[None, :]).astype(BF16)
    keep = jnp.sum(picker.astype(F32) * own_live[None, :], axis=1)
    chosen = dot(picker, output.astype(BF16), BF16)
    labels = (targets + 1) * (keep > 0).astype(jnp.int32)
    codes = on_chip(labels[None, :])
    codes = jnp.concatenate([cross(codes), codes], axis=0)
    slots = masked_rows.shape[0]
    vocab = head_weight.shape[1]
    head_parts = gather_parts(chosen, 1)
    logits = [dot(part, head_weight) for part in head_parts]
    top = [jnp.max(part, axis=1) for part in logits]
    total = [jnp.sum(jnp.exp(part - peak[:, None]), axis=1) for part, peak in zip(logits, top)]
    pair = jnp.stack([jnp.concatenate(top), jnp.concatenate(total)]).reshape(2, 4, slots)

    def merge(first, second):
        peak = jnp.maximum(first[0], second[0])
        return jnp.stack(
            [peak, first[1] * jnp.exp(first[0] - peak) + second[1] * jnp.exp(second[0] - peak)]
        )

    other = swap(pair)
    pair = merge(pair, jnp.stack([other[:, 1], other[:, 0], other[:, 3], other[:, 2]], axis=1))
    other = cross(pair)
    pair = merge(pair, jnp.concatenate([other[:, 2:], other[:, :2]], axis=1))
    log_totals = (pair[0] + jnp.log(pair[1])).reshape(2, 2 * slots)
    codes = codes.reshape(2, 2 * slots)
    own_loss = jnp.sum((codes[1, :slots] > 0).astype(F32) * log_totals[1, :slots])
    grad_logits, head_results = [], []
    for k in range(2):
        hits = (codes[k] - 1 - own * vocab)[:, None] == jnp.arange(vocab)[None, :]
        counted = (codes[k] > 0).astype(F32)
        own_loss = own_loss - jnp.sum(jnp.where(hits, logits[k], 0.0))
        shares = jnp.exp(logits[k] - log_totals[k][:, None])
        grad = (counted[:, None] * (shares - hits.astype(F32))).astype(BF16)
        grad_logits.append(grad)
        head_results.append(dot_t(grad, head_weight, BF16))
    grad_head = dot_rows(jnp.concatenate(head_parts), jnp.concatenate(grad_logits))
    grad_chosen = scatter_parts(head_results).astype(BF16)
    grad_output = out_cotangent.astype(F32) + weight_term(picker, grad_chosen)
    (grad_head,) = reduce_weights([grad_head])
    grad_second, final_gain_grad = norm_backward(final_norm, final_gain, grad_output)

    back, second_gain_grad, grad_second_in, grad_second_out = branch_backward(
        second_gain, second_in, second_out, second_kept, 0.5 * grad_second, 2
    )
    grad_mixer = grad_second + back
    grad_second_in, grad_second_out = reduce_weights([grad_second_in, grad_second_out])

    grad_full = on_chip(grad_mixer.astype(BF16))
    grad_shaped = dot_t(grad_full, mixer_out_both) * swish_slope(shaped)
    sums = sum_channels(
        jnp.stack([jnp.sum(grad_shaped, axis=0), jnp.sum(grad_shaped * normal, axis=0)])
    )
    batch_shift_grad, batch_scale_grad = sums[0], sums[1]
    grad_conv = (
        scale_both
        * inverse
        * (grad_shaped - live_column / count * (batch_shift_grad + normal * batch_scale_grad))
    )
    depth_grad = jnp.stack(
        [jnp.sum(grad_conv * shifted(glu, j - half, place), axis=0) for j in range(KERNEL)]
    )
    grad_glu = sum(shifted(grad_conv, half - j, place) * depth[j] for j in range(KERNEL))
    grad_glu = grad_glu * live_column
    grad_value = (grad_glu * gate).astype(BF16)
    grad_gate = (grad_glu * value_in * gate * (1.0 - gate)).astype(BF16)
    summed = matmul_t(grad_value, value_both) + matmul_t(grad_gate, gate_both)
    back, mixer_gain_grad = norm_backward(mixer_norm, mixer_gain, on_chip_sum(summed.astype(BF16)))
    grad_attend = grad_mixer + back
    mixer_grads = [
        dot_rows(mixer_in, grad_value),
        dot_rows(mixer_in, grad_gate),
        dot_rows(grad_full, mixer_active),
    ]
    mixer_grads = [
        jnp.concatenate([grad[:, :width] for grad in mixer_grads], axis=1),
        jnp.concatenate([grad[:, width:] for grad in mixer_grads], axis=1),
    ]
    mixer_grads = (mixer_grads[0].astype(F32) + cross(mixer_grads[1]).astype(F32)).astype(BF16)
    depth_grad = sum_channels(depth_grad)

    grad_full = on_chip(grad_attend.astype(BF16))
    grad_mixed = dot_t(grad_full, attend_out_both, BF16)
    grad_qkv = attend_backward_call(qkv, live_column, grad_mixed, log_total)
    summed = dot_t(grad_qkv, qkv_weight, BF16)
    back, attend_gain_grad = norm_backward(attend_norm, attend_gain, on_chip_sum(summed))
    grad_first = grad_attend + back
    qkv_grad = dot_rows(attend_in, grad_qkv)
    out_grad = dot_rows(grad_full, mixed)
    attend_grads = [
        jnp.concatenate([qkv_grad[:, : 3 * width], out_grad[:, :width]], axis=1),
        jnp.concatenate([qkv_grad[:, 3 * width :], out_grad[:, width:]], axis=1),
    ]
    attend_grads = (attend_grads[0].astype(F32) + cross(attend_grads[1]).astype(F32)).astype(BF16)
    (middle,) = reduce_weights([jnp.concatenate([mixer_grads, attend_grads], axis=1)])
    grad_mixer_value, grad_mixer_gate, grad_mixer_out, grad_query, grad_key, grad_value, grad_out = (
        jnp.split(middle, 7, axis=1)
    )

    back, first_gain_grad, grad_first_in, grad_first_out = branch_backward(
        first_gain, first_in, first_out, first_kept, 0.5 * grad_first, 2
    )
    input_grad = grad_first + back
    grad_first_out, grad_first_in = reduce_weights([grad_first_out, grad_first_in])

    counts = jnp.stack([own_loss, jnp.sum(keep)])
    counts = jnp.concatenate([counts, jnp.zeros((D - 2,), F32)])[None]
    gains = jnp.concatenate(
        [attend_gain_grad, mixer_gain_grad, second_gain_grad, final_gain_grad, counts], axis=0
    )
    gains = sum_over_all(gains)
    first_gain_grad = sum_over_all(first_gain_grad)[0]
    loss = gains[4, 0] / gains[4, 1]
    return (
        output,
        loss,
        input_grad,
        first_gain_grad,
        grad_first_in,
        grad_first_out.T,
        gains[0],
        grad_query,
        grad_key,
        grad_value,
        grad_out.T,
        gains[1],
        grad_mixer_value,
        grad_mixer_gate,
        depth_grad[:, :width],
        batch_scale_grad[:width],
        batch_shift_grad[:width],
        grad_mixer_out.T,
        gains[2],
        grad_second_in,
        grad_second_out.T,
        gains[3],
        grad_head,
    )


def solution(mesh):
    in_specs = (
        P(("dp", "mp"), None),
        P(("dp", "mp"), None),
        P("dp"),
        P(("dp", "mp")),
        P(("dp", "mp")),
        P(("dp", "mp"), None),
        P(),
        P(None, "mp"),
        P("mp", None),
        P(),
        P(None, "mp"),
        P(None, "mp"),
        P(None, "mp"),
        P("mp", None),
        P(),
        P(None, "mp"),
        P(None, "mp"),
        P(None, "mp"),
        P("mp"),
        P("mp"),
        P("mp", None),
        P(),
        P(None, "mp"),
        P("mp", None),
        P(),
        P(None, "mp"),
    )
    out_specs = (
        P(("dp", "mp"), None),
        P(),
        P(("dp", "mp"), None),
        P(),
        P("dp", "mp"),
        P("mp", "dp"),
        P(),
        P("dp", "mp"),
        P("dp", "mp"),
        P("dp", "mp"),
        P("mp", "dp"),
        P(),
        P("dp", "mp"),
        P("dp", "mp"),
        P(None, "mp"),
        P("mp"),
        P("mp"),
        P("mp", "dp"),
        P(),
        P("dp", "mp"),
        P("mp", "dp"),
        P(),
        P("dp", "mp"),
    )
    small = mesh.shape["dp"] == 8 and mesh.shape["mp"] == 4
    on_device = on_device_block if small else on_device_any
    return jax.shard_map(
        on_device, mesh=mesh, in_specs=in_specs, out_specs=out_specs, check_vma=False
    )
```

```python
import jax
import jax.numpy as jnp
from jax import lax
from jax.experimental import pallas as pl
from jax.experimental.pallas import tpu as pltpu
from jax.sharding import PartitionSpec as P

D = 1024
HEAD_DIM = 128
KERNEL = 5
LEN = 1024
SEQ_DEV = 2
TOK_DEV = 2048


NORM_EPSILON = 1e-05
MASKED_SCORE = -1000000000.0


def joined(shard, axis, combine):
    everything = jax.tree.map(lambda part: lax.all_gather(part, axis), shard)
    leading = jax.tree.map(lambda part: part[0], everything)

    def hop(k, so_far):
        return combine(so_far, jax.tree.map(lambda part: part[k], everything))

    return lax.fori_loop(1, lax.axis_size(axis), hop, leading)


def layer_norm(values, gain):
    center = values - jnp.mean(values, axis=-1, keepdims=True)
    spread = jnp.mean(center * center, axis=-1, keepdims=True)
    return center * lax.rsqrt(spread + NORM_EPSILON) * gain


def swish(values):
    return values * jax.nn.sigmoid(values)


def swish_slope(values):
    sigma = jax.nn.sigmoid(values)
    return sigma * (1.0 + values * (1.0 - sigma))


def depth_conv(glu, depth):
    length = glu.shape[1]
    half = KERNEL // 2
    padded = jnp.pad(glu, ((0, 0), (half, half), (0, 0)))
    total = padded[:, 0:length] * depth[0]
    for offset in range(1, KERNEL):
        total = total + padded[:, offset : offset + length] * depth[offset]
    return total


def matmul(left, right):
    return jnp.dot(left, right, preferred_element_type=jnp.float32)


def matmul_t(left, right):
    return lax.dot_general(
        left, right, (((1,), (1,)), ((), ())), preferred_element_type=jnp.float32
    )


def weight_term(left, right):
    return lax.dot_general(
        left, right, (((0,), (0,)), ((), ())), preferred_element_type=jnp.float32
    )


def spread_rows(values):
    return lax.all_gather(values, "mp", axis=0, tiled=True)


def collect_rows(values):
    return lax.psum_scatter(values, "mp", scatter_dimension=0, tiled=True)


def spread_grads(values):
    return lax.all_gather(values, "mp", axis=0, tiled=True)


def collect_grads(values):
    return lax.psum_scatter(values, "mp", scatter_dimension=0, tiled=True)


def weight_grad(left, right):
    return weight_term(left, right)


def combine_parts(first, second):
    top = jnp.maximum(first[0], second[0])
    total = first[1] * jnp.exp(first[0] - top) + second[1] * jnp.exp(second[0] - top)
    return (top, total)


def feed_forward(resid, gain, expand, project):
    normed, norm_pullback = jax.vjp(layer_norm, resid, gain)
    gathered = spread_rows(normed.astype(jnp.bfloat16))
    inner = matmul(gathered, expand)
    active = swish(inner).astype(jnp.bfloat16)
    return (collect_rows(matmul(active, project)), (norm_pullback, gathered, inner, active))


def feed_backward(expand, project, kept, grad_branch):
    norm_pullback, gathered, inner, active = kept
    grad_full = spread_grads(grad_branch.astype(jnp.bfloat16))
    grad_inner = (matmul_t(grad_full, project) * swish_slope(inner)).astype(jnp.bfloat16)
    grad_project = weight_grad(grad_full, active)
    grad_expand = weight_grad(gathered, grad_inner)
    grad_resid, grad_gain = norm_pullback(collect_grads(matmul_t(grad_inner, expand)))
    return (grad_resid, grad_gain, grad_expand, grad_project)


def attend_forward(resid, gain, query_weight, key_weight, value_weight, attend_out, live):
    normed, norm_pullback = jax.vjp(layer_norm, resid, gain)
    gathered = spread_rows(normed.astype(jnp.bfloat16))
    width = query_weight.shape[1]
    shape = (SEQ_DEV, LEN, width // HEAD_DIM, HEAD_DIM)
    query = matmul(gathered, query_weight).astype(jnp.bfloat16).reshape(shape)
    keys = matmul(gathered, key_weight).astype(jnp.bfloat16).reshape(shape)
    values = matmul(gathered, value_weight).astype(jnp.bfloat16).reshape(shape)
    scale = HEAD_DIM ** (-0.5)

    def one_utterance(pack):
        query_part, keys_part, values_part, alive = pack
        scores = (
            jnp.einsum("qhe,khe->hqk", query_part, keys_part, preferred_element_type=jnp.float32)
            * scale
        )
        scores = jnp.where(alive[None, None, :] > 0, scores, MASKED_SCORE)
        top = jnp.max(scores, axis=-1, keepdims=True)
        lifted = jnp.exp(scores - top)
        total = jnp.sum(lifted, axis=-1, keepdims=True)
        shares = (lifted / total).astype(jnp.bfloat16)
        mixed_part = jnp.einsum(
            "hqk,khe->qhe", shares, values_part, preferred_element_type=jnp.float32
        )
        return (mixed_part.astype(jnp.bfloat16), (top + jnp.log(total))[:, :, 0])

    mixed, log_total = lax.map(one_utterance, (query, keys, values, live))
    mixed = mixed.reshape(TOK_DEV, width)
    branch = collect_rows(matmul(mixed, attend_out))
    return (branch, (norm_pullback, gathered, query, keys, values, mixed, log_total))


def attend_backward(query_weight, key_weight, value_weight, attend_out, live, kept, grad_branch):
    norm_pullback, gathered, query, keys, values, mixed, log_total = kept
    width = query_weight.shape[1]
    grad_full = spread_grads(grad_branch.astype(jnp.bfloat16))
    grad_mixed = matmul_t(grad_full, attend_out).astype(jnp.bfloat16).reshape(query.shape)
    grad_attend_out = weight_grad(grad_full, mixed)
    scale = HEAD_DIM ** (-0.5)

    def one_utterance(pack):
        query_part, keys_part, values_part, alive, log_part, grad_part = pack
        scores = (
            jnp.einsum("qhe,khe->hqk", query_part, keys_part, preferred_element_type=jnp.float32)
            * scale
        )
        scores = jnp.where(alive[None, None, :] > 0, scores, MASKED_SCORE)
        shares = jnp.exp(scores - log_part[:, :, None])
        grad_values = jnp.einsum(
            "hqk,qhe->khe",
            shares.astype(jnp.bfloat16),
            grad_part,
            preferred_element_type=jnp.float32,
        )
        grad_shares = jnp.einsum(
            "qhe,khe->hqk", grad_part, values_part, preferred_element_type=jnp.float32
        )
        inner = jnp.sum(shares * grad_shares, axis=-1, keepdims=True)
        grad_scores = (shares * (grad_shares - inner)).astype(jnp.bfloat16)
        grad_query = (
            jnp.einsum("hqk,khe->qhe", grad_scores, keys_part, preferred_element_type=jnp.float32)
            * scale
        )
        grad_keys = (
            jnp.einsum("hqk,qhe->khe", grad_scores, query_part, preferred_element_type=jnp.float32)
            * scale
        )
        return (
            grad_query.astype(jnp.bfloat16),
            grad_keys.astype(jnp.bfloat16),
            grad_values.astype(jnp.bfloat16),
        )

    grad_query, grad_keys, grad_values = lax.map(
        one_utterance, (query, keys, values, live, log_total, grad_mixed)
    )
    grad_query = grad_query.reshape(TOK_DEV, width)
    grad_keys = grad_keys.reshape(TOK_DEV, width)
    grad_values = grad_values.reshape(TOK_DEV, width)
    grad_query_weight = weight_grad(gathered, grad_query)
    grad_key_weight = weight_grad(gathered, grad_keys)
    grad_value_weight = weight_grad(gathered, grad_values)
    summed = (
        matmul_t(grad_query, query_weight)
        + matmul_t(grad_keys, key_weight)
        + matmul_t(grad_values, value_weight)
    )
    grad_resid, grad_gain = norm_pullback(collect_grads(summed))
    return (
        grad_resid,
        grad_gain,
        grad_query_weight,
        grad_key_weight,
        grad_value_weight,
        grad_attend_out,
    )


def mixer_forward(
    resid,
    gain,
    mixer_value,
    mixer_gate,
    mixer_depth,
    batch_scale,
    batch_shift,
    mixer_out,
    live_flat,
):
    normed, norm_pullback = jax.vjp(layer_norm, resid, gain)
    gathered = spread_rows(normed.astype(jnp.bfloat16))
    value_in = matmul(gathered, mixer_value)
    gate_in = matmul(gathered, mixer_gate)
    channels = value_in.shape[1]

    def front(value_part, gate_part, depth):
        glu = value_part * jax.nn.sigmoid(gate_part) * live_flat[:, None]
        return depth_conv(glu.reshape(SEQ_DEV, LEN, channels), depth).reshape(TOK_DEV, channels)

    convolved, front_pullback = jax.vjp(front, value_in, gate_in, mixer_depth)
    weighted = convolved * live_flat[:, None]
    count, first_sum, second_sum = lax.psum(
        (jnp.sum(live_flat), jnp.sum(weighted, axis=0), jnp.sum(weighted * convolved, axis=0)), "dp"
    )
    bn_mean = first_sum / count
    inverse = lax.rsqrt(second_sum / count - bn_mean * bn_mean + NORM_EPSILON)
    normal = (convolved - bn_mean) * inverse
    shaped = normal * batch_scale + batch_shift
    active = swish(shaped).astype(jnp.bfloat16)
    branch = collect_rows(matmul(active, mixer_out))
    return (
        branch,
        (norm_pullback, gathered, front_pullback, normal, inverse, count, shaped, active),
    )


def mixer_backward(mixer_value, mixer_gate, batch_scale, mixer_out, live_flat, kept, grad_branch):
    norm_pullback, gathered, front_pullback, normal, inverse, count, shaped, active = kept
    grad_full = spread_grads(grad_branch.astype(jnp.bfloat16))
    grad_mixer_out = weight_grad(grad_full, active)
    grad_shaped = matmul_t(grad_full, mixer_out) * swish_slope(shaped)
    shift_grad, scale_grad = lax.psum(
        (jnp.sum(grad_shaped, axis=0), jnp.sum(grad_shaped * normal, axis=0)), "dp"
    )
    grad_conv = (
        batch_scale
        * inverse
        * (grad_shaped - live_flat[:, None] / count * (shift_grad + normal * scale_grad))
    )
    grad_value, grad_gate, depth_grad = front_pullback(grad_conv)
    grad_value = grad_value.astype(jnp.bfloat16)
    grad_gate = grad_gate.astype(jnp.bfloat16)
    grad_mixer_value = weight_grad(gathered, grad_value)
    grad_mixer_gate = weight_grad(gathered, grad_gate)
    summed = matmul_t(grad_value, mixer_value) + matmul_t(grad_gate, mixer_gate)
    grad_resid, grad_gain = norm_pullback(collect_grads(summed))
    return (
        grad_resid,
        grad_gain,
        grad_mixer_value,
        grad_mixer_gate,
        depth_grad,
        scale_grad,
        shift_grad,
        grad_mixer_out,
    )


def masked_head(output, own_live, masked_rows, targets, head_device, head_weight):
    rows = output.shape[0]
    sources = lax.axis_size("dp")
    capacity = rows // sources
    keep = own_live[masked_rows]
    chosen = output[masked_rows].astype(jnp.bfloat16)
    destination = head_device[:, 0]
    marks = (destination[:, None] == jnp.arange(sources)[None, :]).astype(jnp.int32)
    order = jnp.sum((jnp.cumsum(marks, axis=0) - marks) * marks, axis=1)
    placer = (destination * capacity + order)[:, None] == jnp.arange(rows)[None, :]
    packed = weight_term(placer.astype(jnp.bfloat16), chosen).astype(jnp.bfloat16)
    labels = (targets + 1) * (keep > 0).astype(jnp.int32)
    codes = jnp.sum(jnp.where(placer, labels[:, None], 0), axis=0)
    arrived, arrived_codes = (
        lax.all_to_all(packed, "dp", split_axis=0, concat_axis=0, tiled=True),
        lax.all_to_all(codes, "dp", split_axis=0, concat_axis=0, tiled=True),
    )
    shared, shared_codes = (
        lax.all_gather(arrived, "mp", axis=0, tiled=True),
        lax.all_gather(arrived_codes, "mp", axis=0, tiled=True),
    )
    logits = matmul(shared, head_weight)
    vocab = head_weight.shape[1]
    hits = (shared_codes - 1 - lax.axis_index("mp") * vocab)[:, None] == jnp.arange(vocab)[None, :]
    top = jnp.max(logits, axis=1)
    total = jnp.sum(jnp.exp(logits - top[:, None]), axis=1)
    picked = jnp.sum(jnp.where(hits, logits, 0.0), axis=1)
    top_all, total_all = joined((top, total), "mp", combine_parts)
    log_total = top_all + jnp.log(total_all)
    counted = (shared_codes > 0).astype(jnp.float32)
    own_total = jnp.sum(
        lax.dynamic_slice_in_dim(counted * log_total, lax.axis_index("mp") * rows, rows)
    )
    own_loss = own_total - jnp.sum(counted * picked)
    grad_logits = (
        counted[:, None] * (jnp.exp(logits - log_total[:, None]) - hits.astype(jnp.float32))
    ).astype(jnp.bfloat16)
    grad_head = weight_grad(shared, grad_logits)
    grad_shared = lax.psum_scatter(
        matmul_t(grad_logits, head_weight), "mp", scatter_dimension=0, tiled=True
    )
    returned = lax.all_to_all(
        grad_shared.astype(jnp.bfloat16), "dp", split_axis=0, concat_axis=0, tiled=True
    )
    grad_chosen = matmul(placer.astype(jnp.bfloat16), returned).astype(jnp.bfloat16)
    picker = (masked_rows[:, None] == jnp.arange(rows)[None, :]).astype(jnp.bfloat16)
    grad_rows = weight_term(picker, grad_chosen)
    return (grad_rows, grad_head, own_loss, jnp.sum(keep))


def on_device_any(
    frames,
    out_cotangent,
    lengths,
    masked_rows,
    targets,
    head_device,
    first_gain,
    first_in,
    first_out,
    attend_gain,
    query_weight,
    key_weight,
    value_weight,
    attend_out,
    mixer_gain,
    mixer_value,
    mixer_gate,
    mixer_depth,
    batch_scale,
    batch_shift,
    mixer_out,
    second_gain,
    second_in,
    second_out,
    final_gain,
    head_weight,
):
    rows = frames.shape[0]
    live = (jnp.arange(LEN)[None, :] < lengths[:, None]).astype(jnp.float32)
    live_flat = live.reshape(TOK_DEV)
    own_live = lax.dynamic_slice_in_dim(live_flat, lax.axis_index("mp") * rows, rows)
    start = frames.astype(jnp.float32)
    branch, first_kept = feed_forward(start, first_gain, first_in, first_out)
    after_first = start + 0.5 * branch
    branch, attend_kept = attend_forward(
        after_first, attend_gain, query_weight, key_weight, value_weight, attend_out, live
    )
    after_attend = after_first + branch
    branch, mixer_kept = mixer_forward(
        after_attend,
        mixer_gain,
        mixer_value,
        mixer_gate,
        mixer_depth,
        batch_scale,
        batch_shift,
        mixer_out,
        live_flat,
    )
    after_mixer = after_attend + branch
    branch, second_kept = feed_forward(after_mixer, second_gain, second_in, second_out)
    after_second = after_mixer + 0.5 * branch
    output, final_pullback = jax.vjp(layer_norm, after_second, final_gain)
    grad_rows, grad_head, own_loss, own_count = masked_head(
        output, own_live, masked_rows, targets, head_device, head_weight
    )
    grad_second, final_gain_grad = final_pullback(out_cotangent.astype(jnp.float32) + grad_rows)
    back_resid, second_gain_grad, grad_second_in, grad_second_out = feed_backward(
        second_in, second_out, second_kept, 0.5 * grad_second
    )
    grad_mixer = grad_second + back_resid
    (
        back_resid,
        mixer_gain_grad,
        grad_mixer_value,
        grad_mixer_gate,
        depth_grad,
        batch_scale_grad,
        batch_shift_grad,
        grad_mixer_out,
    ) = mixer_backward(
        mixer_value, mixer_gate, batch_scale, mixer_out, live_flat, mixer_kept, grad_mixer
    )
    grad_attend = grad_mixer + back_resid
    back_resid, attend_gain_grad, grad_query, grad_key, grad_value, grad_attend_out = (
        attend_backward(
            query_weight, key_weight, value_weight, attend_out, live, attend_kept, grad_attend
        )
    )
    grad_first = grad_attend + back_resid
    back_resid, first_gain_grad, grad_first_in, grad_first_out = feed_backward(
        first_in, first_out, first_kept, 0.5 * grad_first
    )
    input_grad = grad_first + back_resid
    channels = mixer_value.shape[1]
    offset = lax.axis_index("mp") * channels
    depth_full = lax.dynamic_update_slice_in_dim(
        jnp.zeros((KERNEL, D), jnp.float32), depth_grad, offset, 1
    )
    (
        first_gain_grad,
        attend_gain_grad,
        mixer_gain_grad,
        second_gain_grad,
        final_gain_grad,
        depth_full,
        loss_sum,
        loss_count,
    ) = lax.psum(
        (
            first_gain_grad,
            attend_gain_grad,
            mixer_gain_grad,
            second_gain_grad,
            final_gain_grad,
            depth_full,
            own_loss,
            own_count,
        ),
        ("dp", "mp"),
    )
    mixer_depth_grad = lax.dynamic_slice_in_dim(depth_full, offset, channels, 1)
    loss = loss_sum / loss_count
    (
        grad_first_in,
        grad_first_out,
        grad_query,
        grad_key,
        grad_value,
        grad_attend_out,
        grad_mixer_value,
        grad_mixer_gate,
        grad_mixer_out,
        grad_second_in,
        grad_second_out,
        grad_head,
    ) = (
        lax.psum_scatter(grad_first_in, "dp", scatter_dimension=0, tiled=True),
        lax.psum_scatter(grad_first_out, "dp", scatter_dimension=0, tiled=True),
        lax.psum_scatter(grad_query, "dp", scatter_dimension=0, tiled=True),
        lax.psum_scatter(grad_key, "dp", scatter_dimension=0, tiled=True),
        lax.psum_scatter(grad_value, "dp", scatter_dimension=0, tiled=True),
        lax.psum_scatter(grad_attend_out, "dp", scatter_dimension=0, tiled=True),
        lax.psum_scatter(grad_mixer_value, "dp", scatter_dimension=0, tiled=True),
        lax.psum_scatter(grad_mixer_gate, "dp", scatter_dimension=0, tiled=True),
        lax.psum_scatter(grad_mixer_out, "dp", scatter_dimension=0, tiled=True),
        lax.psum_scatter(grad_second_in, "dp", scatter_dimension=0, tiled=True),
        lax.psum_scatter(grad_second_out, "dp", scatter_dimension=0, tiled=True),
        lax.psum_scatter(grad_head, "dp", scatter_dimension=0, tiled=True),
    )
    return (
        output,
        loss,
        input_grad,
        first_gain_grad,
        grad_first_in,
        grad_first_out.T,
        attend_gain_grad,
        grad_query,
        grad_key,
        grad_value,
        grad_attend_out.T,
        mixer_gain_grad,
        grad_mixer_value,
        grad_mixer_gate,
        mixer_depth_grad,
        batch_scale_grad,
        batch_shift_grad,
        grad_mixer_out.T,
        second_gain_grad,
        grad_second_in,
        grad_second_out.T,
        final_gain_grad,
        grad_head,
    )


BF16 = jnp.bfloat16
F32 = jnp.float32
SCALE = HEAD_DIM ** (-0.5)
CORE_PAIRS = [(0, 1), (1, 0), (2, 3), (3, 2)]
CHIP_PAIRS = [(0, 2), (2, 0), (1, 3), (3, 1)]
X_PAIRS = [(0, 1), (1, 0), (2, 3), (3, 2), (4, 5), (5, 4), (6, 7), (7, 6)]
Z_NEAR_PAIRS = [(0, 2), (2, 0), (1, 3), (3, 1), (4, 6), (6, 4), (5, 7), (7, 5)]
Z_FAR_PAIRS = [(0, 4), (4, 0), (1, 5), (5, 1), (2, 6), (6, 2), (3, 7), (7, 3)]


def swap(values):
    return lax.ppermute(values, "mp", CORE_PAIRS)


def cross(values):
    return lax.ppermute(values, "mp", CHIP_PAIRS)


def sum_over_dp(values):
    for pairs in (X_PAIRS, Z_NEAR_PAIRS, Z_FAR_PAIRS):
        values = values + lax.ppermute(values, "dp", pairs)
    return values


def sum_over_all(values):
    values = values + swap(values)
    values = values + cross(values)
    return sum_over_dp(values)


def sum_channels(values):
    other = cross(values)
    half = values.shape[-1] // 2
    turned = jnp.concatenate([other[..., half:], other[..., :half]], axis=-1)
    return sum_over_dp(values + turned)


def norm_forward(values, gain):
    center = values - jnp.mean(values, axis=-1, keepdims=True)
    spread = jnp.mean(center * center, axis=-1, keepdims=True)
    inverse = lax.rsqrt(spread + NORM_EPSILON)
    unit = center * inverse
    return (unit * gain, (unit, inverse))


def norm_backward(kept, gain, grad):
    unit, inverse = kept
    grad_gain = jnp.sum(grad * unit, axis=0, keepdims=True)
    scaled = grad * gain
    inner = jnp.mean(scaled * unit, axis=-1, keepdims=True)
    return (inverse * (scaled - jnp.mean(scaled, axis=-1, keepdims=True) - unit * inner), grad_gain)


def on_chip(values):
    return jnp.concatenate([values, swap(values)], axis=0)


def on_chip_sum(values):
    half = values.shape[0] // 2
    return values[:half].astype(F32) + swap(values[half:]).astype(F32)


def gather_parts(values, number):
    step = values.shape[0] // number
    far = [cross(values[k * step : (k + 1) * step]) for k in range(number)]
    near = on_chip(values)
    return [on_chip(part) for part in far] + [near]


def scatter_parts(parts):
    far = [cross(on_chip_sum(part).astype(BF16)) for part in parts[:-1]]
    far = far[0] if len(far) == 1 else jnp.concatenate(far, axis=0)
    return on_chip_sum(parts[-1]) + far.astype(F32)


def dot(left, right, kind=F32):
    return jnp.dot(left, right, preferred_element_type=F32).astype(kind)


def dot_t(left, right, kind=F32):
    return matmul_t(left, right).astype(kind)


def dot_rows(lefts, rights):
    total = weight_term(lefts, rights)
    return total.astype(BF16)


def after(values, *earlier):
    return lax.optimization_barrier((values, *earlier))[0]


def early(flops, size):
    return pl.CostEstimate(flops=flops // 1000, bytes_accessed=size // 1000, transcendentals=0)


BLOCK = 256


def pieces_call(body, pieces, row_inputs, weights, row_outputs, held, start, total, name):
    rows, width = pieces[0].shape
    block = min(BLOCK, rows)
    half, first = rows // block, start // block
    steps = 2 * half

    def kernel(*refs):
        refs = list(refs)
        inputs, refs = refs[: 2 + len(row_inputs) + len(weights)], refs[2 + len(row_inputs) + len(weights) :]
        if held is not None:
            refs = refs[len(held) :]
        step = pl.program_id(0)
        piece = jnp.where(step < half, inputs[0][...], inputs[1][...])
        result = body(piece, inputs[2:], refs[: len(row_outputs)])

        @pl.when(step < half)
        def _():
            refs[-2][...] = result

        @pl.when(step >= half)
        def _():
            refs[-1][...] = result

    def kept(array):
        return pl.BlockSpec(array.shape, lambda i: (0,) * array.ndim)

    def placed(size):
        return pl.BlockSpec((block, size), lambda i: (i + first, 0))

    two = [
        pl.BlockSpec((block, width), lambda i: (jnp.minimum(i, half - 1), 0)),
        pl.BlockSpec((block, width), lambda i: (jnp.maximum(i - half, 0), 0)),
    ]
    row_inputs = [pltpu.with_memory_space_constraint(array, pltpu.HBM) for array in row_inputs]
    operands = [*pieces, *row_inputs, *weights]
    in_specs = two + [placed(array.shape[1]) for array in row_inputs] + [kept(w) for w in weights]
    aliases = {}
    if held is not None:
        aliases = {len(operands) + k: k for k in range(len(held))}
        operands += held
        in_specs += [pl.BlockSpec(memory_space=pl.ANY)] * len(held)
    flops = 2 * 2 * rows * sum(w.size for w in weights if w.ndim == 2 and w.shape[0] > 1)
    return pl.pallas_call(
        kernel,
        grid=(steps,),
        in_specs=in_specs,
        out_specs=[placed(size) for size in row_outputs] + two,
        out_shape=[pltpu.HBM((total, size), BF16) for size in row_outputs]
        + [jax.ShapeDtypeStruct((rows, width), BF16)] * 2,
        input_output_aliases=aliases,
        compiler_params=pltpu.CompilerParams(vmem_limit_bytes=32 << 20),
        cost_estimate=early(flops, 2 * sum(w.size for w in weights)),
        name=name,
    )(*operands)


def expand_body(piece, inputs, outputs):
    expand_ref, project_ref = inputs
    held_ref, inner_ref, active_ref = outputs
    inner = matmul(piece, expand_ref[...])
    active = swish(inner).astype(BF16)
    held_ref[...] = piece
    inner_ref[...] = inner.astype(BF16)
    active_ref[...] = active
    return matmul(active, project_ref[...]).astype(BF16)


def expand_back_body(piece, inputs, outputs):
    inner_ref, expand_ref, project_ref = inputs
    held_ref, grad_ref = outputs
    slope = swish_slope(inner_ref[...].astype(F32))
    grad = (matmul_t(piece, project_ref[...]) * slope).astype(BF16)
    held_ref[...] = piece
    grad_ref[...] = grad
    return matmul_t(grad, expand_ref[...]).astype(BF16)


def swap_halves(values):
    half = values.shape[0] // 2
    return jnp.concatenate([swap(values[:half]), swap(values[half:])], axis=0)


def branch_over(values, number, call, beside=None):
    rows = values.shape[0]
    step = rows // number
    far = [cross(values[k * step : (k + 1) * step]) for k in range(number)]
    held, (own, other) = call((values, swap(values)), None, 0)
    near = own.astype(F32) + swap(other).astype(F32)
    done, back = own, []
    for k in range(number):
        part = after(far[k], done) if beside is None else after(far[k], done, *beside[k]())
        held, (own, other) = call((part, swap_halves(part)), held, 2 * rows + 2 * step * k)
        result = (own.astype(F32) + swap_halves(other).astype(F32)).astype(BF16)
        result = after(result, *back)
        back.append(cross(result))
        done = own
    return (near + jnp.concatenate(back, axis=0).astype(F32), held, result)


def branch_forward(resid, gain, expand, project, number, beside=None):
    normed, norm_kept = norm_forward(resid, gain)
    total = 4 * resid.shape[0]
    sizes = [resid.shape[1], expand.shape[1], expand.shape[1]]

    def call(pieces, held, start):
        *held, own, other = pieces_call(
            expand_body, pieces, [], [expand, project], sizes, held, start, total, "branch_forward"
        )
        return (held, (own, other))

    result, held, _ = branch_over(normed.astype(BF16), number, call, beside)
    return (result, (norm_kept, *held))


def branch_backward(gain, expand, project, kept, grad_branch, number, beside=None):
    norm_kept, normed, inner, active = kept
    total = 4 * grad_branch.shape[0]
    sizes = [grad_branch.shape[1], expand.shape[1]]

    def call(pieces, held, start):
        *held, own, other = pieces_call(
            expand_back_body, pieces, [inner], [expand, project], sizes, held, start, total,
            "branch_backward",
        )
        return (held, (own, other))

    result, (grads, grad_inner), sent = branch_over(grad_branch.astype(BF16), number, call, beside)

    held = (grads, active, normed, grad_inner, sent)
    grad_resid, grad_gain = norm_backward(norm_kept, gain, result)
    return (grad_resid, grad_gain, held, result)


def attend_kernel(live_ref, query_ref, keys_ref, values_ref, mixed_ref, total_ref):
    scores = matmul_t(keys_ref[...], query_ref[...]) * SCALE
    scores = jnp.where(live_ref[...] > 0, scores, MASKED_SCORE)
    top = jnp.max(scores, axis=0, keepdims=True)
    lifted = jnp.exp(scores - top)
    total = jnp.sum(lifted, axis=0, keepdims=True)
    mixed = weight_term(values_ref[...], lifted.astype(BF16)) * (1.0 / total)
    mixed_ref[...] = mixed.T.astype(BF16)
    total_ref[0] = top + jnp.log(total)


def head_column(head, kind):
    return (head // 2) * 6 + kind * 2 + head % 2


def attend_forward_call(qkv, live_column):
    length = qkv.shape[0]
    heads = qkv.shape[1] // (3 * HEAD_DIM)
    block = length

    def whole(kind):
        return pl.BlockSpec((length, HEAD_DIM), lambda h, b: (0, head_column(h, kind)))

    return pl.pallas_call(
        attend_kernel,
        grid=(heads, length // block),
        in_specs=[
            pl.BlockSpec((length, 1), lambda h, b: (0, 0)),
            pl.BlockSpec((block, HEAD_DIM), lambda h, b: (b, head_column(h, 0))),
            whole(1),
            whole(2),
        ],
        out_specs=[
            pl.BlockSpec((block, HEAD_DIM), lambda h, b: (b, h)),
            pl.BlockSpec((1, 1, block), lambda h, b: (h, 0, b)),
        ],
        out_shape=[
            jax.ShapeDtypeStruct((length, heads * HEAD_DIM), BF16),
            jax.ShapeDtypeStruct((heads, 1, length), F32),
        ],
        compiler_params=pltpu.CompilerParams(vmem_limit_bytes=32 << 20),
        cost_estimate=early(4 * heads * length * length * HEAD_DIM, 8 * qkv.size),
        name="attend_forward",
    )(live_column, qkv, qkv, qkv)


def attend_back_kernel(
    live_ref, query_ref, keys_ref, values_ref, grad_ref, total_ref, out_ref, keys_sum, values_sum
):
    head, block = pl.program_id(0), pl.program_id(1)
    rows = query_ref.shape[0]
    query, keys, grad = query_ref[...], keys_ref[...], grad_ref[...]
    scores = matmul_t(keys, query) * SCALE
    scores = jnp.where(live_ref[...] > 0, scores, MASKED_SCORE)
    shares = jnp.exp(scores - total_ref[0])
    grad_shares = matmul_t(values_ref[...], grad)
    inner = jnp.sum(shares * grad_shares, axis=0, keepdims=True)
    grad_scores = (shares * (grad_shares - inner)).astype(BF16)
    grad_values = dot(shares.astype(BF16), grad)
    grad_keys = dot(grad_scores, query) * SCALE
    grad_query = (weight_term(keys, grad_scores) * SCALE).T.astype(BF16)

    def columns(kind):
        start = head_column(head, kind) * HEAD_DIM
        return pl.ds(pl.multiple_of(start, HEAD_DIM), HEAD_DIM)

    out_ref[pl.ds(pl.multiple_of(block * rows, rows), rows), columns(0)] = grad_query

    @pl.when(block == 0)
    def _():
        keys_sum[...] = grad_keys
        values_sum[...] = grad_values

    @pl.when(block > 0)
    def _():
        keys_sum[...] += grad_keys
        values_sum[...] += grad_values

    @pl.when(block == pl.num_programs(1) - 1)
    def _():
        out_ref[:, columns(1)] = keys_sum[...].astype(BF16)
        out_ref[:, columns(2)] = values_sum[...].astype(BF16)


def attend_backward_call(qkv, live_column, grad_mixed, log_total):
    length = qkv.shape[0]
    heads = qkv.shape[1] // (3 * HEAD_DIM)
    block = length // 2

    def whole(kind):
        return pl.BlockSpec((length, HEAD_DIM), lambda h, b: (0, head_column(h, kind)))

    return pl.pallas_call(
        attend_back_kernel,
        grid=(heads, length // block),
        in_specs=[
            pl.BlockSpec((length, 1), lambda h, b: (0, 0)),
            pl.BlockSpec((block, HEAD_DIM), lambda h, b: (b, head_column(h, 0))),
            whole(1),
            whole(2),
            pl.BlockSpec((block, HEAD_DIM), lambda h, b: (b, h)),
            pl.BlockSpec((1, 1, block), lambda h, b: (h, 0, b)),
        ],
        out_specs=pl.BlockSpec(qkv.shape, lambda h, b: (0, 0)),
        out_shape=jax.ShapeDtypeStruct(qkv.shape, BF16),
        scratch_shapes=[pltpu.VMEM((length, HEAD_DIM), F32), pltpu.VMEM((length, HEAD_DIM), F32)],
        compiler_params=pltpu.CompilerParams(vmem_limit_bytes=40 << 20),
        cost_estimate=early(10 * heads * length * length * HEAD_DIM, 8 * qkv.size),
        name="attend_backward",
    )(live_column, qkv, qkv, qkv, grad_mixed, log_total)


def shifted(values, offset, position):
    if offset == 0:
        return values
    moved = jnp.roll(values, -offset, axis=0)
    place = position + offset
    return jnp.where((place >= 0) & (place < LEN), moved, 0.0)


def weights_kernel(number, *refs):
    out_ref = refs[-1]
    start = 0
    for k in range(number):
        left_ref, right_ref = refs[2 * k], refs[2 * k + 1]
        size = right_ref.shape[1]
        out_ref[:, start : start + size] = weight_term(left_ref[...], right_ref[...]).astype(BF16)
        start += size


def weights_turn_kernel(number, *refs):
    out_ref = refs[-1]
    for k in range(number):

        @pl.when(pl.program_id(0) == k)
        def _(left_ref=refs[2 * k], right_ref=refs[2 * k + 1]):
            out_ref[...] = weight_term(left_ref[...], right_ref[...]).astype(BF16)


def weights_call(lefts, rights, name):
    rows, width = lefts[0].shape
    number = len(lefts)
    total = sum(right.shape[1] for right in rights)
    block = 512
    steps = width // block
    turns = len({right.shape[1] for right in rights}) == 1
    operands, in_specs = [], []
    for k in range(number):
        left_rows, size = rights[k].shape
        if turns:
            place = lambda i, j, k=k: (0, jnp.clip((i - k) * steps + j, 0, steps - 1))
            held = lambda i, j: (0, 0)
        else:
            place = lambda j: (0, j)
            held = lambda j: (0, 0)
        in_specs.append(pl.BlockSpec((left_rows, block), place))
        in_specs.append(pl.BlockSpec((left_rows, size), held))
        operands += [lefts[k], rights[k]]
    if turns:
        grid, kernel = (number, steps), weights_turn_kernel
        out_spec = pl.BlockSpec((block, rights[0].shape[1]), lambda i, j: (j, i))
    else:
        grid, kernel = (steps,), weights_kernel
        out_spec = pl.BlockSpec((block, total), lambda j: (j, 0))
    return pl.pallas_call(
        lambda *refs: kernel(number, *refs),
        grid=grid,
        in_specs=in_specs,
        out_specs=out_spec,
        out_shape=jax.ShapeDtypeStruct((width, total), BF16),
        compiler_params=pltpu.CompilerParams(vmem_limit_bytes=48 << 20),
        cost_estimate=early(2 * rows * width * total, 2 * width * total),
        name=name,
    )(*operands)


def fetch_other(packed):
    place = lax.axis_index("dp")
    x, z = place % 2, (place // 2) % 2
    rows = packed.shape[0] // 4

    def over_x(values):
        return lax.ppermute(values, "dp", X_PAIRS)

    def over_z(values):
        return lax.ppermute(values, "dp", Z_NEAR_PAIRS)

    def first():
        return cross(lax.dynamic_slice_in_dim(packed, (2 * z + x) * rows, rows))

    def second(piece):
        return (over_x(piece), over_z(piece))

    def third(beside, above):
        return (over_z(beside[: rows // 2]), over_x(above[rows // 2 :]))

    def whole(piece, beside, above, corner):
        corner = jnp.concatenate(corner, axis=0)
        pieces = ((x, z, piece), (1 - x, z, beside), (x, 1 - z, above), (1 - x, 1 - z, corner))
        result = jnp.zeros_like(packed)
        for at_x, at_z, part in pieces:
            result = lax.dynamic_update_slice_in_dim(result, part, (2 * at_z + at_x) * rows, 0)
        return result

    return (first, second, third, whole)


def reduce_weights(grad):
    return lax.psum_scatter(grad, "dp", scatter_dimension=0, tiled=True)


def sum_steps(values):
    for axis, pairs in (
        ("mp", CORE_PAIRS),
        ("mp", CHIP_PAIRS),
        ("dp", X_PAIRS),
        ("dp", Z_NEAR_PAIRS),
        ("dp", Z_FAR_PAIRS),
    ):
        arrived = lax.ppermute(values, axis, pairs)
        earlier = yield arrived
        values = values + after(arrived, *earlier)
    yield values


def reduce_by_steps(grad):
    place = lax.axis_index("dp")
    size = grad.shape[0] // 8
    x, near, far = place % 2, (place // 2) % 2, place // 4
    steps = (
        ((4, 2, size, -1), 1, x, X_PAIRS),
        ((2, 2, size, -1), 1, near, Z_NEAR_PAIRS),
        ((2, size, -1), 0, far, Z_FAR_PAIRS),
    )
    for shape, axis, at, pairs in steps:
        parts = grad.reshape(shape)
        keep = lax.dynamic_index_in_dim(parts, at, axis, keepdims=False)
        send = lax.dynamic_index_in_dim(parts, 1 - at, axis, keepdims=False)
        arrived = lax.ppermute(send, "dp", pairs)
        earlier = yield arrived
        total = keep.astype(F32) + after(arrived, *earlier).astype(F32)
        grad = total.astype(BF16)
    yield total


def on_device_block(
    frames,
    out_cotangent,
    lengths,
    masked_rows,
    targets,
    head_device,
    first_gain,
    first_in,
    first_out,
    attend_gain,
    query_weight,
    key_weight,
    value_weight,
    attend_out,
    mixer_gain,
    mixer_value,
    mixer_gate,
    mixer_depth,
    batch_scale,
    batch_shift,
    mixer_out,
    second_gain,
    second_in,
    second_out,
    final_gain,
    head_weight,
):
    rows = frames.shape[0]
    own = lax.axis_index("mp")
    core, chip = own % 2, own // 2
    length = lax.dynamic_index_in_dim(lengths, chip, 0, keepdims=False)
    position = (jnp.arange(LEN) + core * rows) % LEN
    live = (position < length).astype(F32)
    live_column = live[:, None]
    place = position[:, None]

    attend_pack = jnp.concatenate(
        [query_weight, key_weight, value_weight, attend_out.reshape(D, -1)], axis=1
    )
    mixer_pack = jnp.concatenate([mixer_value, mixer_gate], axis=1)
    width = query_weight.shape[1]
    channels = jnp.concatenate([mixer_depth, batch_scale[None], batch_shift[None]], axis=0)
    own_live = live[:rows]
    picker = (masked_rows[:, None] == jnp.arange(rows)[None, :]).astype(BF16)
    keep = jnp.sum(picker.astype(F32) * own_live[None, :], axis=1)
    labels = (targets + 1) * (keep > 0).astype(jnp.int32)
    codes = on_chip(labels[None, :])

    first, second, third, whole = fetch_other(attend_pack)
    fetched = []

    def fetch_first():
        fetched.append(first())
        return fetched

    start = frames.astype(F32)
    branch, first_kept = branch_forward(
        start, first_gain, first_in, first_out, 2, (lambda: [], fetch_first)
    )
    piece = fetched[0]
    beside, above = second(piece)
    channels_other, codes_other = cross(channels), cross(codes)
    branch = after(branch, beside, above, channels_other, codes_other)
    attend_other = whole(piece, beside, above, third(beside, above))
    after_first = start + 0.5 * branch

    qkv_weight = jnp.concatenate([attend_pack[:, : 3 * width], attend_other[:, : 3 * width]], axis=1)
    attend_out_both = jnp.concatenate(
        [attend_out, attend_other[:, 3 * width :].reshape(width, D)], axis=0
    )
    normed, attend_norm = norm_forward(after_first, attend_gain)
    mixer_other, mixer_out_other = cross(mixer_pack), cross(mixer_out)
    attend_in = on_chip(normed.astype(BF16))
    qkv = dot(attend_in, qkv_weight, BF16)
    mixed, log_total = attend_forward_call(after(qkv, mixer_other), live_column)
    mixed = after(mixed, mixer_out_other)
    after_attend = after_first + on_chip_sum(dot(mixed, attend_out_both, BF16))

    mixer_both = jnp.concatenate([mixer_pack, mixer_other], axis=1)
    mixer_out_both = jnp.concatenate([mixer_out, mixer_out_other], axis=0)
    channels = jnp.concatenate([channels, channels_other], axis=1)
    depth, scale_both, shift_both = channels[:KERNEL], channels[KERNEL], channels[KERNEL + 1]
    normed, mixer_norm = norm_forward(after_attend, mixer_gain)
    mixer_in = on_chip(normed.astype(BF16))
    both_in = dot(mixer_in, mixer_both)

    def sides(first, second):
        return jnp.concatenate([first, second], axis=1)

    value_in = sides(both_in[:, :width], both_in[:, 2 * width : 3 * width])
    gate_in = sides(both_in[:, width : 2 * width], both_in[:, 3 * width :])
    gate = jax.nn.sigmoid(gate_in)
    glu = value_in * gate * live_column
    half = KERNEL // 2
    convolved = sum(shifted(glu, j - half, place) * depth[j] for j in range(KERNEL))
    weighted = convolved * live_column
    sums = jnp.stack(
        [
            jnp.sum(weighted, axis=0),
            jnp.sum(weighted * convolved, axis=0),
            jnp.broadcast_to(jnp.sum(live), (2 * width,)),
        ]
    )
    sums = sum_channels(sums)
    count = sums[2]
    bn_mean = sums[0] / count
    inverse = lax.rsqrt(sums[1] / count - bn_mean * bn_mean + NORM_EPSILON)
    normal = (convolved - bn_mean) * inverse
    shaped = normal * scale_both + shift_both
    mixer_active = swish(shaped).astype(BF16)
    after_mixer = after_attend + on_chip_sum(dot(mixer_active, mixer_out_both, BF16))

    branch, second_kept = branch_forward(after_mixer, second_gain, second_in, second_out, 2)
    after_second = after_mixer + 0.5 * branch
    output, final_norm = norm_forward(after_second, final_gain)

    chosen = dot(picker, output.astype(BF16), BF16)
    codes = jnp.concatenate([codes_other, codes], axis=0)
    slots = masked_rows.shape[0]
    vocab = head_weight.shape[1]
    near = on_chip(chosen)
    far = cross(chosen)

    def evaluate(part):
        logits = dot(part, head_weight)
        top = jnp.max(logits, axis=1)
        return (logits, top, jnp.sum(jnp.exp(logits - top[:, None]), axis=1))

    near_values = evaluate(near)
    far = on_chip(after(far, near_values[2]))
    far_values = evaluate(far)
    head_parts = [far, near]
    logits, top, total = zip(far_values, near_values)
    pair = jnp.stack([jnp.concatenate(top), jnp.concatenate(total)]).reshape(2, 4, slots)

    def merge(first, second):
        peak = jnp.maximum(first[0], second[0])
        return jnp.stack(
            [peak, first[1] * jnp.exp(first[0] - peak) + second[1] * jnp.exp(second[0] - peak)]
        )

    other = swap(pair)
    pair = merge(pair, jnp.stack([other[:, 1], other[:, 0], other[:, 3], other[:, 2]], axis=1))
    other = cross(pair)
    pair = merge(pair, jnp.concatenate([other[:, 2:], other[:, :2]], axis=1))
    log_totals = (pair[0] + jnp.log(pair[1])).reshape(2, 2 * slots)
    codes = codes.reshape(2, 2 * slots)
    own_loss = jnp.sum((codes[1, :slots] > 0).astype(F32) * log_totals[1, :slots])
    grad_logits, head_results = [], []
    for k in range(2):
        hits = (codes[k] - 1 - own * vocab)[:, None] == jnp.arange(vocab)[None, :]
        counted = (codes[k] > 0).astype(F32)
        own_loss = own_loss - jnp.sum(jnp.where(hits, logits[k], 0.0))
        shares = jnp.exp(logits[k] - log_totals[k][:, None])
        grad = (counted[:, None] * (shares - hits.astype(F32))).astype(BF16)
        grad_logits.append(grad)
        head_results.append(dot_t(grad, head_weight, BF16))
    grad_head = dot_rows(jnp.concatenate(head_parts), jnp.concatenate(grad_logits))
    grad_chosen = scatter_parts(head_results).astype(BF16)
    grad_output = out_cotangent.astype(F32) + weight_term(picker, grad_chosen)
    grad_second, final_gain_grad = norm_backward(final_norm, final_gain, grad_output)

    back, second_gain_grad, second_held, _ = branch_backward(
        second_gain,
        second_in,
        second_out,
        second_kept,
        0.5 * grad_second,
        2,
        (lambda: [grad_head], lambda: []),
    )
    grad_head = reduce_weights(grad_head)
    grad_mixer = grad_second + back

    grad_full = on_chip(grad_mixer.astype(BF16))
    grads, active, normed, grad_inner, _ = second_held
    grad_second_both = weights_call(
        [after(grads, grad_full), normed], [active, grad_inner], "second_weights"
    )
    grad_second_both = reduce_weights(grad_second_both)
    grad_shaped = dot_t(grad_full, mixer_out_both) * swish_slope(shaped)
    sums = sum_channels(
        jnp.stack([jnp.sum(grad_shaped, axis=0), jnp.sum(grad_shaped * normal, axis=0)])
    )
    batch_shift_grad, batch_scale_grad = sums[0], sums[1]
    grad_conv = (
        scale_both
        * inverse
        * (grad_shaped - live_column / count * (batch_shift_grad + normal * batch_scale_grad))
    )
    depth_grad = jnp.stack(
        [jnp.sum(grad_conv * shifted(glu, j - half, place), axis=0) for j in range(KERNEL)]
    )
    grad_glu = sum(shifted(grad_conv, half - j, place) * depth[j] for j in range(KERNEL))
    grad_glu = grad_glu * live_column
    grad_value = (grad_glu * gate).astype(BF16)
    grad_gate = (grad_glu * value_in * gate * (1.0 - gate)).astype(BF16)
    grad_both = jnp.concatenate(
        [grad_value[:, :width], grad_gate[:, :width], grad_value[:, width:], grad_gate[:, width:]],
        axis=1,
    )
    summed = dot_t(grad_both, mixer_both, BF16)
    back, mixer_gain_grad = norm_backward(mixer_norm, mixer_gain, on_chip_sum(summed))
    grad_attend = grad_mixer + back
    mixer_grads = weights_call([mixer_in, grad_full], [grad_both, mixer_active], "mixer_weights")
    counts = jnp.stack([own_loss, jnp.sum(keep)])
    counts = jnp.concatenate([counts, jnp.zeros((D - 2,), F32)])[None]
    depth_full = jnp.zeros((KERNEL, D), F32)
    for side, at in ((0, own), (1, (own + 2) % 4)):
        depth_full = lax.dynamic_update_slice_in_dim(
            depth_full, depth_grad[:, side * width : (side + 1) * width], at * width, 1
        )
    gains = jnp.concatenate(
        [mixer_gain_grad, second_gain_grad, final_gain_grad, counts, depth_full], axis=0
    )
    gain_run = sum_steps(gains)
    next(gain_run)
    gain_run.send(())
    gain_crossed = gain_run.send(())
    mixer_crossed = [
        cross(after(part, gain_crossed))
        for part in (mixer_grads[:, 2 * width : 4 * width], mixer_grads[:, 5 * width :])
    ]
    gain_run.send(())
    gain_run.send(())
    gains = gain_run.send(())
    loss = gains[3, 0] / gains[3, 1]
    depth_grad = lax.dynamic_slice_in_dim(gains[4:], own * width, width, 1)

    grad_full = on_chip(grad_attend.astype(BF16))
    grad_mixed = dot_t(grad_full, attend_out_both, BF16)
    grad_qkv = attend_backward_call(qkv, live_column, grad_mixed, log_total)
    mixer_crossed = after(jnp.concatenate(mixer_crossed, axis=1), grad_qkv)
    summed = dot_t(grad_qkv, qkv_weight, BF16)
    back, attend_gain_grad = norm_backward(attend_norm, attend_gain, on_chip_sum(summed))
    grad_first = grad_attend + back
    middle = weights_call([attend_in, grad_full], [grad_qkv, mixed], "attend_weights")
    mixer_sum = sides(mixer_grads[:, : 2 * width], mixer_grads[:, 4 * width : 5 * width])
    mixer_sum = (mixer_sum.astype(F32) + mixer_crossed.astype(F32)).astype(BF16)
    middle = reduce_weights(jnp.concatenate([middle, mixer_sum], axis=1))

    back, first_gain_grad, (grads, active, normed, grad_inner, sent), result = branch_backward(
        first_gain, first_in, first_out, first_kept, after(0.5 * grad_first, gains), 2
    )
    input_grad = grad_first + back
    gain_run = sum_steps(jnp.concatenate([attend_gain_grad, first_gain_grad], axis=0))
    next(gain_run)
    gain_run.send(())
    gain_run.send(())
    grad_out = dot_rows(after(grads, sent), active)
    run_out = reduce_by_steps(grad_out)
    next(run_out)
    grad_in = dot_rows(normed, after(grad_inner, grad_out))
    run_in = reduce_by_steps(grad_in)
    next(run_in)
    grad_head = after(grad_head, grad_in).astype(F32)
    grad_second_both = after(grad_second_both, grad_in).astype(F32)
    arrived = run_out.send((grad_in,))
    arrived = run_in.send((arrived,))
    gain_run.send((arrived,))
    run_out.send((arrived,))
    arrived = run_in.send(())
    gain_run.send((arrived,))
    grad_first_out = run_out.send(())
    grad_first_in = run_in.send(())
    first_gain_grad = gain_run.send((grad_first_in,))
    grad_second_out, grad_second_in = jnp.split(grad_second_both, 2, axis=1)
    middle = after(middle, grad_first_in).astype(F32)
    crossed = cross(
        jnp.concatenate([middle[:, 3 * width : 6 * width], middle[:, 7 * width : 8 * width]], axis=1).astype(BF16)
    )
    own_part = jnp.concatenate([middle[:, : 3 * width], middle[:, 6 * width : 7 * width]], axis=1)
    attend_grads = own_part + crossed.astype(F32)
    grad_query, grad_key, grad_value, grad_out = jnp.split(attend_grads, 4, axis=1)
    grad_mixer_value, grad_mixer_gate, grad_mixer_out = jnp.split(middle[:, 8 * width :], 3, axis=1)
    return (
        output,
        loss,
        input_grad,
        first_gain_grad[1],
        grad_first_in,
        grad_first_out.T,
        first_gain_grad[0],
        grad_query,
        grad_key,
        grad_value,
        grad_out.T,
        gains[0],
        grad_mixer_value,
        grad_mixer_gate,
        depth_grad,
        batch_scale_grad[:width],
        batch_shift_grad[:width],
        grad_mixer_out.T,
        gains[1],
        grad_second_in,
        grad_second_out.T,
        gains[2],
        grad_head,
    )


def solution(mesh):
    in_specs = (
        P(("dp", "mp"), None),
        P(("dp", "mp"), None),
        P("dp"),
        P(("dp", "mp")),
        P(("dp", "mp")),
        P(("dp", "mp"), None),
        P(),
        P(None, "mp"),
        P("mp", None),
        P(),
        P(None, "mp"),
        P(None, "mp"),
        P(None, "mp"),
        P("mp", None),
        P(),
        P(None, "mp"),
        P(None, "mp"),
        P(None, "mp"),
        P("mp"),
        P("mp"),
        P("mp", None),
        P(),
        P(None, "mp"),
        P("mp", None),
        P(),
        P(None, "mp"),
    )
    out_specs = (
        P(("dp", "mp"), None),
        P(),
        P(("dp", "mp"), None),
        P(),
        P("dp", "mp"),
        P("mp", "dp"),
        P(),
        P("dp", "mp"),
        P("dp", "mp"),
        P("dp", "mp"),
        P("mp", "dp"),
        P(),
        P("dp", "mp"),
        P("dp", "mp"),
        P(None, "mp"),
        P("mp"),
        P("mp"),
        P("mp", "dp"),
        P(),
        P("dp", "mp"),
        P("mp", "dp"),
        P(),
        P("dp", "mp"),
    )
    small = mesh.shape["dp"] == 8 and mesh.shape["mp"] == 4
    on_device = on_device_block if small else on_device_any
    return jax.shard_map(
        on_device, mesh=mesh, in_specs=in_specs, out_specs=out_specs, check_vma=False
    )
```

```python
import jax
import jax.numpy as jnp
from jax import lax
from jax.experimental import pallas as pl
from jax.experimental.pallas import tpu as pltpu
from jax.sharding import PartitionSpec as P

D = 1024
HEAD_DIM = 128
KERNEL = 5
LEN = 1024
SEQ_DEV = 2
TOK_DEV = 2048


NORM_EPSILON = 1e-05
MASKED_SCORE = -1000000000.0


def joined(shard, axis, combine):
    everything = jax.tree.map(lambda part: lax.all_gather(part, axis), shard)
    leading = jax.tree.map(lambda part: part[0], everything)

    def hop(k, so_far):
        return combine(so_far, jax.tree.map(lambda part: part[k], everything))

    return lax.fori_loop(1, lax.axis_size(axis), hop, leading)


def layer_norm(values, gain):
    center = values - jnp.mean(values, axis=-1, keepdims=True)
    spread = jnp.mean(center * center, axis=-1, keepdims=True)
    return center * lax.rsqrt(spread + NORM_EPSILON) * gain


def swish(values):
    return values * jax.nn.sigmoid(values)


def swish_slope(values):
    sigma = jax.nn.sigmoid(values)
    return sigma * (1.0 + values * (1.0 - sigma))


def depth_conv(glu, depth):
    length = glu.shape[1]
    half = KERNEL // 2
    padded = jnp.pad(glu, ((0, 0), (half, half), (0, 0)))
    total = padded[:, 0:length] * depth[0]
    for offset in range(1, KERNEL):
        total = total + padded[:, offset : offset + length] * depth[offset]
    return total


def matmul(left, right):
    return jnp.dot(left, right, preferred_element_type=jnp.float32)


def matmul_t(left, right):
    return lax.dot_general(
        left, right, (((1,), (1,)), ((), ())), preferred_element_type=jnp.float32
    )


def weight_term(left, right):
    return lax.dot_general(
        left, right, (((0,), (0,)), ((), ())), preferred_element_type=jnp.float32
    )


def spread_rows(values):
    return lax.all_gather(values, "mp", axis=0, tiled=True)


def collect_rows(values):
    return lax.psum_scatter(values, "mp", scatter_dimension=0, tiled=True)


def spread_grads(values):
    return lax.all_gather(values, "mp", axis=0, tiled=True)


def collect_grads(values):
    return lax.psum_scatter(values, "mp", scatter_dimension=0, tiled=True)


def weight_grad(left, right):
    return weight_term(left, right)


def combine_parts(first, second):
    top = jnp.maximum(first[0], second[0])
    total = first[1] * jnp.exp(first[0] - top) + second[1] * jnp.exp(second[0] - top)
    return (top, total)


def feed_forward(resid, gain, expand, project):
    normed, norm_pullback = jax.vjp(layer_norm, resid, gain)
    gathered = spread_rows(normed.astype(jnp.bfloat16))
    inner = matmul(gathered, expand)
    active = swish(inner).astype(jnp.bfloat16)
    return (collect_rows(matmul(active, project)), (norm_pullback, gathered, inner, active))


def feed_backward(expand, project, kept, grad_branch):
    norm_pullback, gathered, inner, active = kept
    grad_full = spread_grads(grad_branch.astype(jnp.bfloat16))
    grad_inner = (matmul_t(grad_full, project) * swish_slope(inner)).astype(jnp.bfloat16)
    grad_project = weight_grad(grad_full, active)
    grad_expand = weight_grad(gathered, grad_inner)
    grad_resid, grad_gain = norm_pullback(collect_grads(matmul_t(grad_inner, expand)))
    return (grad_resid, grad_gain, grad_expand, grad_project)


def attend_forward(resid, gain, query_weight, key_weight, value_weight, attend_out, live):
    normed, norm_pullback = jax.vjp(layer_norm, resid, gain)
    gathered = spread_rows(normed.astype(jnp.bfloat16))
    width = query_weight.shape[1]
    shape = (SEQ_DEV, LEN, width // HEAD_DIM, HEAD_DIM)
    query = matmul(gathered, query_weight).astype(jnp.bfloat16).reshape(shape)
    keys = matmul(gathered, key_weight).astype(jnp.bfloat16).reshape(shape)
    values = matmul(gathered, value_weight).astype(jnp.bfloat16).reshape(shape)
    scale = HEAD_DIM ** (-0.5)

    def one_utterance(pack):
        query_part, keys_part, values_part, alive = pack
        scores = (
            jnp.einsum("qhe,khe->hqk", query_part, keys_part, preferred_element_type=jnp.float32)
            * scale
        )
        scores = jnp.where(alive[None, None, :] > 0, scores, MASKED_SCORE)
        top = jnp.max(scores, axis=-1, keepdims=True)
        lifted = jnp.exp(scores - top)
        total = jnp.sum(lifted, axis=-1, keepdims=True)
        shares = (lifted / total).astype(jnp.bfloat16)
        mixed_part = jnp.einsum(
            "hqk,khe->qhe", shares, values_part, preferred_element_type=jnp.float32
        )
        return (mixed_part.astype(jnp.bfloat16), (top + jnp.log(total))[:, :, 0])

    mixed, log_total = lax.map(one_utterance, (query, keys, values, live))
    mixed = mixed.reshape(TOK_DEV, width)
    branch = collect_rows(matmul(mixed, attend_out))
    return (branch, (norm_pullback, gathered, query, keys, values, mixed, log_total))


def attend_backward(query_weight, key_weight, value_weight, attend_out, live, kept, grad_branch):
    norm_pullback, gathered, query, keys, values, mixed, log_total = kept
    width = query_weight.shape[1]
    grad_full = spread_grads(grad_branch.astype(jnp.bfloat16))
    grad_mixed = matmul_t(grad_full, attend_out).astype(jnp.bfloat16).reshape(query.shape)
    grad_attend_out = weight_grad(grad_full, mixed)
    scale = HEAD_DIM ** (-0.5)

    def one_utterance(pack):
        query_part, keys_part, values_part, alive, log_part, grad_part = pack
        scores = (
            jnp.einsum("qhe,khe->hqk", query_part, keys_part, preferred_element_type=jnp.float32)
            * scale
        )
        scores = jnp.where(alive[None, None, :] > 0, scores, MASKED_SCORE)
        shares = jnp.exp(scores - log_part[:, :, None])
        grad_values = jnp.einsum(
            "hqk,qhe->khe",
            shares.astype(jnp.bfloat16),
            grad_part,
            preferred_element_type=jnp.float32,
        )
        grad_shares = jnp.einsum(
            "qhe,khe->hqk", grad_part, values_part, preferred_element_type=jnp.float32
        )
        inner = jnp.sum(shares * grad_shares, axis=-1, keepdims=True)
        grad_scores = (shares * (grad_shares - inner)).astype(jnp.bfloat16)
        grad_query = (
            jnp.einsum("hqk,khe->qhe", grad_scores, keys_part, preferred_element_type=jnp.float32)
            * scale
        )
        grad_keys = (
            jnp.einsum("hqk,qhe->khe", grad_scores, query_part, preferred_element_type=jnp.float32)
            * scale
        )
        return (
            grad_query.astype(jnp.bfloat16),
            grad_keys.astype(jnp.bfloat16),
            grad_values.astype(jnp.bfloat16),
        )

    grad_query, grad_keys, grad_values = lax.map(
        one_utterance, (query, keys, values, live, log_total, grad_mixed)
    )
    grad_query = grad_query.reshape(TOK_DEV, width)
    grad_keys = grad_keys.reshape(TOK_DEV, width)
    grad_values = grad_values.reshape(TOK_DEV, width)
    grad_query_weight = weight_grad(gathered, grad_query)
    grad_key_weight = weight_grad(gathered, grad_keys)
    grad_value_weight = weight_grad(gathered, grad_values)
    summed = (
        matmul_t(grad_query, query_weight)
        + matmul_t(grad_keys, key_weight)
        + matmul_t(grad_values, value_weight)
    )
    grad_resid, grad_gain = norm_pullback(collect_grads(summed))
    return (
        grad_resid,
        grad_gain,
        grad_query_weight,
        grad_key_weight,
        grad_value_weight,
        grad_attend_out,
    )


def mixer_forward(
    resid,
    gain,
    mixer_value,
    mixer_gate,
    mixer_depth,
    batch_scale,
    batch_shift,
    mixer_out,
    live_flat,
):
    normed, norm_pullback = jax.vjp(layer_norm, resid, gain)
    gathered = spread_rows(normed.astype(jnp.bfloat16))
    value_in = matmul(gathered, mixer_value)
    gate_in = matmul(gathered, mixer_gate)
    channels = value_in.shape[1]

    def front(value_part, gate_part, depth):
        glu = value_part * jax.nn.sigmoid(gate_part) * live_flat[:, None]
        return depth_conv(glu.reshape(SEQ_DEV, LEN, channels), depth).reshape(TOK_DEV, channels)

    convolved, front_pullback = jax.vjp(front, value_in, gate_in, mixer_depth)
    weighted = convolved * live_flat[:, None]
    count, first_sum, second_sum = lax.psum(
        (jnp.sum(live_flat), jnp.sum(weighted, axis=0), jnp.sum(weighted * convolved, axis=0)), "dp"
    )
    bn_mean = first_sum / count
    inverse = lax.rsqrt(second_sum / count - bn_mean * bn_mean + NORM_EPSILON)
    normal = (convolved - bn_mean) * inverse
    shaped = normal * batch_scale + batch_shift
    active = swish(shaped).astype(jnp.bfloat16)
    branch = collect_rows(matmul(active, mixer_out))
    return (
        branch,
        (norm_pullback, gathered, front_pullback, normal, inverse, count, shaped, active),
    )


def mixer_backward(mixer_value, mixer_gate, batch_scale, mixer_out, live_flat, kept, grad_branch):
    norm_pullback, gathered, front_pullback, normal, inverse, count, shaped, active = kept
    grad_full = spread_grads(grad_branch.astype(jnp.bfloat16))
    grad_mixer_out = weight_grad(grad_full, active)
    grad_shaped = matmul_t(grad_full, mixer_out) * swish_slope(shaped)
    shift_grad, scale_grad = lax.psum(
        (jnp.sum(grad_shaped, axis=0), jnp.sum(grad_shaped * normal, axis=0)), "dp"
    )
    grad_conv = (
        batch_scale
        * inverse
        * (grad_shaped - live_flat[:, None] / count * (shift_grad + normal * scale_grad))
    )
    grad_value, grad_gate, depth_grad = front_pullback(grad_conv)
    grad_value = grad_value.astype(jnp.bfloat16)
    grad_gate = grad_gate.astype(jnp.bfloat16)
    grad_mixer_value = weight_grad(gathered, grad_value)
    grad_mixer_gate = weight_grad(gathered, grad_gate)
    summed = matmul_t(grad_value, mixer_value) + matmul_t(grad_gate, mixer_gate)
    grad_resid, grad_gain = norm_pullback(collect_grads(summed))
    return (
        grad_resid,
        grad_gain,
        grad_mixer_value,
        grad_mixer_gate,
        depth_grad,
        scale_grad,
        shift_grad,
        grad_mixer_out,
    )


def masked_head(output, own_live, masked_rows, targets, head_device, head_weight):
    rows = output.shape[0]
    sources = lax.axis_size("dp")
    capacity = rows // sources
    keep = own_live[masked_rows]
    chosen = output[masked_rows].astype(jnp.bfloat16)
    destination = head_device[:, 0]
    marks = (destination[:, None] == jnp.arange(sources)[None, :]).astype(jnp.int32)
    order = jnp.sum((jnp.cumsum(marks, axis=0) - marks) * marks, axis=1)
    placer = (destination * capacity + order)[:, None] == jnp.arange(rows)[None, :]
    packed = weight_term(placer.astype(jnp.bfloat16), chosen).astype(jnp.bfloat16)
    labels = (targets + 1) * (keep > 0).astype(jnp.int32)
    codes = jnp.sum(jnp.where(placer, labels[:, None], 0), axis=0)
    arrived, arrived_codes = (
        lax.all_to_all(packed, "dp", split_axis=0, concat_axis=0, tiled=True),
        lax.all_to_all(codes, "dp", split_axis=0, concat_axis=0, tiled=True),
    )
    shared, shared_codes = (
        lax.all_gather(arrived, "mp", axis=0, tiled=True),
        lax.all_gather(arrived_codes, "mp", axis=0, tiled=True),
    )
    logits = matmul(shared, head_weight)
    vocab = head_weight.shape[1]
    hits = (shared_codes - 1 - lax.axis_index("mp") * vocab)[:, None] == jnp.arange(vocab)[None, :]
    top = jnp.max(logits, axis=1)
    total = jnp.sum(jnp.exp(logits - top[:, None]), axis=1)
    picked = jnp.sum(jnp.where(hits, logits, 0.0), axis=1)
    top_all, total_all = joined((top, total), "mp", combine_parts)
    log_total = top_all + jnp.log(total_all)
    counted = (shared_codes > 0).astype(jnp.float32)
    own_total = jnp.sum(
        lax.dynamic_slice_in_dim(counted * log_total, lax.axis_index("mp") * rows, rows)
    )
    own_loss = own_total - jnp.sum(counted * picked)
    grad_logits = (
        counted[:, None] * (jnp.exp(logits - log_total[:, None]) - hits.astype(jnp.float32))
    ).astype(jnp.bfloat16)
    grad_head = weight_grad(shared, grad_logits)
    grad_shared = lax.psum_scatter(
        matmul_t(grad_logits, head_weight), "mp", scatter_dimension=0, tiled=True
    )
    returned = lax.all_to_all(
        grad_shared.astype(jnp.bfloat16), "dp", split_axis=0, concat_axis=0, tiled=True
    )
    grad_chosen = matmul(placer.astype(jnp.bfloat16), returned).astype(jnp.bfloat16)
    picker = (masked_rows[:, None] == jnp.arange(rows)[None, :]).astype(jnp.bfloat16)
    grad_rows = weight_term(picker, grad_chosen)
    return (grad_rows, grad_head, own_loss, jnp.sum(keep))


def on_device_any(
    frames,
    out_cotangent,
    lengths,
    masked_rows,
    targets,
    head_device,
    first_gain,
    first_in,
    first_out,
    attend_gain,
    query_weight,
    key_weight,
    value_weight,
    attend_out,
    mixer_gain,
    mixer_value,
    mixer_gate,
    mixer_depth,
    batch_scale,
    batch_shift,
    mixer_out,
    second_gain,
    second_in,
    second_out,
    final_gain,
    head_weight,
):
    rows = frames.shape[0]
    live = (jnp.arange(LEN)[None, :] < lengths[:, None]).astype(jnp.float32)
    live_flat = live.reshape(TOK_DEV)
    own_live = lax.dynamic_slice_in_dim(live_flat, lax.axis_index("mp") * rows, rows)
    start = frames.astype(jnp.float32)
    branch, first_kept = feed_forward(start, first_gain, first_in, first_out)
    after_first = start + 0.5 * branch
    branch, attend_kept = attend_forward(
        after_first, attend_gain, query_weight, key_weight, value_weight, attend_out, live
    )
    after_attend = after_first + branch
    branch, mixer_kept = mixer_forward(
        after_attend,
        mixer_gain,
        mixer_value,
        mixer_gate,
        mixer_depth,
        batch_scale,
        batch_shift,
        mixer_out,
        live_flat,
    )
    after_mixer = after_attend + branch
    branch, second_kept = feed_forward(after_mixer, second_gain, second_in, second_out)
    after_second = after_mixer + 0.5 * branch
    output, final_pullback = jax.vjp(layer_norm, after_second, final_gain)
    grad_rows, grad_head, own_loss, own_count = masked_head(
        output, own_live, masked_rows, targets, head_device, head_weight
    )
    grad_second, final_gain_grad = final_pullback(out_cotangent.astype(jnp.float32) + grad_rows)
    back_resid, second_gain_grad, grad_second_in, grad_second_out = feed_backward(
        second_in, second_out, second_kept, 0.5 * grad_second
    )
    grad_mixer = grad_second + back_resid
    (
        back_resid,
        mixer_gain_grad,
        grad_mixer_value,
        grad_mixer_gate,
        depth_grad,
        batch_scale_grad,
        batch_shift_grad,
        grad_mixer_out,
    ) = mixer_backward(
        mixer_value, mixer_gate, batch_scale, mixer_out, live_flat, mixer_kept, grad_mixer
    )
    grad_attend = grad_mixer + back_resid
    back_resid, attend_gain_grad, grad_query, grad_key, grad_value, grad_attend_out = (
        attend_backward(
            query_weight, key_weight, value_weight, attend_out, live, attend_kept, grad_attend
        )
    )
    grad_first = grad_attend + back_resid
    back_resid, first_gain_grad, grad_first_in, grad_first_out = feed_backward(
        first_in, first_out, first_kept, 0.5 * grad_first
    )
    input_grad = grad_first + back_resid
    channels = mixer_value.shape[1]
    offset = lax.axis_index("mp") * channels
    depth_full = lax.dynamic_update_slice_in_dim(
        jnp.zeros((KERNEL, D), jnp.float32), depth_grad, offset, 1
    )
    (
        first_gain_grad,
        attend_gain_grad,
        mixer_gain_grad,
        second_gain_grad,
        final_gain_grad,
        depth_full,
        loss_sum,
        loss_count,
    ) = lax.psum(
        (
            first_gain_grad,
            attend_gain_grad,
            mixer_gain_grad,
            second_gain_grad,
            final_gain_grad,
            depth_full,
            own_loss,
            own_count,
        ),
        ("dp", "mp"),
    )
    mixer_depth_grad = lax.dynamic_slice_in_dim(depth_full, offset, channels, 1)
    loss = loss_sum / loss_count
    (
        grad_first_in,
        grad_first_out,
        grad_query,
        grad_key,
        grad_value,
        grad_attend_out,
        grad_mixer_value,
        grad_mixer_gate,
        grad_mixer_out,
        grad_second_in,
        grad_second_out,
        grad_head,
    ) = (
        lax.psum_scatter(grad_first_in, "dp", scatter_dimension=0, tiled=True),
        lax.psum_scatter(grad_first_out, "dp", scatter_dimension=0, tiled=True),
        lax.psum_scatter(grad_query, "dp", scatter_dimension=0, tiled=True),
        lax.psum_scatter(grad_key, "dp", scatter_dimension=0, tiled=True),
        lax.psum_scatter(grad_value, "dp", scatter_dimension=0, tiled=True),
        lax.psum_scatter(grad_attend_out, "dp", scatter_dimension=0, tiled=True),
        lax.psum_scatter(grad_mixer_value, "dp", scatter_dimension=0, tiled=True),
        lax.psum_scatter(grad_mixer_gate, "dp", scatter_dimension=0, tiled=True),
        lax.psum_scatter(grad_mixer_out, "dp", scatter_dimension=0, tiled=True),
        lax.psum_scatter(grad_second_in, "dp", scatter_dimension=0, tiled=True),
        lax.psum_scatter(grad_second_out, "dp", scatter_dimension=0, tiled=True),
        lax.psum_scatter(grad_head, "dp", scatter_dimension=0, tiled=True),
    )
    return (
        output,
        loss,
        input_grad,
        first_gain_grad,
        grad_first_in,
        grad_first_out.T,
        attend_gain_grad,
        grad_query,
        grad_key,
        grad_value,
        grad_attend_out.T,
        mixer_gain_grad,
        grad_mixer_value,
        grad_mixer_gate,
        mixer_depth_grad,
        batch_scale_grad,
        batch_shift_grad,
        grad_mixer_out.T,
        second_gain_grad,
        grad_second_in,
        grad_second_out.T,
        final_gain_grad,
        grad_head,
    )


BF16 = jnp.bfloat16
F32 = jnp.float32
SCALE = HEAD_DIM ** (-0.5)
CORE_PAIRS = [(0, 1), (1, 0), (2, 3), (3, 2)]
CHIP_PAIRS = [(0, 2), (2, 0), (1, 3), (3, 1)]
X_PAIRS = [(0, 1), (1, 0), (2, 3), (3, 2), (4, 5), (5, 4), (6, 7), (7, 6)]
Z_NEAR_PAIRS = [(0, 2), (2, 0), (1, 3), (3, 1), (4, 6), (6, 4), (5, 7), (7, 5)]
Z_FAR_PAIRS = [(0, 4), (4, 0), (1, 5), (5, 1), (2, 6), (6, 2), (3, 7), (7, 3)]


def swap(values):
    return lax.ppermute(values, "mp", CORE_PAIRS)


def cross(values):
    return lax.ppermute(values, "mp", CHIP_PAIRS)


def sum_over_dp(values):
    for pairs in (X_PAIRS, Z_NEAR_PAIRS, Z_FAR_PAIRS):
        values = values + lax.ppermute(values, "dp", pairs)
    return values


def sum_over_all(values):
    values = values + swap(values)
    values = values + cross(values)
    return sum_over_dp(values)


def sum_channels(values, *earlier):
    other = cross(values)
    half = values.shape[-1] // 2
    turned = jnp.concatenate([other[..., half:], other[..., :half]], axis=-1)
    return sum_over_dp(after(values + turned, *earlier))


def clamped(block, width, first, last):
    return pl.BlockSpec((block, width), lambda i: (jnp.clip(i, first, last) - first, 0))


def part_specs(parts, block):
    rows, width = parts[0].shape
    specs, at = [], 0
    for part in parts:
        if part.shape[0] == rows:
            specs.append(clamped(block, width, 0, rows // block - 1))
            continue
        steps = part.shape[0] // block
        specs.append(clamped(block, width, at, at + steps - 1))
        at += steps
    return specs


def part_total(refs, parts, block):
    rows = parts[0].shape[0]
    total, at = None, 0
    for ref, part in zip(refs, parts):
        value = ref[...].astype(F32)
        if part.shape[0] != rows:
            steps = part.shape[0] // block
            step = pl.program_id(0)
            value = jnp.where((step >= at) & (step < at + steps), value, 0.0)
            at += steps
        total = value if total is None else total + value
    return total


NORM_BLOCK = 256


def center_of(values):
    center = values - jnp.mean(values, axis=-1, keepdims=True)
    inverse = lax.rsqrt(jnp.mean(center * center, axis=-1, keepdims=True) + NORM_EPSILON)
    return (center * inverse, inverse)


def streamed(array):
    return pltpu.with_memory_space_constraint(array, pltpu.HBM)


def norm_forward(base, parts, gain, scale, exact=False):
    rows, width = base.shape
    block = NORM_BLOCK
    row = pl.BlockSpec((block, width), lambda i: (i, 0))
    number = len(parts)

    def kernel(base_ref, *refs):
        parts_refs, gain_ref, outs = refs[:number], refs[number], list(refs[number + 1 :])
        values = base_ref[...].astype(F32)
        if parts:
            values = values + scale * part_total(parts_refs, parts, block)
            outs.pop(0)[...] = values
        normed = center_of(values)[0] * gain_ref[...]
        outs.pop(0)[...] = normed.astype(BF16)
        if exact:
            outs.pop(0)[...] = normed

    kinds = ([F32] if parts else []) + [BF16] + ([F32] if exact else [])
    results = pl.pallas_call(
        kernel,
        grid=(rows // block,),
        in_specs=[row]
        + (part_specs(parts, block) if parts else [])
        + [pl.BlockSpec((1, width), lambda i: (0, 0))],
        out_specs=[row] * len(kinds),
        out_shape=[
            jax.ShapeDtypeStruct((rows, width), kind) if kind == BF16 else pltpu.HBM((rows, width), kind)
            for kind in kinds
        ],
        compiler_params=pltpu.CompilerParams(vmem_limit_bytes=24 << 20),
        cost_estimate=cost(10 * base.size, 8 * base.size),
        name="norm_forward",
    )(streamed(base), *parts, gain[None])
    return results if parts else [base, *results]


def norm_backward(values, gain, parts, grad, scale, pick=None):
    rows, width = values.shape
    block = NORM_BLOCK
    row = pl.BlockSpec((block, width), lambda i: (i, 0))
    number = len(parts)
    optional = list(pick) if pick is not None else []
    optional_specs = []
    if pick is not None:
        slots = pick[0].shape[1]
        optional_specs = [
            pl.BlockSpec((block, slots), lambda i: (i, 0)),
            pl.BlockSpec((slots, width), lambda i: (0, 0)),
        ]
    if grad is not None:
        optional.append(streamed(grad))
        optional_specs.append(row)

    def kernel(values_ref, gain_ref, *refs):
        parts_refs, refs = refs[:number], list(refs[number:])
        total = part_total(parts_refs, parts, block)
        if pick is not None:
            total = total + matmul(refs.pop(0)[...], refs.pop(0)[...])
        unit, inverse = center_of(values_ref[...].astype(F32))
        scaled = total * gain_ref[...]
        inner = jnp.mean(scaled * unit, axis=-1, keepdims=True)
        result = inverse * (scaled - jnp.mean(scaled, axis=-1, keepdims=True) - unit * inner)
        if grad is not None:
            result = result + refs.pop(0)[...]
        grad_ref, low_ref, gain_grad_ref = refs
        grad_ref[...] = result
        low_ref[...] = (scale * result).astype(BF16)
        gain_grad = jnp.sum(total * unit, axis=0, keepdims=True)

        @pl.when(pl.program_id(0) == 0)
        def _():
            gain_grad_ref[...] = gain_grad

        @pl.when(pl.program_id(0) > 0)
        def _():
            gain_grad_ref[...] += gain_grad

    one = pl.BlockSpec((1, width), lambda i: (0, 0))
    return pl.pallas_call(
        kernel,
        grid=(rows // block,),
        in_specs=[row, one] + part_specs(parts, block) + optional_specs,
        out_specs=[row, row, one],
        out_shape=[
            pltpu.HBM((rows, width), F32),
            jax.ShapeDtypeStruct((rows, width), BF16),
            jax.ShapeDtypeStruct((1, width), F32),
        ],
        compiler_params=pltpu.CompilerParams(vmem_limit_bytes=24 << 20),
        cost_estimate=cost(20 * values.size, 12 * values.size),
        name="norm_backward",
    )(streamed(values), gain[None], *parts, *optional)


def on_chip(values):
    return jnp.concatenate([values, swap(values)], axis=0)


def on_chip_sum(own, other):
    return own.astype(F32) + swap(other).astype(F32)


def dot(left, right, kind=F32):
    return jnp.dot(left, right, preferred_element_type=F32).astype(kind)


def dot_t(left, right, kind=F32):
    return matmul_t(left, right).astype(kind)


def dot_rows(lefts, rights):
    total = weight_term(lefts, rights)
    return total.astype(BF16)


def after(values, *earlier):
    return lax.optimization_barrier((values, *earlier))[0]


def early(flops, size):
    return pl.CostEstimate(flops=flops // 1000, bytes_accessed=size // 1000, transcendentals=0)


def cost(flops, size):
    return pl.CostEstimate(flops=flops, bytes_accessed=size, transcendentals=0)


BLOCK = 256


def pieces_call(body, pieces, row_inputs, weights, row_outputs, held, start, total, name):
    rows, width = pieces[0].shape
    block = min(BLOCK, rows)
    half, first = rows // block, start // block
    steps = 2 * half

    def kernel(*refs):
        refs = list(refs)
        inputs, refs = refs[: 2 + len(row_inputs) + len(weights)], refs[2 + len(row_inputs) + len(weights) :]
        if held is not None:
            refs = refs[len(held) :]
        step = pl.program_id(0)
        piece = jnp.where(step < half, inputs[0][...], inputs[1][...])
        result = body(piece, inputs[2:], refs[: len(row_outputs)])

        @pl.when(step < half)
        def _():
            refs[-2][...] = result

        @pl.when(step >= half)
        def _():
            refs[-1][...] = result

    def kept(array):
        return pl.BlockSpec(array.shape, lambda i: (0,) * array.ndim)

    def placed(size):
        return pl.BlockSpec((block, size), lambda i: (i + first, 0))

    two = [
        pl.BlockSpec((block, width), lambda i: (jnp.minimum(i, half - 1), 0)),
        pl.BlockSpec((block, width), lambda i: (jnp.maximum(i - half, 0), 0)),
    ]
    row_inputs = [pltpu.with_memory_space_constraint(array, pltpu.HBM) for array in row_inputs]
    operands = [*pieces, *row_inputs, *weights]
    in_specs = two + [placed(array.shape[1]) for array in row_inputs] + [kept(w) for w in weights]
    aliases = {}
    if held is not None:
        aliases = {len(operands) + k: k for k in range(len(held))}
        operands += held
        in_specs += [pl.BlockSpec(memory_space=pl.ANY)] * len(held)
    flops = 2 * 2 * rows * sum(w.size for w in weights if w.ndim == 2 and w.shape[0] > 1)
    return pl.pallas_call(
        kernel,
        grid=(steps,),
        in_specs=in_specs,
        out_specs=[placed(size) for size in row_outputs] + two,
        out_shape=[pltpu.HBM((total, size), BF16) for size in row_outputs]
        + [jax.ShapeDtypeStruct((rows, width), BF16)] * 2,
        input_output_aliases=aliases,
        compiler_params=pltpu.CompilerParams(vmem_limit_bytes=32 << 20),
        cost_estimate=early(flops, 2 * sum(w.size for w in weights)),
        name=name,
    )(*operands)


def expand_body(piece, inputs, outputs):
    expand_ref, project_ref = inputs
    held_ref, inner_ref, active_ref = outputs
    inner = matmul(piece, expand_ref[...])
    active = swish(inner).astype(BF16)
    held_ref[...] = piece
    inner_ref[...] = inner.astype(BF16)
    active_ref[...] = active
    return matmul(active, project_ref[...]).astype(BF16)


def expand_back_body(piece, inputs, outputs):
    inner_ref, expand_ref, project_ref = inputs
    held_ref, grad_ref = outputs
    slope = swish_slope(inner_ref[...].astype(F32))
    grad = (matmul_t(piece, project_ref[...]) * slope).astype(BF16)
    held_ref[...] = piece
    grad_ref[...] = grad
    return matmul_t(grad, expand_ref[...]).astype(BF16)


def swap_halves(values):
    half = values.shape[0] // 2
    return jnp.concatenate([swap(values[:half]), swap(values[half:])], axis=0)


def branch_over(values, number, call, beside=None, last=None):
    rows = values.shape[0]
    step = rows // number
    far = [cross(values[k * step : (k + 1) * step]) for k in range(number)]
    held, (own, other) = call((values, swap(values)), None, 0)
    near = [own, swap(other)]
    done, back = own, []
    for k in range(number):
        part = after(far[k], done)
        other = swap_halves(part)
        if beside is not None:
            other = after(other, *beside[k](done))
        held, (own, other) = call((part, other), held, 2 * rows + 2 * step * k)
        result = (own.astype(F32) + swap_halves(other).astype(F32)).astype(BF16)
        result = after(result, *back)
        back.append(cross(result))
        done = own
    extra = None
    if last is not None:
        extra = last(held, result)
        back[-1] = after(back[-1], extra[0])
    return (near + back, held, extra)


def branch_forward(normed, expand, project, number, beside=None):
    total = 4 * normed.shape[0]
    sizes = [normed.shape[1], expand.shape[1], expand.shape[1]]

    def call(pieces, held, start):
        *held, own, other = pieces_call(
            expand_body, pieces, [], [expand, project], sizes, held, start, total, "branch_forward"
        )
        return (held, (own, other))

    parts, held, _ = branch_over(normed, number, call, beside)
    return (parts, held)


def branch_backward(expand, project, kept, grad_branch, number, beside, last):
    normed, inner, active = kept
    total = 4 * grad_branch.shape[0]
    sizes = [grad_branch.shape[1], expand.shape[1]]

    def call(pieces, held, start):
        *held, own, other = pieces_call(
            expand_back_body, pieces, [inner], [expand, project], sizes, held, start, total,
            "branch_backward",
        )
        return (held, (own, other))

    def weights(held, sent):
        grads, grad_inner = held
        return last(after(grads, sent), active, normed, grad_inner)

    parts, held, extra = branch_over(grad_branch, number, call, beside, weights)
    return (parts, (*held, active, normed), extra)


def attend_kernel(live_ref, query_ref, keys_ref, values_ref, mixed_ref, total_ref):
    scores = matmul_t(keys_ref[...], query_ref[...]) * SCALE
    scores = jnp.where(live_ref[...] > 0, scores, MASKED_SCORE)
    top = jnp.max(scores, axis=0, keepdims=True)
    lifted = jnp.exp(scores - top)
    total = jnp.sum(lifted, axis=0, keepdims=True)
    mixed = weight_term(values_ref[...], lifted.astype(BF16)) * (1.0 / total)
    mixed_ref[...] = mixed.T.astype(BF16)
    total_ref[0] = top + jnp.log(total)


def head_column(head, kind):
    return (head // 2) * 6 + kind * 2 + head % 2


def attend_forward_call(qkv, live_column):
    length = qkv.shape[0]
    heads = qkv.shape[1] // (3 * HEAD_DIM)
    block = length

    def whole(kind):
        return pl.BlockSpec((length, HEAD_DIM), lambda h, b: (0, head_column(h, kind)))

    return pl.pallas_call(
        attend_kernel,
        grid=(heads, length // block),
        in_specs=[
            pl.BlockSpec((length, 1), lambda h, b: (0, 0)),
            pl.BlockSpec((block, HEAD_DIM), lambda h, b: (b, head_column(h, 0))),
            whole(1),
            whole(2),
        ],
        out_specs=[
            pl.BlockSpec((block, HEAD_DIM), lambda h, b: (b, h)),
            pl.BlockSpec((1, 1, block), lambda h, b: (h, 0, b)),
        ],
        out_shape=[
            jax.ShapeDtypeStruct((length, heads * HEAD_DIM), BF16),
            jax.ShapeDtypeStruct((heads, 1, length), F32),
        ],
        compiler_params=pltpu.CompilerParams(vmem_limit_bytes=32 << 20),
        cost_estimate=cost(4 * heads * length * length * HEAD_DIM, 8 * qkv.size),
        name="attend_forward",
    )(live_column, qkv, qkv, qkv)


def attend_back_kernel(
    live_ref, query_ref, keys_ref, values_ref, grad_ref, total_ref, out_ref, keys_sum, values_sum
):
    head, block = pl.program_id(0), pl.program_id(1)
    rows = query_ref.shape[0]
    query, keys, grad = query_ref[...], keys_ref[...], grad_ref[...]
    scores = matmul_t(keys, query) * SCALE
    scores = jnp.where(live_ref[...] > 0, scores, MASKED_SCORE)
    shares = jnp.exp(scores - total_ref[0])
    grad_shares = matmul_t(values_ref[...], grad)
    inner = jnp.sum(shares * grad_shares, axis=0, keepdims=True)
    grad_scores = (shares * (grad_shares - inner)).astype(BF16)
    grad_values = dot(shares.astype(BF16), grad)
    grad_keys = dot(grad_scores, query) * SCALE
    grad_query = (weight_term(keys, grad_scores) * SCALE).T.astype(BF16)

    def columns(kind):
        start = head_column(head, kind) * HEAD_DIM
        return pl.ds(pl.multiple_of(start, HEAD_DIM), HEAD_DIM)

    out_ref[pl.ds(pl.multiple_of(block * rows, rows), rows), columns(0)] = grad_query

    @pl.when(block == 0)
    def _():
        keys_sum[...] = grad_keys
        values_sum[...] = grad_values

    @pl.when(block > 0)
    def _():
        keys_sum[...] += grad_keys
        values_sum[...] += grad_values

    @pl.when(block == pl.num_programs(1) - 1)
    def _():
        out_ref[:, columns(1)] = keys_sum[...].astype(BF16)
        out_ref[:, columns(2)] = values_sum[...].astype(BF16)


def attend_backward_call(qkv, live_column, grad_mixed, log_total):
    length = qkv.shape[0]
    heads = qkv.shape[1] // (3 * HEAD_DIM)
    block = length // 2

    def whole(kind):
        return pl.BlockSpec((length, HEAD_DIM), lambda h, b: (0, head_column(h, kind)))

    return pl.pallas_call(
        attend_back_kernel,
        grid=(heads, length // block),
        in_specs=[
            pl.BlockSpec((length, 1), lambda h, b: (0, 0)),
            pl.BlockSpec((block, HEAD_DIM), lambda h, b: (b, head_column(h, 0))),
            whole(1),
            whole(2),
            pl.BlockSpec((block, HEAD_DIM), lambda h, b: (b, h)),
            pl.BlockSpec((1, 1, block), lambda h, b: (h, 0, b)),
        ],
        out_specs=pl.BlockSpec(qkv.shape, lambda h, b: (0, 0)),
        out_shape=jax.ShapeDtypeStruct(qkv.shape, BF16),
        scratch_shapes=[pltpu.VMEM((length, HEAD_DIM), F32), pltpu.VMEM((length, HEAD_DIM), F32)],
        compiler_params=pltpu.CompilerParams(vmem_limit_bytes=40 << 20),
        cost_estimate=cost(10 * heads * length * length * HEAD_DIM, 8 * qkv.size),
        name="attend_backward",
    )(live_column, qkv, qkv, qkv, grad_mixed, log_total)


def rows_call(
    body, name, pieces, row_inputs, weights, row_outputs, result, sums=None, scalars=None, turned=True
):
    rows = 2 * pieces[0].shape[0] if pieces is not None else row_inputs[0].shape[0]
    block = BLOCK
    half = rows // 2 // block
    steps = 2 * half
    number, stay = len(row_inputs), len(weights)

    def kernel(scalar_ref, *refs):
        refs = list(refs)
        step = pl.program_id(0)
        piece = None
        if pieces is not None:
            piece = jnp.where(step < half, refs[0][...], refs[1][...])
            refs = refs[2:]
        inputs, refs = refs[:number], refs[number:]
        held, refs = refs[:stay], refs[stay:]
        outputs, refs = refs[: len(row_outputs)], refs[len(row_outputs) :]
        sums_ref = refs[-1] if sums is not None else None
        if sums is not None:

            @pl.when(step == 0)
            def _():
                sums_ref[...] = jnp.zeros_like(sums_ref)

        value = body(scalar_ref, piece, inputs, held, outputs, sums_ref)
        if result is not None:

            @pl.when(step < half)
            def _():
                refs[0][...] = value

            @pl.when(step >= half)
            def _():
                refs[1][...] = value

    def row(width):
        if turned:
            return pl.BlockSpec((block, width), lambda i, at: ((i + at[0] * half) % steps, 0))
        return pl.BlockSpec((block, width), lambda i, at: (i, 0))

    def two(width):
        return [
            pl.BlockSpec((block, width), lambda i, at: (jnp.minimum(i, half - 1), 0)),
            pl.BlockSpec((block, width), lambda i, at: (jnp.maximum(i, half) - half, 0)),
        ]

    def kept(shape):
        return pl.BlockSpec(shape, lambda i, at: (0,) * len(shape))

    in_specs, operands = [], [scalars]
    if pieces is not None:
        in_specs += two(pieces[0].shape[1])
        operands += pieces
    in_specs += [row(array.shape[1]) for array in row_inputs] + [kept(w.shape) for w in weights]
    operands += [*row_inputs, *(streamed(w) if w.shape[0] >= BLOCK else w for w in weights)]
    out_specs = [row(width) for width, _ in row_outputs]
    out_shape = [
        pltpu.HBM((rows, width), BF16) if kind is None else jax.ShapeDtypeStruct((rows, width), kind)
        for width, kind in row_outputs
    ]
    if result is not None:
        out_specs += two(result)
        out_shape += [jax.ShapeDtypeStruct((rows // 2, result), BF16)] * 2
    if sums is not None:
        out_specs.append(kept(sums))
        out_shape.append(jax.ShapeDtypeStruct(sums, F32))
    return pl.pallas_call(
        kernel,
        grid_spec=pltpu.PrefetchScalarGridSpec(
            num_scalar_prefetch=1, grid=(steps,), in_specs=in_specs, out_specs=out_specs
        ),
        out_shape=out_shape,
        compiler_params=pltpu.CompilerParams(vmem_limit_bytes=28 << 20),
        cost_estimate=cost(2 * rows * sum(w.size for w in weights), 2 * sum(w.size for w in weights)),
        name=name,
    )(*operands)


def quarter(scalar_ref, k):
    rows = D // 4
    at = scalar_ref[1] ^ k
    return pl.ds(pl.multiple_of(at * rows, rows), rows)


def qkv_body(scalar_ref, piece, inputs, held, outputs, sums_ref):
    out_ref, held_ref = outputs
    width = held[0].shape[1]
    held_ref[...] = piece
    for k in range(3):
        out_ref[:, k * width : (k + 1) * width] = matmul(piece, held[k][...]).astype(BF16)
    total = None
    for k in range(4):
        part = matmul(held_ref[:, quarter(scalar_ref, k)], held[3 + k][...])
        total = part if total is None else total + part
    out_ref[:, 3 * width :] = total.astype(BF16)


def qkv_back_body(scalar_ref, piece, inputs, held, outputs, sums_ref):
    width = held[0].shape[1]
    grad_ref = inputs[0]
    own = None
    for k in range(3):
        part = matmul_t(grad_ref[:, k * width : (k + 1) * width], held[k][...])
        own = part if own is None else own + part
    far = [matmul_t(grad_ref[:, 3 * width :], held[3 + k][...]) for k in range(4)]
    at = scalar_ref[1]
    near = [jnp.where(at % 2 == 0, far[k], far[k ^ 1]) for k in range(4)]
    placed = [jnp.where(at // 2 == 0, near[k], near[k ^ 2]) for k in range(4)]
    return (own + jnp.concatenate(placed, axis=1)).astype(BF16)


def out_body(scalar_ref, piece, inputs, held, outputs, sums_ref):
    width = held[0].shape[0]
    values = inputs[0][...]
    total = matmul(values[:, :width], held[0][...]) + matmul(values[:, width:], held[1][...])
    return total.astype(BF16)


def out_back_body(scalar_ref, piece, inputs, held, outputs, sums_ref):
    width = held[0].shape[0]
    outputs[0][:, :width] = matmul_t(piece, held[0][...]).astype(BF16)
    outputs[0][:, width:] = matmul_t(piece, held[1][...]).astype(BF16)
    outputs[1][...] = piece


def shape_body(scalar_ref, piece, inputs, held, outputs, sums_ref):
    stats_ref, *weights = held
    stats = stats_ref[...]
    normal = (inputs[0][...] - stats[0:1]) * stats[1:2]
    shaped = normal * stats[2:3] + stats[3:4]
    active = swish(shaped).astype(BF16)
    outputs[0][...] = active
    width = weights[0].shape[0]
    total = matmul(active[:, :width], weights[0][...]) + matmul(active[:, width:], weights[1][...])
    return total.astype(BF16)


def shape_back_body(scalar_ref, piece, inputs, held, outputs, sums_ref):
    stats_ref, *weights = held
    stats = stats_ref[...]
    width = weights[0].shape[0]
    outputs[1][...] = piece
    for side in range(2):
        columns = slice(side * width, (side + 1) * width)
        normal = (inputs[0][:, columns] - stats[0:1, columns]) * stats[1:2, columns]
        shaped = normal * stats[2:3, columns] + stats[3:4, columns]
        grad = matmul_t(piece, weights[side][...]) * swish_slope(shaped)
        outputs[0][:, columns] = grad
        sums_ref[0:1, columns] += jnp.sum(grad, axis=0, keepdims=True)
        sums_ref[1:2, columns] += jnp.sum(grad * normal, axis=0, keepdims=True)


EDGE = 8


def set_padded(padded_ref, values):
    rows = values.shape[0]
    zeros = jnp.zeros((EDGE, values.shape[1]), F32)
    padded_ref[:EDGE] = zeros
    padded_ref[EDGE + rows :] = zeros
    padded_ref[EDGE : EDGE + rows] = values


def moved(padded_ref, offset):
    rows = padded_ref.shape[0] - 2 * EDGE
    return padded_ref[EDGE + offset : EDGE + offset + rows]


def live_rows(scalar_ref, rows):
    return (lax.broadcasted_iota(jnp.int32, (rows, 1), 0) < scalar_ref[1]).astype(F32)


def mixer_front_kernel(
    scalar_ref, own_ref, other_ref, value_ref, gate_ref, value_far_ref, gate_far_ref, depth_ref,
    held_ref, value_out, gate_out, conv_out, sums_ref, padded_ref,
):
    side = pl.program_id(0)
    half = own_ref.shape[0]
    rows = 2 * half
    core = scalar_ref[0]
    value_weight = jnp.where(side == 0, value_ref[...], value_far_ref[...])
    gate_weight = jnp.where(side == 0, gate_ref[...], gate_far_ref[...])
    for at, ref in ((core, own_ref), (1 - core, other_ref)):
        piece = ref[...]
        place = pl.ds(pl.multiple_of(at * half, half), half)
        value_out[place] = matmul(piece, value_weight)
        gate_out[place] = jax.nn.sigmoid(matmul(piece, gate_weight))
        held_ref[place] = piece
    live = live_rows(scalar_ref, rows)
    set_padded(padded_ref, value_out[...] * gate_out[...] * live)
    middle = KERNEL // 2
    conv = sum(moved(padded_ref, j - middle) * depth_ref[j : j + 1] for j in range(KERNEL))
    conv_out[...] = conv
    weighted = conv * live
    sums_ref[0:1] = jnp.sum(weighted, axis=0, keepdims=True)
    sums_ref[1:2] = jnp.sum(weighted * conv, axis=0, keepdims=True)
    sums_ref[2:3] = jnp.broadcast_to(jnp.sum(live, axis=0, keepdims=True), (1, weighted.shape[1]))


def mixer_front_call(scalars, own, other, weights, depth):
    half, width = own.shape
    rows, channels = 2 * half, weights[0].shape[1]

    def kept(shape):
        return pl.BlockSpec(shape, lambda i: (0,) * len(shape))

    def side(height):
        return pl.BlockSpec((height, channels), lambda i: (0, i))

    return pl.pallas_call(
        mixer_front_kernel,
        grid=(2,),
        in_specs=[pl.BlockSpec(memory_space=pltpu.SMEM), kept(own.shape), kept(other.shape)]
        + [kept(w.shape) for w in weights]
        + [side(depth.shape[0])],
        out_specs=[kept((rows, width)), side(rows), side(rows), side(rows), side(3)],
        out_shape=[pltpu.HBM((rows, width), BF16)]
        + [pltpu.HBM((rows, 2 * channels), F32)] * 2
        + [jax.ShapeDtypeStruct((rows, 2 * channels), F32)]
        + [jax.ShapeDtypeStruct((3, 2 * channels), F32)],
        scratch_shapes=[pltpu.VMEM((rows + 2 * EDGE, channels), F32)],
        compiler_params=pltpu.CompilerParams(vmem_limit_bytes=36 << 20),
        cost_estimate=cost(8 * rows * width * channels, 8 * width * channels),
        name="mixer_front",
    )(scalars, own, other, *map(streamed, weights), depth)


def mixer_back_kernel(
    scalar_ref, grad_ref, conv_ref, value_in, gate_in, stats_ref, sums_ref, depth_ref,
    value_ref, gate_ref, value_far_ref, gate_far_ref,
    both_ref, depth_out, own_ref, other_ref, total_ref, padded_ref, padded_glu_ref,
):
    side = pl.program_id(0)
    rows, channels = grad_ref.shape
    core = scalar_ref[0]
    live = live_rows(scalar_ref, rows)
    stats, sums = stats_ref[...], sums_ref[...]
    normal = (conv_ref[...] - stats[0:1]) * stats[1:2]
    share = live * stats[4:5, 0:1]
    grad_conv = stats[2:3] * stats[1:2] * (grad_ref[...] - share * (sums[0:1] + normal * sums[1:2]))
    set_padded(padded_ref, grad_conv)
    set_padded(padded_glu_ref, value_in[...] * gate_in[...] * live)
    middle = KERNEL // 2
    for j in range(KERNEL):
        term = padded_ref[EDGE : EDGE + rows] * moved(padded_glu_ref, j - middle)
        depth_out[j : j + 1] = jnp.sum(term, axis=0, keepdims=True)
    grad_glu = sum(moved(padded_ref, middle - j) * depth_ref[j : j + 1] for j in range(KERNEL))
    grad_glu = grad_glu * live
    value, gate = value_in[...], gate_in[...]
    grad_value = (grad_glu * gate).astype(BF16)
    grad_gate = (grad_glu * value * gate * (1.0 - gate)).astype(BF16)
    both_ref[:, :channels] = grad_value
    both_ref[:, channels:] = grad_gate
    value_weight = jnp.where(side == 0, value_ref[...], value_far_ref[...])
    gate_weight = jnp.where(side == 0, gate_ref[...], gate_far_ref[...])
    total = matmul_t(grad_value, value_weight) + matmul_t(grad_gate, gate_weight)

    @pl.when(side == 0)
    def _():
        total_ref[...] = total

    @pl.when(side == 1)
    def _():
        total_ref[...] += total
        half = rows // 2
        for at, ref in ((core, own_ref), (1 - core, other_ref)):
            ref[...] = total_ref[pl.ds(pl.multiple_of(at * half, half), half)].astype(BF16)


def mixer_back_call(scalars, grad, conv, value, gate, stats, sums, depth, weights):
    rows, both = grad.shape
    width, channels = weights[0].shape

    def kept(shape):
        return pl.BlockSpec(shape, lambda i: (0,) * len(shape))

    def side(height, size=channels):
        return pl.BlockSpec((height, size), lambda i: (0, i))

    return pl.pallas_call(
        mixer_back_kernel,
        grid=(2,),
        in_specs=[pl.BlockSpec(memory_space=pltpu.SMEM)]
        + [side(rows)] * 4
        + [side(stats.shape[0]), side(sums.shape[0]), side(depth.shape[0])]
        + [kept(w.shape) for w in weights],
        out_specs=[side(rows, 2 * channels), side(KERNEL)] + [kept((rows // 2, width))] * 2,
        out_shape=[
            jax.ShapeDtypeStruct((rows, 2 * both), BF16),
            jax.ShapeDtypeStruct((KERNEL, both), F32),
        ]
        + [jax.ShapeDtypeStruct((rows // 2, width), BF16)] * 2,
        scratch_shapes=[pltpu.VMEM((rows, width), F32)]
        + [pltpu.VMEM((rows + 2 * EDGE, channels), F32)] * 2,
        compiler_params=pltpu.CompilerParams(vmem_limit_bytes=40 << 20),
        cost_estimate=cost(8 * rows * width * channels, 8 * width * channels),
        name="mixer_back",
    )(scalars, *map(streamed, (grad, conv, value, gate)), stats, sums, depth, *map(streamed, weights))


def row_of(column):
    return jnp.broadcast_to(column, (column.shape[0], 128)).T[:1]


def column_of(row):
    return jnp.broadcast_to(row, (128, row.shape[1])).T[:, :1]


def head_kernel(first_ref, second_ref, weight_ref, logits_ref, stats_ref):
    step = pl.program_id(0)
    piece = jnp.where(step == 0, first_ref[...], second_ref[...])
    logits = matmul(piece, weight_ref[...])
    logits_ref[...] = logits
    top = jnp.max(logits, axis=1, keepdims=True)
    stats_ref[0:1] = row_of(top)
    stats_ref[1:2] = row_of(jnp.sum(jnp.exp(logits - top), axis=1, keepdims=True))


def head_call(pieces, weight):
    rows, width = pieces[0].shape
    vocab = weight.shape[1]
    piece = pl.BlockSpec((rows, width), lambda i: (0, 0))
    return pl.pallas_call(
        head_kernel,
        grid=(2,),
        in_specs=[piece, piece, pl.BlockSpec(weight.shape, lambda i: (0, 0))],
        out_specs=[
            pl.BlockSpec((rows, vocab), lambda i: (i, 0)),
            pl.BlockSpec((2, rows), lambda i: (0, i)),
        ],
        out_shape=[
            pltpu.HBM((2 * rows, vocab), F32),
            jax.ShapeDtypeStruct((2, 2 * rows), F32),
        ],
        compiler_params=pltpu.CompilerParams(vmem_limit_bytes=28 << 20),
        cost_estimate=cost(4 * rows * weight.size, 2 * weight.size),
        name="head",
    )(*pieces, weight)


def merged(first, second):
    top = jnp.maximum(first[0:1], second[0:1])
    total = first[1:2] * jnp.exp(first[0:1] - top) + second[1:2] * jnp.exp(second[0:1] - top)
    return (top, total)


def merge_kernel(own_ref, other_ref, out_ref):
    quarter = own_ref.shape[1] // 4
    other = other_ref[...]
    parts = [other[:, k * quarter : (k + 1) * quarter] for k in (1, 0, 3, 2)]
    top, total = merged(own_ref[...], jnp.concatenate(parts, axis=1))
    out_ref[0:1] = top
    out_ref[1:2] = total


def merge_call(own, other):
    return pl.pallas_call(
        merge_kernel, out_shape=jax.ShapeDtypeStruct(own.shape, F32), name="head_merge"
    )(own, other)


def head_back_kernel(
    logits_ref, own_ref, far_ref, codes_ref, weight_ref, grad_ref, first_ref, second_ref, loss_ref
):
    step = pl.program_id(0)
    top, total = merged(own_ref[...], far_ref[...])
    log_total = top + jnp.log(total)
    codes = codes_ref[...]
    logits = logits_ref[...]
    place = lax.broadcasted_iota(jnp.int32, logits.shape, 1)
    target = column_of(codes[0:1])
    hits = place == target.astype(jnp.int32)
    shares = jnp.exp(logits - column_of(log_total))
    grad = (column_of(codes[1:2]) * (shares - hits.astype(F32))).astype(BF16)
    grad_ref[...] = grad
    result = matmul_t(grad, weight_ref[...]).astype(BF16)
    picked = jnp.sum(jnp.where(hits, logits, 0.0), axis=1, keepdims=True)
    loss = jnp.sum(codes[2:3] * log_total, keepdims=True)
    loss = loss - jnp.sum(column_of(codes[1:2]) * picked, keepdims=True)
    loss = jnp.broadcast_to(loss, loss_ref.shape)

    @pl.when(step == 0)
    def _():
        first_ref[...] = result
        loss_ref[...] = loss

    @pl.when(step == 1)
    def _():
        second_ref[...] = result
        loss_ref[...] += loss


def head_back_call(logits, own, far, codes, weight):
    slots, vocab = logits.shape
    rows = slots // 2
    width = weight.shape[0]
    piece = pl.BlockSpec((rows, width), lambda i: (0, 0))
    stat = pl.BlockSpec((2, rows), lambda i: (0, i))
    return pl.pallas_call(
        head_back_kernel,
        grid=(2,),
        in_specs=[
            pl.BlockSpec((rows, vocab), lambda i: (i, 0)),
            stat,
            stat,
            pl.BlockSpec((3, rows), lambda i: (0, i)),
            pl.BlockSpec(weight.shape, lambda i: (0, 0)),
        ],
        out_specs=[
            pl.BlockSpec((rows, vocab), lambda i: (i, 0)),
            piece,
            piece,
            pl.BlockSpec((1, 128), lambda i: (0, 0)),
        ],
        out_shape=[
            jax.ShapeDtypeStruct((slots, vocab), BF16),
            jax.ShapeDtypeStruct((rows, width), BF16),
            jax.ShapeDtypeStruct((rows, width), BF16),
            jax.ShapeDtypeStruct((1, 128), F32),
        ],
        compiler_params=pltpu.CompilerParams(vmem_limit_bytes=32 << 20),
        cost_estimate=cost(2 * slots * weight.size, 2 * weight.size),
        name="head_back",
    )(streamed(logits), own, far, codes, weight)


def weights_kernel(number, *refs):
    out_ref = refs[-1]
    start = 0
    for k in range(number):
        left_ref, right_ref = refs[2 * k], refs[2 * k + 1]
        size = right_ref.shape[1]
        out_ref[:, start : start + size] = weight_term(left_ref[...], right_ref[...]).astype(BF16)
        start += size


def weights_turn_kernel(number, *refs):
    out_ref = refs[-1]
    for k in range(number):

        @pl.when(pl.program_id(0) == k)
        def _(left_ref=refs[2 * k], right_ref=refs[2 * k + 1]):
            out_ref[...] = weight_term(left_ref[...], right_ref[...]).astype(BF16)


def head_weights_kernel(*refs):
    lefts, rights, out_ref = refs[:4], refs[4:6], refs[6]
    total = None
    for k in range(2):
        left = jnp.concatenate([lefts[2 * k][...], lefts[2 * k + 1][...]], axis=0)
        part = weight_term(left, rights[k][...])
        total = part if total is None else total + part
    out_ref[...] = total.astype(BF16)


def head_weights_call(lefts, rights, total):
    width, size = lefts[0].shape[1], rights[0].shape[1]
    block = 256
    return pl.pallas_call(
        head_weights_kernel,
        grid=(width // block,),
        in_specs=[pl.BlockSpec((left.shape[0], block), lambda j: (0, j)) for left in lefts]
        + [pl.BlockSpec(right.shape, lambda j: (0, 0)) for right in rights],
        out_specs=pl.BlockSpec((block, size), lambda j: (j, 0)),
        out_shape=pltpu.HBM((width, total), BF16),
        compiler_params=pltpu.CompilerParams(vmem_limit_bytes=32 << 20),
        cost_estimate=cost(4 * rights[0].size * width, 2 * width * size),
        name="head_weights",
    )(*lefts, *rights)


def weights_call(lefts, rights, name, held=None):
    rows, width = lefts[0].shape
    number = len(lefts)
    total = sum(right.shape[1] for right in rights)
    block = 512
    steps = width // block
    turns = len({right.shape[1] for right in rights}) == 1
    operands, in_specs = [], []
    for k in range(number):
        left_rows, size = rights[k].shape
        if turns:
            place = lambda i, j, k=k: (0, jnp.clip((i - k) * steps + j, 0, steps - 1))
            whole = lambda i, j: (0, 0)
        else:
            place = lambda j: (0, j)
            whole = lambda j: (0, 0)
        in_specs.append(pl.BlockSpec((left_rows, block), place))
        in_specs.append(pl.BlockSpec((left_rows, size), whole))
        operands += [lefts[k], rights[k]]
    aliases = {}
    if held is not None:
        first = (held.shape[1] - total) // rights[0].shape[1]
        total = held.shape[1]
        aliases = {len(operands): 0}
        operands.append(held)
        in_specs.append(pl.BlockSpec(memory_space=pl.ANY))
    else:
        first = 0
    if turns:
        grid, kernel = (number, steps), weights_turn_kernel
        out_spec = pl.BlockSpec((block, rights[0].shape[1]), lambda i, j: (j, i + first))
    else:
        grid, kernel = (steps,), weights_kernel
        out_spec = pl.BlockSpec((block, total), lambda j: (j, 0))
    return pl.pallas_call(
        lambda *refs: kernel(number, *refs[: 2 * number], refs[-1]),
        grid=grid,
        in_specs=in_specs,
        out_specs=out_spec,
        out_shape=pltpu.HBM((width, total), BF16),
        input_output_aliases=aliases,
        compiler_params=pltpu.CompilerParams(vmem_limit_bytes=40 << 20),
        cost_estimate=cost(2 * rows * width * total, 2 * width * total),
        name=name,
    )(*operands)


def fetch_other(packed):
    place = lax.axis_index("dp") % 4
    rows = packed.shape[0] // 4
    piece = cross(lax.dynamic_slice_in_dim(packed, place * rows, rows))

    def over_x(values):
        return lax.ppermute(values, "dp", X_PAIRS)

    def over_z(values):
        return lax.ppermute(values, "dp", Z_NEAR_PAIRS)

    def rest():
        beside, above = over_x(piece), over_z(piece)
        return (beside, above, over_z(beside[: rows // 2]), over_x(above[rows // 2 :]))

    return (piece, rest)


def reduce_weights(grad):
    return lax.psum_scatter(grad, "dp", scatter_dimension=0, tiled=True)


def sum_steps(values):
    for axis, pairs in (
        ("mp", CORE_PAIRS),
        ("mp", CHIP_PAIRS),
        ("dp", X_PAIRS),
        ("dp", Z_NEAR_PAIRS),
        ("dp", Z_FAR_PAIRS),
    ):
        arrived = lax.ppermute(values, axis, pairs)
        earlier = yield arrived
        values = values + after(arrived, *earlier)
    yield values


def reduce_by_steps(grad):
    place = lax.axis_index("dp")
    size = grad.shape[0] // 8
    x, near, far = place % 2, (place // 2) % 2, place // 4
    steps = (
        ((4, 2, size, -1), 1, x, X_PAIRS),
        ((2, 2, size, -1), 1, near, Z_NEAR_PAIRS),
        ((2, size, -1), 0, far, Z_FAR_PAIRS),
    )
    for shape, axis, at, pairs in steps:
        parts = grad.reshape(shape)
        keep = lax.dynamic_index_in_dim(parts, at, axis, keepdims=False)
        send = lax.dynamic_index_in_dim(parts, 1 - at, axis, keepdims=False)
        arrived = lax.ppermute(send, "dp", pairs)
        earlier = yield arrived
        total = keep.astype(F32) + after(arrived, *earlier).astype(F32)
        grad = total.astype(BF16)
    yield total


def on_device_block(
    frames,
    out_cotangent,
    lengths,
    masked_rows,
    targets,
    head_device,
    first_gain,
    first_in,
    first_out,
    attend_gain,
    query_weight,
    key_weight,
    value_weight,
    attend_out,
    mixer_gain,
    mixer_value,
    mixer_gate,
    mixer_depth,
    batch_scale,
    batch_shift,
    mixer_out,
    second_gain,
    second_in,
    second_out,
    final_gain,
    head_weight,
):
    rows = frames.shape[0]
    own = lax.axis_index("mp")
    core, chip = own % 2, own // 2
    length = lax.dynamic_index_in_dim(lengths, chip, 0, keepdims=False)
    position = (jnp.arange(LEN) + core * rows) % LEN
    live = (position < length).astype(F32)
    live_column = live[:, None]
    place = position[:, None]

    scalars = jnp.stack([core, length]).astype(jnp.int32)
    attend_pack = jnp.concatenate([query_weight, key_weight, value_weight], axis=1)
    width = query_weight.shape[1]
    channels = jnp.concatenate([mixer_depth, batch_scale[None], batch_shift[None]], axis=0)
    own_live = live[:rows]
    picker = (masked_rows[:, None] == jnp.arange(rows)[None, :]).astype(BF16)
    keep = jnp.sum(picker.astype(F32) * own_live[None, :], axis=1)
    labels = (targets + 1) * (keep > 0).astype(jnp.int32)
    codes = on_chip(labels[None, :])

    fetched = []

    def fetch(done):
        fetched.append(fetch_other(attend_pack))
        fetched.append((cross(channels), cross(codes)))
        return [fetched[0][0], *fetched[1]]

    _, normed = norm_forward(frames, [], first_gain, 1.0)
    parts, first_kept = branch_forward(normed, first_in, first_out, 2, (lambda done: [], fetch))
    piece, rest = fetched[0]
    beside, above, *corner = rest()
    channels_other, codes_other = fetched[1]
    slots = masked_rows.shape[0]
    vocab = head_weight.shape[1]

    def slot_codes(codes, first):
        codes = codes.reshape(1, 2 * slots)
        counted = (codes > 0).astype(F32)
        here = counted * (jnp.arange(2 * slots)[None, :] < first).astype(F32)
        return jnp.concatenate([(codes - 1 - own * vocab).astype(F32), counted, here], axis=0)

    codes_near, codes_far = slot_codes(codes, slots), slot_codes(codes_other, 0)
    parts[0] = after(parts[0], beside, above, codes_near, codes_far)
    after_first, normed = norm_forward(frames, parts, attend_gain, 0.5)

    attend_out_other = cross(attend_out)
    mixer_others = [cross(weight) for weight in (mixer_value, mixer_gate)]
    mixer_out_other = cross(mixer_out)
    quarters = [piece, beside, above, jnp.concatenate(corner, axis=0)]
    place = jnp.stack([core, lax.axis_index("dp") % 4]).astype(jnp.int32)
    qkv_weights = [query_weight, key_weight, value_weight, *quarters]
    swapped = swap(normed)
    swapped = after(swapped, attend_out_other)
    qkv, attend_in = rows_call(
        qkv_body, "qkv", (normed, swapped), [], qkv_weights,
        [(6 * width, BF16), (D, None)], None, scalars=place, turned=False,
    )
    mixed, log_total = attend_forward_call(after(qkv, mixer_others[0]), live_column)
    attend_outs = [attend_out, attend_out_other]
    own_part, other_part = rows_call(
        out_body, "attend_out", None, [after(mixed, mixer_others[1])], attend_outs, [], D,
        scalars=place, turned=False,
    )
    parts = [own_part, swap(other_part)]
    after_attend, normed = norm_forward(after_first, parts, mixer_gain, 1.0)

    channels = jnp.concatenate([channels, channels_other], axis=1)
    depth, scale_both, shift_both = channels[:KERNEL], channels[KERNEL], channels[KERNEL + 1]
    mixer_weights = [mixer_value, mixer_gate, *mixer_others]
    mixer_outs = [mixer_out, mixer_out_other]
    swapped = swap(normed)
    mixer_in, value_in, gate, convolved, sums = mixer_front_call(
        scalars, normed, swapped, mixer_weights, depth
    )
    sums = sum_channels(sums, mixer_out_other)
    count = sums[2]
    bn_mean = sums[0] / count
    inverse = lax.rsqrt(sums[1] / count - bn_mean * bn_mean + NORM_EPSILON)
    stats = jnp.stack([bn_mean, inverse, scale_both, shift_both, 1.0 / count])
    mixer_active, own_part, other_part = rows_call(
        shape_body, "mixer_shape", None, [convolved], [stats, *mixer_outs],
        [(2 * width, None)], D, scalars=scalars,
    )
    parts = [own_part, swap(other_part)]
    after_mixer, normed = norm_forward(after_attend, parts, second_gain, 1.0)

    parts, second_kept = branch_forward(normed, second_in, second_out, 2)
    after_second, output_low, output = norm_forward(after_mixer, parts, final_gain, 0.5, True)

    chosen = dot(picker, output_low, BF16)
    vocab = head_weight.shape[1]
    far = cross(chosen)
    near_pieces = (chosen, swap(chosen))
    near_logits, near_stats = head_call(near_pieces, head_weight)
    far = after(far, near_stats)
    far_pieces = (far, swap(far))
    far_logits, far_stats = head_call(far_pieces, head_weight)
    stats_own = jnp.concatenate([near_stats, far_stats], axis=1)
    stats_own = merge_call(stats_own, swap(stats_own))
    stats_far = cross(stats_own)
    near, far = slice(0, 2 * slots), slice(2 * slots, 4 * slots)
    far_grad, *far_results, far_loss = head_back_call(
        far_logits, stats_own[:, far], stats_far[:, near], codes_far, head_weight
    )
    sent = on_chip_sum(*far_results).astype(BF16)
    crossed = cross(sent)
    near_grad, *near_results, near_loss = head_back_call(
        near_logits, stats_own[:, near], stats_far[:, far], codes_near, head_weight
    )
    own_loss = near_loss[0, 0] + far_loss[0, 0]
    grad_chosen = on_chip_sum(*near_results) + crossed.astype(F32)
    grad_second, grad_low, final_gain_grad = norm_backward(
        after_second, final_gain, [out_cotangent], None, 0.5, (picker.T, grad_chosen.astype(BF16))
    )

    grad_head = head_weights_call(
        [*far_pieces, *near_pieces], [after(far_grad, grad_low), near_grad], vocab
    )

    def second_weights(grads, active, normed, grad_inner):
        lefts, rights = [grads, normed], [active, grad_inner]
        return (
            weights_call(
                [streamed(left) for left in lefts], [streamed(right) for right in rights],
                "second_weights",
            ),
        )

    parts, _, (grad_second_both,) = branch_backward(
        second_in, second_out, second_kept, grad_low, 2, (lambda done: [grad_head], lambda done: []),
        second_weights,
    )
    grad_head = reduce_weights(grad_head)
    grad_mixer, grad_low, second_gain_grad = norm_backward(
        after_mixer, second_gain, parts, grad_second, 1.0
    )

    grad_shaped, grad_full, sums = rows_call(
        shape_back_body, "mixer_shape_back", (grad_low, swap(grad_low)), [streamed(convolved)],
        [stats, *mixer_outs], [(2 * width, F32), (D, None)], None, (2, 2 * width), scalars,
    )
    sums = sum_channels(sums)
    batch_shift_grad, batch_scale_grad = sums[0], sums[1]
    grad_second_both = reduce_weights(after(grad_second_both, grad_head, sums))
    grad_both, depth_grad, own_part, other_part = mixer_back_call(
        scalars, grad_shaped, convolved, value_in, gate, stats, sums, depth, mixer_weights
    )
    grad_attend, grad_low, mixer_gain_grad = norm_backward(
        after_attend, mixer_gain, [own_part, swap(other_part)], grad_mixer, 1.0
    )
    mixer_grads = weights_call(
        [streamed(mixer_in), streamed(grad_full)], [grad_both, streamed(mixer_active)], "mixer_weights"
    )
    counts = jnp.stack([own_loss, jnp.sum(keep)])
    counts = jnp.concatenate([counts, jnp.zeros((D - 2,), F32)])[None]
    depth_full = jnp.zeros((KERNEL, D), F32)
    for side, at in ((0, own), (1, (own + 2) % 4)):
        depth_full = lax.dynamic_update_slice_in_dim(
            depth_full, depth_grad[:, side * width : (side + 1) * width], at * width, 1
        )
    gains = jnp.concatenate(
        [mixer_gain_grad, second_gain_grad, final_gain_grad, counts, depth_full], axis=0
    )
    all_run = sum_steps(gains)
    next(all_run)
    all_run.send(())
    gain_crossed = all_run.send(())
    mixer_crossed = [
        cross(after(part, gain_crossed))
        for part in (mixer_grads[:, 2 * width : 4 * width], mixer_grads[:, 5 * width :])
    ]

    grad_mixed, grad_full = rows_call(
        out_back_body, "attend_out_back", (grad_low, swap(grad_low)), [], attend_outs,
        [(2 * width, BF16), (D, None)], None, scalars=place, turned=False,
    )
    grad_mixed = after(grad_mixed, mixer_grads, gain_crossed)
    grad_qkv = attend_backward_call(qkv, live_column, grad_mixed, log_total)
    own_part, other_part = rows_call(
        qkv_back_body, "qkv_back", None, [after(grad_qkv, mixer_crossed[0])], qkv_weights, [], D, scalars=place,
        turned=False,
    )
    grad_first, grad_low, attend_gain_grad = norm_backward(
        after_first, attend_gain, [own_part, swap(other_part)], grad_attend, 0.5
    )
    attend_grads = weights_call(
        [streamed(attend_in), streamed(grad_full)], [after(grad_qkv, grad_low), streamed(mixed)], "attend_weights"
    )

    def sides(first, second):
        return jnp.concatenate([first, second], axis=1)

    mixer_sum = sides(mixer_grads[:, : 2 * width], mixer_grads[:, 4 * width : 5 * width])
    mixer_crossed = sides(*after(mixer_crossed, attend_grads))
    mixer_sum = (mixer_sum.astype(F32) + mixer_crossed.astype(F32)).astype(BF16)
    middle = reduce_weights(after(sides(attend_grads, mixer_sum), grad_second_both))

    def first_weights(grads, active, normed, grad_inner):
        grad_out = dot_rows(grads, active)
        run_out = reduce_by_steps(grad_out)
        return (grad_out, run_out, next(run_out))

    parts, (grads, grad_inner, active, normed), (grad_out, run_out, _) = branch_backward(
        first_in, first_out, first_kept, grad_low, 2, (lambda done: [attend_grads], lambda done: []), first_weights
    )
    grad_in = dot_rows(normed, after(grad_inner, grad_out))
    run_in = reduce_by_steps(grad_in)
    next(run_in)
    all_run.send((grad_in,))
    input_grad, _, first_gain_grad = norm_backward(frames, first_gain, parts, grad_first, 1.0)
    gain_run = sum_steps(jnp.concatenate([attend_gain_grad, first_gain_grad], axis=0))
    next(gain_run)
    gain_run.send(())
    gain_run.send(())
    all_run.send((input_grad,))
    grad_head = after(grad_head, input_grad).astype(F32)
    grad_second_both = after(grad_second_both, input_grad).astype(F32)
    arrived = run_out.send((input_grad,))
    gains = all_run.send((arrived,))
    loss = gains[3, 0] / gains[3, 1]
    depth_grad = lax.dynamic_slice_in_dim(gains[4:], own * width, width, 1)
    arrived = run_in.send((arrived,))
    gain_run.send((arrived,))
    middle = after(middle, arrived).astype(F32)
    attend_grads, mixer_sum = middle[:, : 8 * width], middle[:, 8 * width :]
    crossed = cross(sides(attend_grads[:, 3 * width : 6 * width], attend_grads[:, 7 * width :]).astype(BF16))
    own_part = sides(attend_grads[:, : 3 * width], attend_grads[:, 6 * width : 7 * width])
    run_out.send((arrived,))
    arrived = run_in.send((own_part,))
    attend_grads = own_part + after(crossed, arrived).astype(F32)
    gain_run.send((arrived,))
    grad_first_out = run_out.send(())
    grad_first_in = run_in.send(())
    first_gain_grad = gain_run.send((grad_first_in,))
    grad_second_out, grad_second_in = jnp.split(grad_second_both, 2, axis=1)
    grad_query, grad_key, grad_value, grad_out = jnp.split(attend_grads, 4, axis=1)
    grad_mixer_value, grad_mixer_gate, grad_mixer_out = jnp.split(mixer_sum, 3, axis=1)
    return (
        output,
        loss,
        input_grad,
        first_gain_grad[1],
        grad_first_in,
        grad_first_out.T,
        first_gain_grad[0],
        grad_query,
        grad_key,
        grad_value,
        grad_out.T,
        gains[0],
        grad_mixer_value,
        grad_mixer_gate,
        depth_grad,
        batch_scale_grad[:width],
        batch_shift_grad[:width],
        grad_mixer_out.T,
        gains[1],
        grad_second_in,
        grad_second_out.T,
        gains[2],
        grad_head,
    )


def solution(mesh):
    in_specs = (
        P(("dp", "mp"), None),
        P(("dp", "mp"), None),
        P("dp"),
        P(("dp", "mp")),
        P(("dp", "mp")),
        P(("dp", "mp"), None),
        P(),
        P(None, "mp"),
        P("mp", None),
        P(),
        P(None, "mp"),
        P(None, "mp"),
        P(None, "mp"),
        P("mp", None),
        P(),
        P(None, "mp"),
        P(None, "mp"),
        P(None, "mp"),
        P("mp"),
        P("mp"),
        P("mp", None),
        P(),
        P(None, "mp"),
        P("mp", None),
        P(),
        P(None, "mp"),
    )
    out_specs = (
        P(("dp", "mp"), None),
        P(),
        P(("dp", "mp"), None),
        P(),
        P("dp", "mp"),
        P("mp", "dp"),
        P(),
        P("dp", "mp"),
        P("dp", "mp"),
        P("dp", "mp"),
        P("mp", "dp"),
        P(),
        P("dp", "mp"),
        P("dp", "mp"),
        P(None, "mp"),
        P("mp"),
        P("mp"),
        P("mp", "dp"),
        P(),
        P("dp", "mp"),
        P("mp", "dp"),
        P(),
        P("dp", "mp"),
    )
    small = mesh.shape["dp"] == 8 and mesh.shape["mp"] == 4
    on_device = on_device_block if small else on_device_any
    return jax.shard_map(
        on_device, mesh=mesh, in_specs=in_specs, out_specs=out_specs, check_vma=False
    )
```

```python
import jax
import jax.numpy as jnp
from jax import lax
from jax.experimental import pallas as pl
from jax.experimental.pallas import tpu as pltpu
from jax.sharding import PartitionSpec as P

D = 1024
HEAD_DIM = 128
KERNEL = 5
LEN = 1024
SEQ_DEV = 2
TOK_DEV = 2048


NORM_EPSILON = 1e-05
MASKED_SCORE = -1000000000.0


def joined(shard, axis, combine):
    everything = jax.tree.map(lambda part: lax.all_gather(part, axis), shard)
    leading = jax.tree.map(lambda part: part[0], everything)

    def hop(k, so_far):
        return combine(so_far, jax.tree.map(lambda part: part[k], everything))

    return lax.fori_loop(1, lax.axis_size(axis), hop, leading)


def layer_norm(values, gain):
    center = values - jnp.mean(values, axis=-1, keepdims=True)
    spread = jnp.mean(center * center, axis=-1, keepdims=True)
    return center * lax.rsqrt(spread + NORM_EPSILON) * gain


def swish(values):
    return values * jax.nn.sigmoid(values)


def swish_slope(values):
    sigma = jax.nn.sigmoid(values)
    return sigma * (1.0 + values * (1.0 - sigma))


def depth_conv(glu, depth):
    length = glu.shape[1]
    half = KERNEL // 2
    padded = jnp.pad(glu, ((0, 0), (half, half), (0, 0)))
    total = padded[:, 0:length] * depth[0]
    for offset in range(1, KERNEL):
        total = total + padded[:, offset : offset + length] * depth[offset]
    return total


def matmul(left, right):
    return jnp.dot(left, right, preferred_element_type=jnp.float32)


def matmul_t(left, right):
    return lax.dot_general(
        left, right, (((1,), (1,)), ((), ())), preferred_element_type=jnp.float32
    )


def weight_term(left, right):
    return lax.dot_general(
        left, right, (((0,), (0,)), ((), ())), preferred_element_type=jnp.float32
    )


def spread_rows(values):
    return lax.all_gather(values, "mp", axis=0, tiled=True)


def collect_rows(values):
    return lax.psum_scatter(values, "mp", scatter_dimension=0, tiled=True)


def spread_grads(values):
    return lax.all_gather(values, "mp", axis=0, tiled=True)


def collect_grads(values):
    return lax.psum_scatter(values, "mp", scatter_dimension=0, tiled=True)


def weight_grad(left, right):
    return weight_term(left, right)


def combine_parts(first, second):
    top = jnp.maximum(first[0], second[0])
    total = first[1] * jnp.exp(first[0] - top) + second[1] * jnp.exp(second[0] - top)
    return (top, total)


def feed_forward(resid, gain, expand, project):
    normed, norm_pullback = jax.vjp(layer_norm, resid, gain)
    gathered = spread_rows(normed.astype(jnp.bfloat16))
    inner = matmul(gathered, expand)
    active = swish(inner).astype(jnp.bfloat16)
    return (collect_rows(matmul(active, project)), (norm_pullback, gathered, inner, active))


def feed_backward(expand, project, kept, grad_branch):
    norm_pullback, gathered, inner, active = kept
    grad_full = spread_grads(grad_branch.astype(jnp.bfloat16))
    grad_inner = (matmul_t(grad_full, project) * swish_slope(inner)).astype(jnp.bfloat16)
    grad_project = weight_grad(grad_full, active)
    grad_expand = weight_grad(gathered, grad_inner)
    grad_resid, grad_gain = norm_pullback(collect_grads(matmul_t(grad_inner, expand)))
    return (grad_resid, grad_gain, grad_expand, grad_project)


def attend_forward(resid, gain, query_weight, key_weight, value_weight, attend_out, live):
    normed, norm_pullback = jax.vjp(layer_norm, resid, gain)
    gathered = spread_rows(normed.astype(jnp.bfloat16))
    width = query_weight.shape[1]
    shape = (SEQ_DEV, LEN, width // HEAD_DIM, HEAD_DIM)
    query = matmul(gathered, query_weight).astype(jnp.bfloat16).reshape(shape)
    keys = matmul(gathered, key_weight).astype(jnp.bfloat16).reshape(shape)
    values = matmul(gathered, value_weight).astype(jnp.bfloat16).reshape(shape)
    scale = HEAD_DIM ** (-0.5)

    def one_utterance(pack):
        query_part, keys_part, values_part, alive = pack
        scores = (
            jnp.einsum("qhe,khe->hqk", query_part, keys_part, preferred_element_type=jnp.float32)
            * scale
        )
        scores = jnp.where(alive[None, None, :] > 0, scores, MASKED_SCORE)
        top = jnp.max(scores, axis=-1, keepdims=True)
        lifted = jnp.exp(scores - top)
        total = jnp.sum(lifted, axis=-1, keepdims=True)
        shares = (lifted / total).astype(jnp.bfloat16)
        mixed_part = jnp.einsum(
            "hqk,khe->qhe", shares, values_part, preferred_element_type=jnp.float32
        )
        return (mixed_part.astype(jnp.bfloat16), (top + jnp.log(total))[:, :, 0])

    mixed, log_total = lax.map(one_utterance, (query, keys, values, live))
    mixed = mixed.reshape(TOK_DEV, width)
    branch = collect_rows(matmul(mixed, attend_out))
    return (branch, (norm_pullback, gathered, query, keys, values, mixed, log_total))


def attend_backward(query_weight, key_weight, value_weight, attend_out, live, kept, grad_branch):
    norm_pullback, gathered, query, keys, values, mixed, log_total = kept
    width = query_weight.shape[1]
    grad_full = spread_grads(grad_branch.astype(jnp.bfloat16))
    grad_mixed = matmul_t(grad_full, attend_out).astype(jnp.bfloat16).reshape(query.shape)
    grad_attend_out = weight_grad(grad_full, mixed)
    scale = HEAD_DIM ** (-0.5)

    def one_utterance(pack):
        query_part, keys_part, values_part, alive, log_part, grad_part = pack
        scores = (
            jnp.einsum("qhe,khe->hqk", query_part, keys_part, preferred_element_type=jnp.float32)
            * scale
        )
        scores = jnp.where(alive[None, None, :] > 0, scores, MASKED_SCORE)
        shares = jnp.exp(scores - log_part[:, :, None])
        grad_values = jnp.einsum(
            "hqk,qhe->khe",
            shares.astype(jnp.bfloat16),
            grad_part,
            preferred_element_type=jnp.float32,
        )
        grad_shares = jnp.einsum(
            "qhe,khe->hqk", grad_part, values_part, preferred_element_type=jnp.float32
        )
        inner = jnp.sum(shares * grad_shares, axis=-1, keepdims=True)
        grad_scores = (shares * (grad_shares - inner)).astype(jnp.bfloat16)
        grad_query = (
            jnp.einsum("hqk,khe->qhe", grad_scores, keys_part, preferred_element_type=jnp.float32)
            * scale
        )
        grad_keys = (
            jnp.einsum("hqk,qhe->khe", grad_scores, query_part, preferred_element_type=jnp.float32)
            * scale
        )
        return (
            grad_query.astype(jnp.bfloat16),
            grad_keys.astype(jnp.bfloat16),
            grad_values.astype(jnp.bfloat16),
        )

    grad_query, grad_keys, grad_values = lax.map(
        one_utterance, (query, keys, values, live, log_total, grad_mixed)
    )
    grad_query = grad_query.reshape(TOK_DEV, width)
    grad_keys = grad_keys.reshape(TOK_DEV, width)
    grad_values = grad_values.reshape(TOK_DEV, width)
    grad_query_weight = weight_grad(gathered, grad_query)
    grad_key_weight = weight_grad(gathered, grad_keys)
    grad_value_weight = weight_grad(gathered, grad_values)
    summed = (
        matmul_t(grad_query, query_weight)
        + matmul_t(grad_keys, key_weight)
        + matmul_t(grad_values, value_weight)
    )
    grad_resid, grad_gain = norm_pullback(collect_grads(summed))
    return (
        grad_resid,
        grad_gain,
        grad_query_weight,
        grad_key_weight,
        grad_value_weight,
        grad_attend_out,
    )


def mixer_forward(
    resid,
    gain,
    mixer_value,
    mixer_gate,
    mixer_depth,
    batch_scale,
    batch_shift,
    mixer_out,
    live_flat,
):
    normed, norm_pullback = jax.vjp(layer_norm, resid, gain)
    gathered = spread_rows(normed.astype(jnp.bfloat16))
    value_in = matmul(gathered, mixer_value)
    gate_in = matmul(gathered, mixer_gate)
    channels = value_in.shape[1]

    def front(value_part, gate_part, depth):
        glu = value_part * jax.nn.sigmoid(gate_part) * live_flat[:, None]
        return depth_conv(glu.reshape(SEQ_DEV, LEN, channels), depth).reshape(TOK_DEV, channels)

    convolved, front_pullback = jax.vjp(front, value_in, gate_in, mixer_depth)
    weighted = convolved * live_flat[:, None]
    count, first_sum, second_sum = lax.psum(
        (jnp.sum(live_flat), jnp.sum(weighted, axis=0), jnp.sum(weighted * convolved, axis=0)), "dp"
    )
    bn_mean = first_sum / count
    inverse = lax.rsqrt(second_sum / count - bn_mean * bn_mean + NORM_EPSILON)
    normal = (convolved - bn_mean) * inverse
    shaped = normal * batch_scale + batch_shift
    active = swish(shaped).astype(jnp.bfloat16)
    branch = collect_rows(matmul(active, mixer_out))
    return (
        branch,
        (norm_pullback, gathered, front_pullback, normal, inverse, count, shaped, active),
    )


def mixer_backward(mixer_value, mixer_gate, batch_scale, mixer_out, live_flat, kept, grad_branch):
    norm_pullback, gathered, front_pullback, normal, inverse, count, shaped, active = kept
    grad_full = spread_grads(grad_branch.astype(jnp.bfloat16))
    grad_mixer_out = weight_grad(grad_full, active)
    grad_shaped = matmul_t(grad_full, mixer_out) * swish_slope(shaped)
    shift_grad, scale_grad = lax.psum(
        (jnp.sum(grad_shaped, axis=0), jnp.sum(grad_shaped * normal, axis=0)), "dp"
    )
    grad_conv = (
        batch_scale
        * inverse
        * (grad_shaped - live_flat[:, None] / count * (shift_grad + normal * scale_grad))
    )
    grad_value, grad_gate, depth_grad = front_pullback(grad_conv)
    grad_value = grad_value.astype(jnp.bfloat16)
    grad_gate = grad_gate.astype(jnp.bfloat16)
    grad_mixer_value = weight_grad(gathered, grad_value)
    grad_mixer_gate = weight_grad(gathered, grad_gate)
    summed = matmul_t(grad_value, mixer_value) + matmul_t(grad_gate, mixer_gate)
    grad_resid, grad_gain = norm_pullback(collect_grads(summed))
    return (
        grad_resid,
        grad_gain,
        grad_mixer_value,
        grad_mixer_gate,
        depth_grad,
        scale_grad,
        shift_grad,
        grad_mixer_out,
    )


def masked_head(output, own_live, masked_rows, targets, head_device, head_weight):
    rows = output.shape[0]
    sources = lax.axis_size("dp")
    capacity = rows // sources
    keep = own_live[masked_rows]
    chosen = output[masked_rows].astype(jnp.bfloat16)
    destination = head_device[:, 0]
    marks = (destination[:, None] == jnp.arange(sources)[None, :]).astype(jnp.int32)
    order = jnp.sum((jnp.cumsum(marks, axis=0) - marks) * marks, axis=1)
    placer = (destination * capacity + order)[:, None] == jnp.arange(rows)[None, :]
    packed = weight_term(placer.astype(jnp.bfloat16), chosen).astype(jnp.bfloat16)
    labels = (targets + 1) * (keep > 0).astype(jnp.int32)
    codes = jnp.sum(jnp.where(placer, labels[:, None], 0), axis=0)
    arrived, arrived_codes = (
        lax.all_to_all(packed, "dp", split_axis=0, concat_axis=0, tiled=True),
        lax.all_to_all(codes, "dp", split_axis=0, concat_axis=0, tiled=True),
    )
    shared, shared_codes = (
        lax.all_gather(arrived, "mp", axis=0, tiled=True),
        lax.all_gather(arrived_codes, "mp", axis=0, tiled=True),
    )
    logits = matmul(shared, head_weight)
    vocab = head_weight.shape[1]
    hits = (shared_codes - 1 - lax.axis_index("mp") * vocab)[:, None] == jnp.arange(vocab)[None, :]
    top = jnp.max(logits, axis=1)
    total = jnp.sum(jnp.exp(logits - top[:, None]), axis=1)
    picked = jnp.sum(jnp.where(hits, logits, 0.0), axis=1)
    top_all, total_all = joined((top, total), "mp", combine_parts)
    log_total = top_all + jnp.log(total_all)
    counted = (shared_codes > 0).astype(jnp.float32)
    own_total = jnp.sum(
        lax.dynamic_slice_in_dim(counted * log_total, lax.axis_index("mp") * rows, rows)
    )
    own_loss = own_total - jnp.sum(counted * picked)
    grad_logits = (
        counted[:, None] * (jnp.exp(logits - log_total[:, None]) - hits.astype(jnp.float32))
    ).astype(jnp.bfloat16)
    grad_head = weight_grad(shared, grad_logits)
    grad_shared = lax.psum_scatter(
        matmul_t(grad_logits, head_weight), "mp", scatter_dimension=0, tiled=True
    )
    returned = lax.all_to_all(
        grad_shared.astype(jnp.bfloat16), "dp", split_axis=0, concat_axis=0, tiled=True
    )
    grad_chosen = matmul(placer.astype(jnp.bfloat16), returned).astype(jnp.bfloat16)
    picker = (masked_rows[:, None] == jnp.arange(rows)[None, :]).astype(jnp.bfloat16)
    grad_rows = weight_term(picker, grad_chosen)
    return (grad_rows, grad_head, own_loss, jnp.sum(keep))


def on_device_any(
    frames,
    out_cotangent,
    lengths,
    masked_rows,
    targets,
    head_device,
    first_gain,
    first_in,
    first_out,
    attend_gain,
    query_weight,
    key_weight,
    value_weight,
    attend_out,
    mixer_gain,
    mixer_value,
    mixer_gate,
    mixer_depth,
    batch_scale,
    batch_shift,
    mixer_out,
    second_gain,
    second_in,
    second_out,
    final_gain,
    head_weight,
):
    rows = frames.shape[0]
    live = (jnp.arange(LEN)[None, :] < lengths[:, None]).astype(jnp.float32)
    live_flat = live.reshape(TOK_DEV)
    own_live = lax.dynamic_slice_in_dim(live_flat, lax.axis_index("mp") * rows, rows)
    start = frames.astype(jnp.float32)
    branch, first_kept = feed_forward(start, first_gain, first_in, first_out)
    after_first = start + 0.5 * branch
    branch, attend_kept = attend_forward(
        after_first, attend_gain, query_weight, key_weight, value_weight, attend_out, live
    )
    after_attend = after_first + branch
    branch, mixer_kept = mixer_forward(
        after_attend,
        mixer_gain,
        mixer_value,
        mixer_gate,
        mixer_depth,
        batch_scale,
        batch_shift,
        mixer_out,
        live_flat,
    )
    after_mixer = after_attend + branch
    branch, second_kept = feed_forward(after_mixer, second_gain, second_in, second_out)
    after_second = after_mixer + 0.5 * branch
    output, final_pullback = jax.vjp(layer_norm, after_second, final_gain)
    grad_rows, grad_head, own_loss, own_count = masked_head(
        output, own_live, masked_rows, targets, head_device, head_weight
    )
    grad_second, final_gain_grad = final_pullback(out_cotangent.astype(jnp.float32) + grad_rows)
    back_resid, second_gain_grad, grad_second_in, grad_second_out = feed_backward(
        second_in, second_out, second_kept, 0.5 * grad_second
    )
    grad_mixer = grad_second + back_resid
    (
        back_resid,
        mixer_gain_grad,
        grad_mixer_value,
        grad_mixer_gate,
        depth_grad,
        batch_scale_grad,
        batch_shift_grad,
        grad_mixer_out,
    ) = mixer_backward(
        mixer_value, mixer_gate, batch_scale, mixer_out, live_flat, mixer_kept, grad_mixer
    )
    grad_attend = grad_mixer + back_resid
    back_resid, attend_gain_grad, grad_query, grad_key, grad_value, grad_attend_out = (
        attend_backward(
            query_weight, key_weight, value_weight, attend_out, live, attend_kept, grad_attend
        )
    )
    grad_first = grad_attend + back_resid
    back_resid, first_gain_grad, grad_first_in, grad_first_out = feed_backward(
        first_in, first_out, first_kept, 0.5 * grad_first
    )
    input_grad = grad_first + back_resid
    channels = mixer_value.shape[1]
    offset = lax.axis_index("mp") * channels
    depth_full = lax.dynamic_update_slice_in_dim(
        jnp.zeros((KERNEL, D), jnp.float32), depth_grad, offset, 1
    )
    (
        first_gain_grad,
        attend_gain_grad,
        mixer_gain_grad,
        second_gain_grad,
        final_gain_grad,
        depth_full,
        loss_sum,
        loss_count,
    ) = lax.psum(
        (
            first_gain_grad,
            attend_gain_grad,
            mixer_gain_grad,
            second_gain_grad,
            final_gain_grad,
            depth_full,
            own_loss,
            own_count,
        ),
        ("dp", "mp"),
    )
    mixer_depth_grad = lax.dynamic_slice_in_dim(depth_full, offset, channels, 1)
    loss = loss_sum / loss_count
    (
        grad_first_in,
        grad_first_out,
        grad_query,
        grad_key,
        grad_value,
        grad_attend_out,
        grad_mixer_value,
        grad_mixer_gate,
        grad_mixer_out,
        grad_second_in,
        grad_second_out,
        grad_head,
    ) = (
        lax.psum_scatter(grad_first_in, "dp", scatter_dimension=0, tiled=True),
        lax.psum_scatter(grad_first_out, "dp", scatter_dimension=0, tiled=True),
        lax.psum_scatter(grad_query, "dp", scatter_dimension=0, tiled=True),
        lax.psum_scatter(grad_key, "dp", scatter_dimension=0, tiled=True),
        lax.psum_scatter(grad_value, "dp", scatter_dimension=0, tiled=True),
        lax.psum_scatter(grad_attend_out, "dp", scatter_dimension=0, tiled=True),
        lax.psum_scatter(grad_mixer_value, "dp", scatter_dimension=0, tiled=True),
        lax.psum_scatter(grad_mixer_gate, "dp", scatter_dimension=0, tiled=True),
        lax.psum_scatter(grad_mixer_out, "dp", scatter_dimension=0, tiled=True),
        lax.psum_scatter(grad_second_in, "dp", scatter_dimension=0, tiled=True),
        lax.psum_scatter(grad_second_out, "dp", scatter_dimension=0, tiled=True),
        lax.psum_scatter(grad_head, "dp", scatter_dimension=0, tiled=True),
    )
    return (
        output,
        loss,
        input_grad,
        first_gain_grad,
        grad_first_in,
        grad_first_out.T,
        attend_gain_grad,
        grad_query,
        grad_key,
        grad_value,
        grad_attend_out.T,
        mixer_gain_grad,
        grad_mixer_value,
        grad_mixer_gate,
        mixer_depth_grad,
        batch_scale_grad,
        batch_shift_grad,
        grad_mixer_out.T,
        second_gain_grad,
        grad_second_in,
        grad_second_out.T,
        final_gain_grad,
        grad_head,
    )


BF16 = jnp.bfloat16
F32 = jnp.float32
SCALE = HEAD_DIM ** (-0.5)
CORE_PAIRS = [(0, 1), (1, 0), (2, 3), (3, 2)]
CHIP_PAIRS = [(0, 2), (2, 0), (1, 3), (3, 1)]
X_PAIRS = [(0, 1), (1, 0), (2, 3), (3, 2), (4, 5), (5, 4), (6, 7), (7, 6)]
Z_NEAR_PAIRS = [(0, 2), (2, 0), (1, 3), (3, 1), (4, 6), (6, 4), (5, 7), (7, 5)]
Z_FAR_PAIRS = [(0, 4), (4, 0), (1, 5), (5, 1), (2, 6), (6, 2), (3, 7), (7, 3)]


def swap(values):
    return lax.ppermute(values, "mp", CORE_PAIRS)


def cross(values):
    return lax.ppermute(values, "mp", CHIP_PAIRS)


def sum_over_dp(values):
    for pairs in (X_PAIRS, Z_NEAR_PAIRS, Z_FAR_PAIRS):
        values = values + lax.ppermute(values, "dp", pairs)
    return values


def sum_over_all(values):
    values = values + swap(values)
    values = values + cross(values)
    return sum_over_dp(values)


def sum_channels(values, *earlier):
    other = cross(values)
    half = values.shape[-1] // 2
    turned = jnp.concatenate([other[..., half:], other[..., :half]], axis=-1)
    return sum_over_dp(after(values + turned, *earlier))


def clamped(block, width, first, last):
    return pl.BlockSpec((block, width), lambda i: (jnp.clip(i, first, last) - first, 0))


def part_specs(parts, block):
    rows, width = parts[0].shape
    specs, at = [], 0
    for part in parts:
        if part.shape[0] == rows:
            specs.append(clamped(block, width, 0, rows // block - 1))
            continue
        steps = part.shape[0] // block
        specs.append(clamped(block, width, at, at + steps - 1))
        at += steps
    return specs


def part_total(refs, parts, block):
    rows = parts[0].shape[0]
    total, at = None, 0
    for ref, part in zip(refs, parts):
        value = ref[...].astype(F32)
        if part.shape[0] != rows:
            steps = part.shape[0] // block
            step = pl.program_id(0)
            value = jnp.where((step >= at) & (step < at + steps), value, 0.0)
            at += steps
        total = value if total is None else total + value
    return total


NORM_BLOCK = 256


def center_of(values):
    center = values - jnp.mean(values, axis=-1, keepdims=True)
    inverse = lax.rsqrt(jnp.mean(center * center, axis=-1, keepdims=True) + NORM_EPSILON)
    return (center * inverse, inverse)


def streamed(array):
    return pltpu.with_memory_space_constraint(array, pltpu.HBM)


def norm_forward(base, parts, gain, scale, exact=False):
    rows, width = base.shape
    block = NORM_BLOCK
    row = pl.BlockSpec((block, width), lambda i: (i, 0))
    number = len(parts)

    def kernel(base_ref, *refs):
        parts_refs, gain_ref, outs = refs[:number], refs[number], list(refs[number + 1 :])
        values = base_ref[...].astype(F32)
        if parts:
            values = values + scale * part_total(parts_refs, parts, block)
            outs.pop(0)[...] = values
        normed = center_of(values)[0] * gain_ref[...]
        outs.pop(0)[...] = normed.astype(BF16)
        if exact:
            outs.pop(0)[...] = normed

    kinds = ([F32] if parts else []) + [BF16] + ([F32] if exact else [])
    results = pl.pallas_call(
        kernel,
        grid=(rows // block,),
        in_specs=[row]
        + (part_specs(parts, block) if parts else [])
        + [pl.BlockSpec((1, width), lambda i: (0, 0))],
        out_specs=[row] * len(kinds),
        out_shape=[
            jax.ShapeDtypeStruct((rows, width), kind) if kind == BF16 else pltpu.HBM((rows, width), kind)
            for kind in kinds
        ],
        compiler_params=pltpu.CompilerParams(vmem_limit_bytes=24 << 20),
        cost_estimate=cost(10 * base.size, 8 * base.size),
        name="norm_forward",
    )(streamed(base), *parts, gain[None])
    return results if parts else [base, *results]


def norm_backward(values, gain, parts, grad, scale, pick=None):
    rows, width = values.shape
    block = NORM_BLOCK
    row = pl.BlockSpec((block, width), lambda i: (i, 0))
    number = len(parts)
    optional = list(pick) if pick is not None else []
    optional_specs = []
    if pick is not None:
        slots = pick[0].shape[1]
        optional_specs = [
            pl.BlockSpec((block, slots), lambda i: (i, 0)),
            pl.BlockSpec((slots, width), lambda i: (0, 0)),
        ]
    if grad is not None:
        optional.append(streamed(grad))
        optional_specs.append(row)

    def kernel(values_ref, gain_ref, *refs):
        parts_refs, refs = refs[:number], list(refs[number:])
        total = part_total(parts_refs, parts, block)
        if pick is not None:
            total = total + matmul(refs.pop(0)[...], refs.pop(0)[...])
        unit, inverse = center_of(values_ref[...].astype(F32))
        scaled = total * gain_ref[...]
        inner = jnp.mean(scaled * unit, axis=-1, keepdims=True)
        result = inverse * (scaled - jnp.mean(scaled, axis=-1, keepdims=True) - unit * inner)
        if grad is not None:
            result = result + refs.pop(0)[...]
        grad_ref, low_ref, gain_grad_ref = refs
        grad_ref[...] = result
        low_ref[...] = (scale * result).astype(BF16)
        gain_grad = jnp.sum(total * unit, axis=0, keepdims=True)

        @pl.when(pl.program_id(0) == 0)
        def _():
            gain_grad_ref[...] = gain_grad

        @pl.when(pl.program_id(0) > 0)
        def _():
            gain_grad_ref[...] += gain_grad

    one = pl.BlockSpec((1, width), lambda i: (0, 0))
    return pl.pallas_call(
        kernel,
        grid=(rows // block,),
        in_specs=[row, one] + part_specs(parts, block) + optional_specs,
        out_specs=[row, row, one],
        out_shape=[
            pltpu.HBM((rows, width), F32),
            jax.ShapeDtypeStruct((rows, width), BF16),
            jax.ShapeDtypeStruct((1, width), F32),
        ],
        compiler_params=pltpu.CompilerParams(vmem_limit_bytes=24 << 20),
        cost_estimate=cost(20 * values.size, 12 * values.size),
        name="norm_backward",
    )(streamed(values), gain[None], *parts, *optional)


def on_chip(values):
    return jnp.concatenate([values, swap(values)], axis=0)


def on_chip_sum(own, other):
    return own.astype(F32) + swap(other).astype(F32)


def dot(left, right, kind=F32):
    return jnp.dot(left, right, preferred_element_type=F32).astype(kind)


def dot_t(left, right, kind=F32):
    return matmul_t(left, right).astype(kind)


def dot_rows(lefts, rights):
    total = weight_term(lefts, rights)
    return total.astype(BF16)


def after(values, *earlier):
    return lax.optimization_barrier((values, *earlier))[0]


def early(flops, size):
    return pl.CostEstimate(flops=flops // 1000, bytes_accessed=size // 1000, transcendentals=0)


def cost(flops, size):
    return pl.CostEstimate(flops=flops, bytes_accessed=size, transcendentals=0)


BLOCK = 256


def pieces_call(body, pieces, row_inputs, weights, row_outputs, held, start, total, name):
    rows, width = pieces[0].shape
    block = min(BLOCK, rows)
    half, first = rows // block, start // block
    steps = 2 * half

    def kernel(*refs):
        refs = list(refs)
        inputs, refs = refs[: 2 + len(row_inputs) + len(weights)], refs[2 + len(row_inputs) + len(weights) :]
        if held is not None:
            refs = refs[len(held) :]
        step = pl.program_id(0)
        piece = jnp.where(step < half, inputs[0][...], inputs[1][...])
        result = body(piece, inputs[2:], refs[: len(row_outputs)])

        @pl.when(step < half)
        def _():
            refs[-2][...] = result

        @pl.when(step >= half)
        def _():
            refs[-1][...] = result

    def kept(array):
        return pl.BlockSpec(array.shape, lambda i: (0,) * array.ndim)

    def placed(size):
        return pl.BlockSpec((block, size), lambda i: (i + first, 0))

    two = [
        pl.BlockSpec((block, width), lambda i: (jnp.minimum(i, half - 1), 0)),
        pl.BlockSpec((block, width), lambda i: (jnp.maximum(i - half, 0), 0)),
    ]
    row_inputs = [pltpu.with_memory_space_constraint(array, pltpu.HBM) for array in row_inputs]
    operands = [*pieces, *row_inputs, *weights]
    in_specs = two + [placed(array.shape[1]) for array in row_inputs] + [kept(w) for w in weights]
    aliases = {}
    if held is not None:
        aliases = {len(operands) + k: k for k in range(len(held))}
        operands += held
        in_specs += [pl.BlockSpec(memory_space=pl.ANY)] * len(held)
    flops = 2 * 2 * rows * sum(w.size for w in weights if w.ndim == 2 and w.shape[0] > 1)
    return pl.pallas_call(
        kernel,
        grid=(steps,),
        in_specs=in_specs,
        out_specs=[placed(size) for size in row_outputs] + two,
        out_shape=[pltpu.HBM((total, size), BF16) for size in row_outputs]
        + [jax.ShapeDtypeStruct((rows, width), BF16)] * 2,
        input_output_aliases=aliases,
        compiler_params=pltpu.CompilerParams(vmem_limit_bytes=32 << 20),
        cost_estimate=early(flops, 2 * sum(w.size for w in weights)),
        name=name,
    )(*operands)


def expand_body(piece, inputs, outputs):
    expand_ref, project_ref = inputs
    held_ref, inner_ref, active_ref = outputs
    inner = matmul(piece, expand_ref[...])
    active = swish(inner).astype(BF16)
    held_ref[...] = piece
    inner_ref[...] = inner.astype(BF16)
    active_ref[...] = active
    return matmul(active, project_ref[...]).astype(BF16)


def expand_back_body(piece, inputs, outputs):
    inner_ref, expand_ref, project_ref = inputs
    held_ref, grad_ref = outputs
    slope = swish_slope(inner_ref[...].astype(F32))
    grad = (matmul_t(piece, project_ref[...]) * slope).astype(BF16)
    held_ref[...] = piece
    grad_ref[...] = grad
    return matmul_t(grad, expand_ref[...]).astype(BF16)


def swap_halves(values):
    half = values.shape[0] // 2
    return jnp.concatenate([swap(values[:half]), swap(values[half:])], axis=0)


def branch_over(values, number, call, beside=None, last=None):
    rows = values.shape[0]
    step = rows // number
    far = [cross(values[k * step : (k + 1) * step]) for k in range(number)]
    held, (own, other) = call((values, swap(values)), None, 0)
    near = [own, swap(other)]
    done, back = own, []
    for k in range(number):
        part = after(far[k], done)
        other = swap_halves(part)
        if beside is not None:
            other = after(other, *beside[k](done))
        held, (own, other) = call((part, other), held, 2 * rows + 2 * step * k)
        result = (own.astype(F32) + swap_halves(other).astype(F32)).astype(BF16)
        result = after(result, *back)
        back.append(cross(result))
        done = own
    extra = None
    if last is not None:
        extra = last(held, result)
        back[-1] = after(back[-1], extra[0])
    return (near + back, held, extra)


def branch_forward(normed, expand, project, number, beside=None):
    total = 4 * normed.shape[0]
    sizes = [normed.shape[1], expand.shape[1], expand.shape[1]]

    def call(pieces, held, start):
        *held, own, other = pieces_call(
            expand_body, pieces, [], [expand, project], sizes, held, start, total, "branch_forward"
        )
        return (held, (own, other))

    parts, held, _ = branch_over(normed, number, call, beside)
    return (parts, held)


def branch_backward(expand, project, kept, grad_branch, number, beside, last):
    normed, inner, active = kept
    total = 4 * grad_branch.shape[0]
    sizes = [grad_branch.shape[1], expand.shape[1]]

    def call(pieces, held, start):
        *held, own, other = pieces_call(
            expand_back_body, pieces, [inner], [expand, project], sizes, held, start, total,
            "branch_backward",
        )
        return (held, (own, other))

    def weights(held, sent):
        grads, grad_inner = held
        return last(after(grads, sent), active, normed, grad_inner)

    parts, held, extra = branch_over(grad_branch, number, call, beside, weights)
    return (parts, (*held, active, normed), extra)


def attend_kernel(live_ref, query_ref, keys_ref, values_ref, mixed_ref, total_ref):
    scores = matmul_t(keys_ref[...], query_ref[...]) * SCALE
    scores = jnp.where(live_ref[...] > 0, scores, MASKED_SCORE)
    top = jnp.max(scores, axis=0, keepdims=True)
    lifted = jnp.exp(scores - top)
    total = jnp.sum(lifted, axis=0, keepdims=True)
    mixed = weight_term(values_ref[...], lifted.astype(BF16)) * (1.0 / total)
    mixed_ref[...] = mixed.T.astype(BF16)
    total_ref[0] = top + jnp.log(total)


def head_column(head, kind):
    return (head // 2) * 6 + kind * 2 + head % 2


def attend_forward_call(qkv, live_column):
    length = qkv.shape[0]
    heads = qkv.shape[1] // (3 * HEAD_DIM)
    block = length

    def whole(kind):
        return pl.BlockSpec((length, HEAD_DIM), lambda h, b: (0, head_column(h, kind)))

    return pl.pallas_call(
        attend_kernel,
        grid=(heads, length // block),
        in_specs=[
            pl.BlockSpec((length, 1), lambda h, b: (0, 0)),
            pl.BlockSpec((block, HEAD_DIM), lambda h, b: (b, head_column(h, 0))),
            whole(1),
            whole(2),
        ],
        out_specs=[
            pl.BlockSpec((block, HEAD_DIM), lambda h, b: (b, h)),
            pl.BlockSpec((1, 1, block), lambda h, b: (h, 0, b)),
        ],
        out_shape=[
            jax.ShapeDtypeStruct((length, heads * HEAD_DIM), BF16),
            jax.ShapeDtypeStruct((heads, 1, length), F32),
        ],
        compiler_params=pltpu.CompilerParams(vmem_limit_bytes=32 << 20),
        cost_estimate=cost(4 * heads * length * length * HEAD_DIM, 8 * qkv.size),
        name="attend_forward",
    )(live_column, qkv, qkv, qkv)


def attend_back_kernel(
    live_ref, query_ref, keys_ref, values_ref, grad_ref, total_ref, out_ref, keys_sum, values_sum
):
    head, block = pl.program_id(0), pl.program_id(1)
    rows = query_ref.shape[0]
    query, keys, grad = query_ref[...], keys_ref[...], grad_ref[...]
    scores = matmul_t(keys, query) * SCALE
    scores = jnp.where(live_ref[...] > 0, scores, MASKED_SCORE)
    shares = jnp.exp(scores - total_ref[0])
    grad_shares = matmul_t(values_ref[...], grad)
    inner = jnp.sum(shares * grad_shares, axis=0, keepdims=True)
    grad_scores = (shares * (grad_shares - inner)).astype(BF16)
    grad_values = dot(shares.astype(BF16), grad)
    grad_keys = dot(grad_scores, query) * SCALE
    grad_query = (weight_term(keys, grad_scores) * SCALE).T.astype(BF16)

    def columns(kind):
        start = head_column(head, kind) * HEAD_DIM
        return pl.ds(pl.multiple_of(start, HEAD_DIM), HEAD_DIM)

    out_ref[pl.ds(pl.multiple_of(block * rows, rows), rows), columns(0)] = grad_query

    @pl.when(block == 0)
    def _():
        keys_sum[...] = grad_keys
        values_sum[...] = grad_values

    @pl.when(block > 0)
    def _():
        keys_sum[...] += grad_keys
        values_sum[...] += grad_values

    @pl.when(block == pl.num_programs(1) - 1)
    def _():
        out_ref[:, columns(1)] = keys_sum[...].astype(BF16)
        out_ref[:, columns(2)] = values_sum[...].astype(BF16)


def attend_backward_call(qkv, live_column, grad_mixed, log_total):
    length = qkv.shape[0]
    heads = qkv.shape[1] // (3 * HEAD_DIM)
    block = length

    def whole(kind):
        return pl.BlockSpec((length, HEAD_DIM), lambda h, b: (0, head_column(h, kind)))

    return pl.pallas_call(
        attend_back_kernel,
        grid=(heads, length // block),
        in_specs=[
            pl.BlockSpec((length, 1), lambda h, b: (0, 0)),
            pl.BlockSpec((block, HEAD_DIM), lambda h, b: (b, head_column(h, 0))),
            whole(1),
            whole(2),
            pl.BlockSpec((block, HEAD_DIM), lambda h, b: (b, h)),
            pl.BlockSpec((1, 1, block), lambda h, b: (h, 0, b)),
        ],
        out_specs=pl.BlockSpec(qkv.shape, lambda h, b: (0, 0)),
        out_shape=jax.ShapeDtypeStruct(qkv.shape, BF16),
        scratch_shapes=[pltpu.VMEM((length, HEAD_DIM), F32), pltpu.VMEM((length, HEAD_DIM), F32)],
        compiler_params=pltpu.CompilerParams(vmem_limit_bytes=44 << 20),
        cost_estimate=cost(10 * heads * length * length * HEAD_DIM, 8 * qkv.size),
        name="attend_backward",
    )(live_column, qkv, qkv, qkv, grad_mixed, log_total)


def rows_call(
    body, name, pieces, row_inputs, weights, row_outputs, result, sums=None, scalars=None, turned=True
):
    rows = 2 * pieces[0].shape[0] if pieces is not None else row_inputs[0].shape[0]
    block = BLOCK
    half = rows // 2 // block
    steps = 2 * half
    number, stay = len(row_inputs), len(weights)

    def kernel(scalar_ref, *refs):
        refs = list(refs)
        step = pl.program_id(0)
        piece = None
        if pieces is not None:
            piece = jnp.where(step < half, refs[0][...], refs[1][...])
            refs = refs[2:]
        inputs, refs = refs[:number], refs[number:]
        held, refs = refs[:stay], refs[stay:]
        outputs, refs = refs[: len(row_outputs)], refs[len(row_outputs) :]
        sums_ref = refs[-1] if sums is not None else None
        if sums is not None:

            @pl.when(step == 0)
            def _():
                sums_ref[...] = jnp.zeros_like(sums_ref)

        value = body(scalar_ref, piece, inputs, held, outputs, sums_ref)
        if result is not None:

            @pl.when(step < half)
            def _():
                refs[0][...] = value

            @pl.when(step >= half)
            def _():
                refs[1][...] = value

    def row(width):
        if turned:
            return pl.BlockSpec((block, width), lambda i, at: ((i + at[0] * half) % steps, 0))
        return pl.BlockSpec((block, width), lambda i, at: (i, 0))

    def two(width):
        return [
            pl.BlockSpec((block, width), lambda i, at: (jnp.minimum(i, half - 1), 0)),
            pl.BlockSpec((block, width), lambda i, at: (jnp.maximum(i, half) - half, 0)),
        ]

    def kept(shape):
        return pl.BlockSpec(shape, lambda i, at: (0,) * len(shape))

    in_specs, operands = [], [scalars]
    if pieces is not None:
        in_specs += two(pieces[0].shape[1])
        operands += pieces
    in_specs += [row(array.shape[1]) for array in row_inputs] + [kept(w.shape) for w in weights]
    operands += [*row_inputs, *(streamed(w) if w.shape[0] >= BLOCK else w for w in weights)]
    out_specs = [row(width) for width, _ in row_outputs]
    out_shape = [
        pltpu.HBM((rows, width), BF16) if kind is None else jax.ShapeDtypeStruct((rows, width), kind)
        for width, kind in row_outputs
    ]
    if result is not None:
        out_specs += two(result)
        out_shape += [jax.ShapeDtypeStruct((rows // 2, result), BF16)] * 2
    if sums is not None:
        out_specs.append(kept(sums))
        out_shape.append(jax.ShapeDtypeStruct(sums, F32))
    return pl.pallas_call(
        kernel,
        grid_spec=pltpu.PrefetchScalarGridSpec(
            num_scalar_prefetch=1, grid=(steps,), in_specs=in_specs, out_specs=out_specs
        ),
        out_shape=out_shape,
        compiler_params=pltpu.CompilerParams(vmem_limit_bytes=28 << 20),
        cost_estimate=cost(2 * rows * sum(w.size for w in weights), 2 * sum(w.size for w in weights)),
        name=name,
    )(*operands)


def quarter(scalar_ref, k):
    rows = D // 4
    at = scalar_ref[1] ^ k
    return pl.ds(pl.multiple_of(at * rows, rows), rows)


def qkv_body(scalar_ref, piece, inputs, held, outputs, sums_ref):
    out_ref, held_ref = outputs
    width = held[0].shape[1]
    held_ref[...] = piece
    for k in range(3):
        out_ref[:, k * width : (k + 1) * width] = matmul(piece, held[k][...]).astype(BF16)
    total = None
    for k in range(4):
        part = matmul(held_ref[:, quarter(scalar_ref, k)], held[3 + k][...])
        total = part if total is None else total + part
    out_ref[:, 3 * width :] = total.astype(BF16)


def qkv_back_body(scalar_ref, piece, inputs, held, outputs, sums_ref):
    width = held[0].shape[1]
    grad_ref = inputs[0]
    own = None
    for k in range(3):
        part = matmul_t(grad_ref[:, k * width : (k + 1) * width], held[k][...])
        own = part if own is None else own + part
    far = [matmul_t(grad_ref[:, 3 * width :], held[3 + k][...]) for k in range(4)]
    at = scalar_ref[1]
    near = [jnp.where(at % 2 == 0, far[k], far[k ^ 1]) for k in range(4)]
    placed = [jnp.where(at // 2 == 0, near[k], near[k ^ 2]) for k in range(4)]
    return (own + jnp.concatenate(placed, axis=1)).astype(BF16)


def out_body(scalar_ref, piece, inputs, held, outputs, sums_ref):
    width = held[0].shape[0]
    values = inputs[0][...]
    total = matmul(values[:, :width], held[0][...]) + matmul(values[:, width:], held[1][...])
    return total.astype(BF16)


def out_back_body(scalar_ref, piece, inputs, held, outputs, sums_ref):
    width = held[0].shape[0]
    outputs[0][:, :width] = matmul_t(piece, held[0][...]).astype(BF16)
    outputs[0][:, width:] = matmul_t(piece, held[1][...]).astype(BF16)
    outputs[1][...] = piece


def shape_body(scalar_ref, piece, inputs, held, outputs, sums_ref):
    stats_ref, *weights = held
    stats = stats_ref[...]
    normal = (inputs[0][...] - stats[0:1]) * stats[1:2]
    shaped = normal * stats[2:3] + stats[3:4]
    active = swish(shaped).astype(BF16)
    outputs[0][...] = active
    width = weights[0].shape[0]
    total = matmul(active[:, :width], weights[0][...]) + matmul(active[:, width:], weights[1][...])
    return total.astype(BF16)


def shape_back_body(scalar_ref, piece, inputs, held, outputs, sums_ref):
    stats_ref, *weights = held
    stats = stats_ref[...]
    width = weights[0].shape[0]
    outputs[1][...] = piece
    for side in range(2):
        columns = slice(side * width, (side + 1) * width)
        normal = (inputs[0][:, columns] - stats[0:1, columns]) * stats[1:2, columns]
        shaped = normal * stats[2:3, columns] + stats[3:4, columns]
        grad = matmul_t(piece, weights[side][...]) * swish_slope(shaped)
        outputs[0][:, columns] = grad
        sums_ref[0:1, columns] += jnp.sum(grad, axis=0, keepdims=True)
        sums_ref[1:2, columns] += jnp.sum(grad * normal, axis=0, keepdims=True)


EDGE = 8


def set_padded(padded_ref, values):
    rows = values.shape[0]
    zeros = jnp.zeros((EDGE, values.shape[1]), F32)
    padded_ref[:EDGE] = zeros
    padded_ref[EDGE + rows :] = zeros
    padded_ref[EDGE : EDGE + rows] = values


def moved(padded_ref, offset):
    rows = padded_ref.shape[0] - 2 * EDGE
    return padded_ref[EDGE + offset : EDGE + offset + rows]


def live_rows(scalar_ref, rows):
    return (lax.broadcasted_iota(jnp.int32, (rows, 1), 0) < scalar_ref[1]).astype(F32)


def mixer_front_kernel(
    scalar_ref, own_ref, other_ref, value_ref, gate_ref, value_far_ref, gate_far_ref, depth_ref,
    held_ref, value_out, gate_out, conv_out, sums_ref, padded_ref,
):
    side = pl.program_id(0)
    half = own_ref.shape[0]
    rows = 2 * half
    core = scalar_ref[0]
    value_weight = jnp.where(side == 0, value_ref[...], value_far_ref[...])
    gate_weight = jnp.where(side == 0, gate_ref[...], gate_far_ref[...])
    for at, ref in ((core, own_ref), (1 - core, other_ref)):
        piece = ref[...]
        place = pl.ds(pl.multiple_of(at * half, half), half)
        value_out[place] = matmul(piece, value_weight)
        gate_out[place] = jax.nn.sigmoid(matmul(piece, gate_weight))
        held_ref[place] = piece
    live = live_rows(scalar_ref, rows)
    set_padded(padded_ref, value_out[...] * gate_out[...] * live)
    middle = KERNEL // 2
    conv = sum(moved(padded_ref, j - middle) * depth_ref[j : j + 1] for j in range(KERNEL))
    conv_out[...] = conv
    weighted = conv * live
    sums_ref[0:1] = jnp.sum(weighted, axis=0, keepdims=True)
    sums_ref[1:2] = jnp.sum(weighted * conv, axis=0, keepdims=True)
    sums_ref[2:3] = jnp.broadcast_to(jnp.sum(live, axis=0, keepdims=True), (1, weighted.shape[1]))


def mixer_front_call(scalars, own, other, weights, depth):
    half, width = own.shape
    rows, channels = 2 * half, weights[0].shape[1]

    def kept(shape):
        return pl.BlockSpec(shape, lambda i: (0,) * len(shape))

    def side(height):
        return pl.BlockSpec((height, channels), lambda i: (0, i))

    return pl.pallas_call(
        mixer_front_kernel,
        grid=(2,),
        in_specs=[pl.BlockSpec(memory_space=pltpu.SMEM), kept(own.shape), kept(other.shape)]
        + [kept(w.shape) for w in weights]
        + [side(depth.shape[0])],
        out_specs=[kept((rows, width)), side(rows), side(rows), side(rows), side(3)],
        out_shape=[pltpu.HBM((rows, width), BF16)]
        + [pltpu.HBM((rows, 2 * channels), F32)] * 2
        + [jax.ShapeDtypeStruct((rows, 2 * channels), F32)]
        + [jax.ShapeDtypeStruct((3, 2 * channels), F32)],
        scratch_shapes=[pltpu.VMEM((rows + 2 * EDGE, channels), F32)],
        compiler_params=pltpu.CompilerParams(vmem_limit_bytes=36 << 20),
        cost_estimate=cost(8 * rows * width * channels, 8 * width * channels),
        name="mixer_front",
    )(scalars, own, other, *map(streamed, weights), depth)


def mixer_back_kernel(
    scalar_ref, grad_ref, conv_ref, value_in, gate_in, stats_ref, sums_ref, depth_ref,
    value_ref, gate_ref, value_far_ref, gate_far_ref,
    both_ref, depth_out, own_ref, other_ref, total_ref, padded_ref, padded_glu_ref,
):
    side = pl.program_id(0)
    rows, channels = grad_ref.shape
    core = scalar_ref[0]
    live = live_rows(scalar_ref, rows)
    stats, sums = stats_ref[...], sums_ref[...]
    normal = (conv_ref[...] - stats[0:1]) * stats[1:2]
    share = live * stats[4:5, 0:1]
    grad_conv = stats[2:3] * stats[1:2] * (grad_ref[...] - share * (sums[0:1] + normal * sums[1:2]))
    set_padded(padded_ref, grad_conv)
    set_padded(padded_glu_ref, value_in[...] * gate_in[...] * live)
    middle = KERNEL // 2
    for j in range(KERNEL):
        term = padded_ref[EDGE : EDGE + rows] * moved(padded_glu_ref, j - middle)
        depth_out[j : j + 1] = jnp.sum(term, axis=0, keepdims=True)
    grad_glu = sum(moved(padded_ref, middle - j) * depth_ref[j : j + 1] for j in range(KERNEL))
    grad_glu = grad_glu * live
    value, gate = value_in[...], gate_in[...]
    grad_value = (grad_glu * gate).astype(BF16)
    grad_gate = (grad_glu * value * gate * (1.0 - gate)).astype(BF16)
    both_ref[:, :channels] = grad_value
    both_ref[:, channels:] = grad_gate
    value_weight = jnp.where(side == 0, value_ref[...], value_far_ref[...])
    gate_weight = jnp.where(side == 0, gate_ref[...], gate_far_ref[...])
    total = matmul_t(grad_value, value_weight) + matmul_t(grad_gate, gate_weight)

    @pl.when(side == 0)
    def _():
        total_ref[...] = total

    @pl.when(side == 1)
    def _():
        total_ref[...] += total
        half = rows // 2
        for at, ref in ((core, own_ref), (1 - core, other_ref)):
            ref[...] = total_ref[pl.ds(pl.multiple_of(at * half, half), half)].astype(BF16)


def mixer_back_call(scalars, grad, conv, value, gate, stats, sums, depth, weights):
    rows, both = grad.shape
    width, channels = weights[0].shape

    def kept(shape):
        return pl.BlockSpec(shape, lambda i: (0,) * len(shape))

    def side(height, size=channels):
        return pl.BlockSpec((height, size), lambda i: (0, i))

    return pl.pallas_call(
        mixer_back_kernel,
        grid=(2,),
        in_specs=[pl.BlockSpec(memory_space=pltpu.SMEM)]
        + [side(rows)] * 4
        + [side(stats.shape[0]), side(sums.shape[0]), side(depth.shape[0])]
        + [kept(w.shape) for w in weights],
        out_specs=[side(rows, 2 * channels), side(KERNEL)] + [kept((rows // 2, width))] * 2,
        out_shape=[
            jax.ShapeDtypeStruct((rows, 2 * both), BF16),
            jax.ShapeDtypeStruct((KERNEL, both), F32),
        ]
        + [jax.ShapeDtypeStruct((rows // 2, width), BF16)] * 2,
        scratch_shapes=[pltpu.VMEM((rows, width), F32)]
        + [pltpu.VMEM((rows + 2 * EDGE, channels), F32)] * 2,
        compiler_params=pltpu.CompilerParams(vmem_limit_bytes=40 << 20),
        cost_estimate=cost(8 * rows * width * channels, 8 * width * channels),
        name="mixer_back",
    )(scalars, *map(streamed, (grad, conv, value, gate)), stats, sums, depth, *map(streamed, weights))


def row_of(column):
    return jnp.broadcast_to(column, (column.shape[0], 128)).T[:1]


def column_of(row):
    return jnp.broadcast_to(row, (128, row.shape[1])).T[:, :1]


def head_kernel(first_ref, second_ref, weight_ref, logits_ref, stats_ref):
    step = pl.program_id(0)
    piece = jnp.where(step == 0, first_ref[...], second_ref[...])
    logits = matmul(piece, weight_ref[...])
    logits_ref[...] = logits
    top = jnp.max(logits, axis=1, keepdims=True)
    stats_ref[0:1] = row_of(top)
    stats_ref[1:2] = row_of(jnp.sum(jnp.exp(logits - top), axis=1, keepdims=True))


def head_call(pieces, weight):
    rows, width = pieces[0].shape
    vocab = weight.shape[1]
    piece = pl.BlockSpec((rows, width), lambda i: (0, 0))
    return pl.pallas_call(
        head_kernel,
        grid=(2,),
        in_specs=[piece, piece, pl.BlockSpec(weight.shape, lambda i: (0, 0))],
        out_specs=[
            pl.BlockSpec((rows, vocab), lambda i: (i, 0)),
            pl.BlockSpec((2, rows), lambda i: (0, i)),
        ],
        out_shape=[
            pltpu.HBM((2 * rows, vocab), F32),
            jax.ShapeDtypeStruct((2, 2 * rows), F32),
        ],
        compiler_params=pltpu.CompilerParams(vmem_limit_bytes=28 << 20),
        cost_estimate=cost(4 * rows * weight.size, 2 * weight.size),
        name="head",
    )(*pieces, weight)


def merged(first, second):
    top = jnp.maximum(first[0:1], second[0:1])
    total = first[1:2] * jnp.exp(first[0:1] - top) + second[1:2] * jnp.exp(second[0:1] - top)
    return (top, total)


def merge_kernel(own_ref, other_ref, out_ref):
    quarter = own_ref.shape[1] // 4
    other = other_ref[...]
    parts = [other[:, k * quarter : (k + 1) * quarter] for k in (1, 0, 3, 2)]
    top, total = merged(own_ref[...], jnp.concatenate(parts, axis=1))
    out_ref[0:1] = top
    out_ref[1:2] = total


def merge_call(own, other):
    return pl.pallas_call(
        merge_kernel, out_shape=jax.ShapeDtypeStruct(own.shape, F32), name="head_merge"
    )(own, other)


def head_back_kernel(
    logits_ref, own_ref, far_ref, codes_ref, weight_ref, grad_ref, first_ref, second_ref, loss_ref
):
    step = pl.program_id(0)
    top, total = merged(own_ref[...], far_ref[...])
    log_total = top + jnp.log(total)
    codes = codes_ref[...]
    logits = logits_ref[...]
    place = lax.broadcasted_iota(jnp.int32, logits.shape, 1)
    target = column_of(codes[0:1])
    hits = place == target.astype(jnp.int32)
    shares = jnp.exp(logits - column_of(log_total))
    grad = (column_of(codes[1:2]) * (shares - hits.astype(F32))).astype(BF16)
    grad_ref[...] = grad
    result = matmul_t(grad, weight_ref[...]).astype(BF16)
    picked = jnp.sum(jnp.where(hits, logits, 0.0), axis=1, keepdims=True)
    loss = jnp.sum(codes[2:3] * log_total, keepdims=True)
    loss = loss - jnp.sum(column_of(codes[1:2]) * picked, keepdims=True)
    loss = jnp.broadcast_to(loss, loss_ref.shape)

    @pl.when(step == 0)
    def _():
        first_ref[...] = result
        loss_ref[...] = loss

    @pl.when(step == 1)
    def _():
        second_ref[...] = result
        loss_ref[...] += loss


def head_back_call(logits, own, far, codes, weight):
    slots, vocab = logits.shape
    rows = slots // 2
    width = weight.shape[0]
    piece = pl.BlockSpec((rows, width), lambda i: (0, 0))
    stat = pl.BlockSpec((2, rows), lambda i: (0, i))
    return pl.pallas_call(
        head_back_kernel,
        grid=(2,),
        in_specs=[
            pl.BlockSpec((rows, vocab), lambda i: (i, 0)),
            stat,
            stat,
            pl.BlockSpec((3, rows), lambda i: (0, i)),
            pl.BlockSpec(weight.shape, lambda i: (0, 0)),
        ],
        out_specs=[
            pl.BlockSpec((rows, vocab), lambda i: (i, 0)),
            piece,
            piece,
            pl.BlockSpec((1, 128), lambda i: (0, 0)),
        ],
        out_shape=[
            jax.ShapeDtypeStruct((slots, vocab), BF16),
            jax.ShapeDtypeStruct((rows, width), BF16),
            jax.ShapeDtypeStruct((rows, width), BF16),
            jax.ShapeDtypeStruct((1, 128), F32),
        ],
        compiler_params=pltpu.CompilerParams(vmem_limit_bytes=32 << 20),
        cost_estimate=cost(2 * slots * weight.size, 2 * weight.size),
        name="head_back",
    )(streamed(logits), own, far, codes, weight)


def weights_kernel(number, *refs):
    out_ref = refs[-1]
    start = 0
    for k in range(number):
        left_ref, right_ref = refs[2 * k], refs[2 * k + 1]
        size = right_ref.shape[1]
        out_ref[:, start : start + size] = weight_term(left_ref[...], right_ref[...]).astype(BF16)
        start += size


def weights_turn_kernel(number, *refs):
    out_ref = refs[-1]
    for k in range(number):

        @pl.when(pl.program_id(0) == k)
        def _(left_ref=refs[2 * k], right_ref=refs[2 * k + 1]):
            out_ref[...] = weight_term(left_ref[...], right_ref[...]).astype(BF16)


def head_weights_kernel(*refs):
    lefts, rights, out_ref = refs[:4], refs[4:6], refs[6]
    total = None
    for k in range(2):
        left = jnp.concatenate([lefts[2 * k][...], lefts[2 * k + 1][...]], axis=0)
        part = weight_term(left, rights[k][...])
        total = part if total is None else total + part
    out_ref[...] = total.astype(BF16)


def head_weights_call(lefts, rights, total):
    width, size = lefts[0].shape[1], rights[0].shape[1]
    block = 256
    return pl.pallas_call(
        head_weights_kernel,
        grid=(width // block,),
        in_specs=[pl.BlockSpec((left.shape[0], block), lambda j: (0, j)) for left in lefts]
        + [pl.BlockSpec(right.shape, lambda j: (0, 0)) for right in rights],
        out_specs=pl.BlockSpec((block, size), lambda j: (j, 0)),
        out_shape=pltpu.HBM((width, total), BF16),
        compiler_params=pltpu.CompilerParams(vmem_limit_bytes=32 << 20),
        cost_estimate=cost(4 * rights[0].size * width, 2 * width * size),
        name="head_weights",
    )(*lefts, *rights)


def weights_call(lefts, rights, name, held=None):
    rows, width = lefts[0].shape
    number = len(lefts)
    total = sum(right.shape[1] for right in rights)
    block = 512
    steps = width // block
    turns = len({right.shape[1] for right in rights}) == 1
    operands, in_specs = [], []
    for k in range(number):
        left_rows, size = rights[k].shape
        if turns:
            place = lambda i, j, k=k: (0, jnp.clip((i - k) * steps + j, 0, steps - 1))
            whole = lambda i, j: (0, 0)
        else:
            place = lambda j: (0, j)
            whole = lambda j: (0, 0)
        in_specs.append(pl.BlockSpec((left_rows, block), place))
        in_specs.append(pl.BlockSpec((left_rows, size), whole))
        operands += [lefts[k], rights[k]]
    aliases = {}
    if held is not None:
        first = (held.shape[1] - total) // rights[0].shape[1]
        total = held.shape[1]
        aliases = {len(operands): 0}
        operands.append(held)
        in_specs.append(pl.BlockSpec(memory_space=pl.ANY))
    else:
        first = 0
    if turns:
        grid, kernel = (number, steps), weights_turn_kernel
        out_spec = pl.BlockSpec((block, rights[0].shape[1]), lambda i, j: (j, i + first))
    else:
        grid, kernel = (steps,), weights_kernel
        out_spec = pl.BlockSpec((block, total), lambda j: (j, 0))
    return pl.pallas_call(
        lambda *refs: kernel(number, *refs[: 2 * number], refs[-1]),
        grid=grid,
        in_specs=in_specs,
        out_specs=out_spec,
        out_shape=pltpu.HBM((width, total), BF16),
        input_output_aliases=aliases,
        compiler_params=pltpu.CompilerParams(vmem_limit_bytes=40 << 20),
        cost_estimate=cost(2 * rows * width * total, 2 * width * total),
        name=name,
    )(*operands)


def fetch_other(packed):
    place = lax.axis_index("dp") % 4
    rows = packed.shape[0] // 4
    piece = cross(lax.dynamic_slice_in_dim(packed, place * rows, rows))

    def over_x(values):
        return lax.ppermute(values, "dp", X_PAIRS)

    def over_z(values):
        return lax.ppermute(values, "dp", Z_NEAR_PAIRS)

    def rest():
        beside, above = over_x(piece), over_z(piece)
        return (beside, above, over_z(beside[: rows // 2]), over_x(above[rows // 2 :]))

    return (piece, rest)


def reduce_weights(grad):
    return lax.psum_scatter(grad, "dp", scatter_dimension=0, tiled=True)


def sum_steps(values):
    for axis, pairs in (
        ("mp", CORE_PAIRS),
        ("mp", CHIP_PAIRS),
        ("dp", X_PAIRS),
        ("dp", Z_NEAR_PAIRS),
        ("dp", Z_FAR_PAIRS),
    ):
        arrived = lax.ppermute(values, axis, pairs)
        earlier = yield arrived
        values = values + after(arrived, *earlier)
    yield values


def reduce_by_steps(grad):
    place = lax.axis_index("dp")
    size = grad.shape[0] // 8
    x, near, far = place % 2, (place // 2) % 2, place // 4
    steps = (
        ((4, 2, size, -1), 1, x, X_PAIRS),
        ((2, 2, size, -1), 1, near, Z_NEAR_PAIRS),
        ((2, size, -1), 0, far, Z_FAR_PAIRS),
    )
    for shape, axis, at, pairs in steps:
        parts = grad.reshape(shape)
        keep = lax.dynamic_index_in_dim(parts, at, axis, keepdims=False)
        send = lax.dynamic_index_in_dim(parts, 1 - at, axis, keepdims=False)
        arrived = lax.ppermute(send, "dp", pairs)
        earlier = yield grad
        total = keep.astype(F32) + after(arrived, *earlier).astype(F32)
        grad = total.astype(BF16)
    yield total


def on_device_block(
    frames,
    out_cotangent,
    lengths,
    masked_rows,
    targets,
    head_device,
    first_gain,
    first_in,
    first_out,
    attend_gain,
    query_weight,
    key_weight,
    value_weight,
    attend_out,
    mixer_gain,
    mixer_value,
    mixer_gate,
    mixer_depth,
    batch_scale,
    batch_shift,
    mixer_out,
    second_gain,
    second_in,
    second_out,
    final_gain,
    head_weight,
):
    rows = frames.shape[0]
    own = lax.axis_index("mp")
    core, chip = own % 2, own // 2
    length = lax.dynamic_index_in_dim(lengths, chip, 0, keepdims=False)
    position = (jnp.arange(LEN) + core * rows) % LEN
    live = (position < length).astype(F32)
    live_column = live[:, None]
    place = position[:, None]

    scalars = jnp.stack([core, length]).astype(jnp.int32)
    attend_pack = jnp.concatenate([query_weight, key_weight, value_weight], axis=1)
    width = query_weight.shape[1]
    channels = jnp.concatenate([mixer_depth, batch_scale[None], batch_shift[None]], axis=0)
    own_live = live[:rows]
    picker = (masked_rows[:, None] == jnp.arange(rows)[None, :]).astype(BF16)
    keep = jnp.sum(picker.astype(F32) * own_live[None, :], axis=1)
    labels = (targets + 1) * (keep > 0).astype(jnp.int32)
    codes = on_chip(labels[None, :])

    fetched = []

    def fetch(done):
        fetched.append(fetch_other(attend_pack))
        fetched.append((cross(channels), cross(codes)))
        return [fetched[0][0], *fetched[1]]

    _, normed = norm_forward(frames, [], first_gain, 1.0)
    parts, first_kept = branch_forward(normed, first_in, first_out, 2, (lambda done: [], fetch))
    piece, rest = fetched[0]
    beside, above, *corner = rest()
    channels_other, codes_other = fetched[1]
    slots = masked_rows.shape[0]
    vocab = head_weight.shape[1]

    def slot_codes(codes, first):
        codes = codes.reshape(1, 2 * slots)
        counted = (codes > 0).astype(F32)
        here = counted * (jnp.arange(2 * slots)[None, :] < first).astype(F32)
        return jnp.concatenate([(codes - 1 - own * vocab).astype(F32), counted, here], axis=0)

    codes_near, codes_far = slot_codes(codes, slots), slot_codes(codes_other, 0)
    parts[0] = after(parts[0], beside, above, codes_near, codes_far)
    after_first, normed = norm_forward(frames, parts, attend_gain, 0.5)

    attend_out_other = cross(attend_out)
    mixer_others = [cross(weight) for weight in (mixer_value, mixer_gate)]
    mixer_out_other = cross(mixer_out)
    quarters = [piece, beside, above, jnp.concatenate(corner, axis=0)]
    place = jnp.stack([core, lax.axis_index("dp") % 4]).astype(jnp.int32)
    qkv_weights = [query_weight, key_weight, value_weight, *quarters]
    swapped = swap(normed)
    swapped = after(swapped, attend_out_other)
    qkv, attend_in = rows_call(
        qkv_body, "qkv", (normed, swapped), [], qkv_weights,
        [(6 * width, BF16), (D, None)], None, scalars=place, turned=False,
    )
    mixed, log_total = attend_forward_call(after(qkv, mixer_others[0]), live_column)
    attend_outs = [attend_out, attend_out_other]
    own_part, other_part = rows_call(
        out_body, "attend_out", None, [after(mixed, mixer_others[1])], attend_outs, [], D,
        scalars=place, turned=False,
    )
    parts = [own_part, swap(other_part)]
    after_attend, normed = norm_forward(after_first, parts, mixer_gain, 1.0)

    channels = jnp.concatenate([channels, channels_other], axis=1)
    depth, scale_both, shift_both = channels[:KERNEL], channels[KERNEL], channels[KERNEL + 1]
    mixer_weights = [mixer_value, mixer_gate, *mixer_others]
    mixer_outs = [mixer_out, mixer_out_other]
    swapped = swap(normed)
    mixer_in, value_in, gate, convolved, sums = mixer_front_call(
        scalars, normed, swapped, mixer_weights, depth
    )
    sums = sum_channels(sums, mixer_out_other)
    count = sums[2]
    bn_mean = sums[0] / count
    inverse = lax.rsqrt(sums[1] / count - bn_mean * bn_mean + NORM_EPSILON)
    stats = jnp.stack([bn_mean, inverse, scale_both, shift_both, 1.0 / count])
    mixer_active, own_part, other_part = rows_call(
        shape_body, "mixer_shape", None, [convolved], [stats, *mixer_outs],
        [(2 * width, None)], D, scalars=scalars,
    )
    parts = [own_part, swap(other_part)]
    after_mixer, normed = norm_forward(after_attend, parts, second_gain, 1.0)

    parts, second_kept = branch_forward(normed, second_in, second_out, 2)
    after_second, output_low, output = norm_forward(after_mixer, parts, final_gain, 0.5, True)

    chosen = dot(picker, output_low, BF16)
    vocab = head_weight.shape[1]
    far = cross(chosen)
    near_pieces = (chosen, swap(chosen))
    near_logits, near_stats = head_call(near_pieces, head_weight)
    far = after(far, near_stats)
    far_pieces = (far, swap(far))
    far_logits, far_stats = head_call(far_pieces, head_weight)
    stats_own = jnp.concatenate([near_stats, far_stats], axis=1)
    stats_own = merge_call(stats_own, swap(stats_own))
    stats_far = cross(stats_own)
    near, far = slice(0, 2 * slots), slice(2 * slots, 4 * slots)
    far_grad, *far_results, far_loss = head_back_call(
        far_logits, stats_own[:, far], stats_far[:, near], codes_far, head_weight
    )
    sent = on_chip_sum(*far_results).astype(BF16)
    crossed = cross(sent)
    near_grad, *near_results, near_loss = head_back_call(
        near_logits, stats_own[:, near], stats_far[:, far], codes_near, head_weight
    )
    own_loss = near_loss[0, 0] + far_loss[0, 0]
    grad_chosen = on_chip_sum(*near_results) + crossed.astype(F32)
    grad_second, grad_low, final_gain_grad = norm_backward(
        after_second, final_gain, [out_cotangent], None, 0.5, (picker.T, grad_chosen.astype(BF16))
    )

    grad_head = head_weights_call(
        [*far_pieces, *near_pieces], [after(far_grad, grad_low), near_grad], vocab
    )

    def second_weights(grads, active, normed, grad_inner):
        lefts, rights = [grads, normed], [active, grad_inner]
        return (
            weights_call(
                [streamed(left) for left in lefts], [streamed(right) for right in rights],
                "second_weights",
            ),
        )

    parts, _, (grad_second_both,) = branch_backward(
        second_in, second_out, second_kept, grad_low, 2, (lambda done: [grad_head], lambda done: []),
        second_weights,
    )
    grad_head = reduce_weights(grad_head)
    grad_mixer, grad_low, second_gain_grad = norm_backward(
        after_mixer, second_gain, parts, grad_second, 1.0
    )

    grad_shaped, grad_full, sums = rows_call(
        shape_back_body, "mixer_shape_back", (grad_low, swap(grad_low)), [streamed(convolved)],
        [stats, *mixer_outs], [(2 * width, F32), (D, None)], None, (2, 2 * width), scalars,
    )
    sums = sum_channels(sums)
    batch_shift_grad, batch_scale_grad = sums[0], sums[1]
    grad_second_both = reduce_weights(after(grad_second_both, grad_head, sums))
    grad_both, depth_grad, own_part, other_part = mixer_back_call(
        scalars, grad_shaped, convolved, value_in, gate, stats, sums, depth, mixer_weights
    )
    grad_attend, grad_low, mixer_gain_grad = norm_backward(
        after_attend, mixer_gain, [own_part, swap(other_part)], grad_mixer, 1.0
    )
    mixer_grads = weights_call(
        [streamed(mixer_in), streamed(grad_full)], [grad_both, streamed(mixer_active)], "mixer_weights"
    )
    counts = jnp.stack([own_loss, jnp.sum(keep)])
    counts = jnp.concatenate([counts, jnp.zeros((D - 2,), F32)])[None]
    depth_full = jnp.zeros((KERNEL, D), F32)
    for side, at in ((0, own), (1, (own + 2) % 4)):
        depth_full = lax.dynamic_update_slice_in_dim(
            depth_full, depth_grad[:, side * width : (side + 1) * width], at * width, 1
        )
    gains = jnp.concatenate(
        [mixer_gain_grad, second_gain_grad, final_gain_grad, counts, depth_full], axis=0
    )
    all_run = sum_steps(gains)
    next(all_run)
    all_run.send(())
    gain_crossed = all_run.send(())
    mixer_crossed = [
        cross(after(part, gain_crossed))
        for part in (mixer_grads[:, 2 * width : 4 * width], mixer_grads[:, 5 * width :])
    ]

    grad_mixed, grad_full = rows_call(
        out_back_body, "attend_out_back", (grad_low, swap(grad_low)), [], attend_outs,
        [(2 * width, BF16), (D, None)], None, scalars=place, turned=False,
    )
    grad_mixed = after(grad_mixed, mixer_grads, gain_crossed)
    grad_qkv = attend_backward_call(qkv, live_column, grad_mixed, log_total)
    own_part, other_part = rows_call(
        qkv_back_body, "qkv_back", None, [after(grad_qkv, mixer_crossed[0])], qkv_weights, [], D, scalars=place,
        turned=False,
    )
    grad_first, grad_low, attend_gain_grad = norm_backward(
        after_first, attend_gain, [own_part, swap(other_part)], grad_attend, 0.5
    )
    attend_grads = weights_call(
        [streamed(attend_in), streamed(grad_full)], [after(grad_qkv, grad_low), streamed(mixed)], "attend_weights"
    )

    def sides(first, second):
        return jnp.concatenate([first, second], axis=1)

    mixer_sum = sides(mixer_grads[:, : 2 * width], mixer_grads[:, 4 * width : 5 * width])
    mixer_crossed = sides(*after(mixer_crossed, attend_grads))
    mixer_sum = (mixer_sum.astype(F32) + mixer_crossed.astype(F32)).astype(BF16)
    middle = reduce_weights(after(sides(attend_grads, mixer_sum), grad_second_both))

    def first_weights(grads, active, normed, grad_inner):
        grad_out = dot_rows(grads, active)
        run_out = reduce_by_steps(grad_out)
        return (grad_out, run_out, next(run_out))

    parts, (grads, grad_inner, active, normed), (grad_out, run_out, _) = branch_backward(
        first_in, first_out, first_kept, grad_low, 2, (lambda done: [attend_grads], lambda done: []), first_weights
    )
    grad_in = dot_rows(normed, after(grad_inner, grad_out))
    run_in = reduce_by_steps(grad_in)
    next(run_in)
    all_run.send((grad_in,))
    input_grad, _, first_gain_grad = norm_backward(frames, first_gain, parts, grad_first, 1.0)
    gain_run = sum_steps(jnp.concatenate([attend_gain_grad, first_gain_grad], axis=0))
    next(gain_run)
    gain_run.send(())
    gain_run.send(())
    out_one = run_out.send((input_grad,))
    all_run.send((out_one,))
    grad_head = after(grad_head, out_one).astype(F32)
    grad_second_both = after(grad_second_both, out_one).astype(F32)
    out_two = run_out.send((out_one,))
    in_one = run_in.send((out_two,))
    gain_run.send((in_one,))
    middle = after(middle, in_one).astype(F32)
    attend_grads, mixer_sum = middle[:, : 8 * width], middle[:, 8 * width :]
    crossed = cross(sides(attend_grads[:, 3 * width : 6 * width], attend_grads[:, 7 * width :]).astype(BF16))
    own_part = sides(attend_grads[:, : 3 * width], attend_grads[:, 6 * width : 7 * width])
    in_two = run_in.send((own_part,))
    gain_run.send((in_two,))
    attend_grads = own_part + after(crossed, in_two).astype(F32)
    gains = all_run.send((attend_grads,))
    loss = gains[3, 0] / gains[3, 1]
    depth_grad = lax.dynamic_slice_in_dim(gains[4:], own * width, width, 1)
    grad_first_out = run_out.send((attend_grads,))
    grad_first_in = run_in.send((grad_first_out,))
    first_gain_grad = gain_run.send((grad_first_in,))
    grad_second_out, grad_second_in = jnp.split(grad_second_both, 2, axis=1)
    grad_query, grad_key, grad_value, grad_out = jnp.split(attend_grads, 4, axis=1)
    grad_mixer_value, grad_mixer_gate, grad_mixer_out = jnp.split(mixer_sum, 3, axis=1)
    return (
        output,
        loss,
        input_grad,
        first_gain_grad[1],
        grad_first_in,
        grad_first_out.T,
        first_gain_grad[0],
        grad_query,
        grad_key,
        grad_value,
        grad_out.T,
        gains[0],
        grad_mixer_value,
        grad_mixer_gate,
        depth_grad,
        batch_scale_grad[:width],
        batch_shift_grad[:width],
        grad_mixer_out.T,
        gains[1],
        grad_second_in,
        grad_second_out.T,
        gains[2],
        grad_head,
    )


def solution(mesh):
    in_specs = (
        P(("dp", "mp"), None),
        P(("dp", "mp"), None),
        P("dp"),
        P(("dp", "mp")),
        P(("dp", "mp")),
        P(("dp", "mp"), None),
        P(),
        P(None, "mp"),
        P("mp", None),
        P(),
        P(None, "mp"),
        P(None, "mp"),
        P(None, "mp"),
        P("mp", None),
        P(),
        P(None, "mp"),
        P(None, "mp"),
        P(None, "mp"),
        P("mp"),
        P("mp"),
        P("mp", None),
        P(),
        P(None, "mp"),
        P("mp", None),
        P(),
        P(None, "mp"),
    )
    out_specs = (
        P(("dp", "mp"), None),
        P(),
        P(("dp", "mp"), None),
        P(),
        P("dp", "mp"),
        P("mp", "dp"),
        P(),
        P("dp", "mp"),
        P("dp", "mp"),
        P("dp", "mp"),
        P("mp", "dp"),
        P(),
        P("dp", "mp"),
        P("dp", "mp"),
        P(None, "mp"),
        P("mp"),
        P("mp"),
        P("mp", "dp"),
        P(),
        P("dp", "mp"),
        P("mp", "dp"),
        P(),
        P("dp", "mp"),
    )
    small = mesh.shape["dp"] == 8 and mesh.shape["mp"] == 4
    on_device = on_device_block if small else on_device_any
    return jax.shard_map(
        on_device, mesh=mesh, in_specs=in_specs, out_specs=out_specs, check_vma=False
    )
```
